32 devices in a mesh: seq: 16 (over z, y, x), head: 2 (over core).
Axes of the slice: x: 2, y: 2, z: 4, core: 2. Of those that a mesh axis runs over, the one named last changes fastest.
Arguments:
- tokens: bfloat16 [2048, 2048], P('seq'), may hold values from -6 to 6
- norm1_gain: float32 [2048], replicated, may hold values from 0.1 to 1.9
- mix_weight: bfloat16 [4, 2048, 2048], P(None, 'seq', 'head'), may hold values from -0.125 to 0.125
- conv_weight: float32 [3, 4, 2048], P(None, None, 'head'), may hold values from -3 to 3
- decay_gap: float32 [2048], P('head'), may hold values from 0.00024414062 to 0.05
- group_gain: float32 [2048], P('head'), may hold values from 0.1 to 1.9
- out_weight: bfloat16 [2048, 2048], P('head', 'seq'), may hold values from -0.25 to 0.25
- norm2_gain: float32 [2048], replicated, may hold values from 0.1 to 1.9
- up_pair: bfloat16 [2, 2048, 5632], P(None, 'seq', 'head'), may hold values from -0.125 to 0.125
- down_weight: bfloat16 [5632, 2048], P('head', 'seq'), may hold values from -0.078125 to 0.078125
- cotangent: bfloat16 [2048, 2048], P('seq'), may hold values from -6 to 6
Outputs:
- block_out: float32 [2048, 2048], P('seq')
- grad_tokens: float32 [2048, 2048], P('seq')
- grad_norm1: float32 [2048], replicated
- grad_mix: float32 [4, 2048, 2048], P(None, 'seq', 'head')
- grad_conv: float32 [3, 4, 2048], P(None, None, 'head')
- grad_gap: float32 [2048], P('head')
- grad_group: float32 [2048], P('head')
- grad_out: float32 [2048, 2048], P('head', 'seq')
- grad_norm2: float32 [2048], replicated
- grad_up: float32 [2, 2048, 5632], P(None, 'seq', 'head')
- grad_down: float32 [5632, 2048], P('head', 'seq')
- inverse_rms: float32 [2, 2048], P(None, 'seq')
The draws below stay inside these ranges and needn't reach their ends.
All inputs are finite; a program needn't handle non-finite values.
Results may differ from the reference program's by a relative error of at most 0.012.
Values may be sent and summed in bfloat16 or wider, within the bound.
No kernel may reach another device: no remote copies, remote signals or barrier semaphores. Data moves between devices by JAX's collectives and lax.ppermute only.
A program may use at most 320 MiB of HBM per device.

```python
import math
import jax
import jax.numpy as jnp
from jax import lax

D = 2048
HEAD_DIM = 128
FF = 5632
SPAN = 64
TOKENS = 2048
HK = 2048


def level_of(rng, shape, shards, low, high):
    gain = 1.0
    for position, shards_of in shards:
        steps = jax.random.uniform(jax.random.fold_in(jax.random.fold_in(rng, 6), position), (shards_of,), jnp.float32, low / len(shards), high / len(shards))
        gain = gain * jnp.repeat(jnp.exp(steps), shape[position] // shards_of).reshape((-1,) + (1,) * (len(shape) - 1 - position))
    return gain


def noise(rng, shape, scale, bound, shards=(), held_as=jnp.bfloat16):
    result = scale * jax.random.normal(rng, shape, jnp.float32)
    if shards:
        result = result * level_of(rng, shape, shards, -0.22, 0.18)
    return jnp.clip(result, -bound, bound).astype(held_as)


def setup_inputs(seed: int = 0) -> dict:
    seeds = jax.random.split(jax.random.key(seed), 12)
    return {
        "tokens": noise(seeds[0], (TOKENS, D), 1.0, 6.0, ((0, 16),)),
        "norm1_gain": jnp.clip(1.0 + 0.18 * jax.random.normal(seeds[1], (D,), jnp.float32), 0.1, 1.9),
        "mix_weight": noise(seeds[2], (4, D, HK), D ** -0.5, 0.125, ((1, 16), (2, 2))),
        "conv_weight": noise(seeds[3], (3, 4, HK), 0.5, 3.0, ((2, 2),), jnp.float32),
        "decay_gap": jnp.clip(jnp.exp(math.log(0.05) - 5.322034 * jax.random.uniform(seeds[4], (HK,), jnp.float32) ** level_of(seeds[4], (HK,), ((0, 2),), -0.2, 0.2)), 0.00024414062, 0.05),
        "group_gain": jnp.clip(1.0 + 0.18 * jax.random.normal(seeds[5], (HK,), jnp.float32), 0.1, 1.9),
        "out_weight": noise(seeds[6], (HK, D), (HK // 4) ** -0.5, 0.25, ((0, 2), (1, 16))),
        "norm2_gain": jnp.clip(1.0 + 0.18 * jax.random.normal(seeds[7], (D,), jnp.float32), 0.1, 1.9),
        "up_pair": noise(seeds[8], (2, D, FF), D ** -0.5, 0.125, ((1, 16), (2, 2))),
        "down_weight": noise(seeds[9], (FF, D), FF ** -0.5, 0.078125, ((0, 2), (1, 16))),
        "cotangent": noise(seeds[10], (TOKENS, D), 1.0, 6.0, ((0, 16),)),
    }


EPS_TOKEN = 1e-06
EPS_GROUP = 1e-05
HIGH = lax.Precision.HIGHEST

@jax.custom_vjp
def low(v):
    return lax.optimization_barrier(v.astype(jnp.bfloat16)).astype(jnp.float32)

@jax.custom_vjp
def low_back(v):
    return v

def low_keep(v):
    return (low(v), None)

def low_pass(kept, grad):
    return (grad,)

def back_keep(v):
    return (v, None)

def back_low(kept, grad):
    return (low(grad),)
low.defvjp(low_keep, low_pass)
low_back.defvjp(back_keep, back_low)

def convolve(extended, conv_taps):
    length = extended.shape[1] - 3
    total = conv_taps[:, 0][:, None] * extended[:, 3:]
    for delay_step in range(1, 4):
        total = total + conv_taps[:, delay_step][:, None] * extended[:, 3 - delay_step:3 - delay_step + length]
    return total

def gates(convolved, decay_gap):
    queries = jax.nn.silu(convolved[0])
    open_share = 1.0 - jax.nn.sigmoid(convolved[1])
    log_forget = jnp.log(1.0 - decay_gap * open_share)
    key_rows = decay_gap * open_share
    return (queries, log_forget, key_rows, convolved[2])

def span_step(carry_state, pieces):
    queries, log_forget, key_rows, values = pieces
    running = jnp.cumsum(log_forget, axis=0)
    decayed_query = queries * jnp.exp(running)
    lifted_key = key_rows * jnp.exp(-running)
    scores = jnp.einsum('thd,shd->hts', decayed_query, lifted_key, precision=HIGH)
    causal = jnp.arange(SPAN)[:, None] >= jnp.arange(SPAN)[None, :]
    scores = jnp.where(causal[None], scores, 0.0)
    mixed_out = jnp.einsum('hts,she->the', scores, values, precision=HIGH)
    mixed_out = mixed_out + jnp.einsum('thd,hde->the', decayed_query, carry_state, precision=HIGH)
    final_log = running[-1]
    carried = key_rows * jnp.exp(final_log[None] - running)
    carry_state = jnp.exp(final_log)[:, :, None] * carry_state + jnp.einsum('thd,the->hde', carried, values, precision=HIGH)
    return (carry_state, mixed_out)

def local_mix(queries, log_forget, key_rows, values, state_in):
    length, heads_here, head_width = queries.shape
    blocks = length // SPAN

    def blocked(array):
        return array.reshape(blocks, SPAN, heads_here, head_width)
    state_out, mixed_out = lax.scan(jax.checkpoint(span_step), state_in, (blocked(queries), blocked(log_forget), blocked(key_rows), blocked(values)))
    return (mixed_out.reshape(length, heads_here, head_width), state_out)

def group_gate(mixed_out, gate_rows, group_gain):
    inverse = lax.rsqrt(lax.optimization_barrier(jnp.mean(mixed_out * mixed_out, axis=-1, keepdims=True)) + EPS_GROUP)
    normed = (mixed_out * inverse).reshape(gate_rows.shape)
    return normed * group_gain * jax.nn.silu(gate_rows)

def split_heads(array):
    return array.reshape(array.shape[0], -1, HEAD_DIM)

def forward(token_rows, norm1_gain, mix_weight, conv_weight, decay_gap, group_gain, out_weight, norm2_gain, up_pair, down_weight):
    inverse1 = lax.rsqrt(lax.optimization_barrier(jnp.mean(token_rows * token_rows, axis=-1, keepdims=True)) + EPS_TOKEN)
    normed1 = low(token_rows * inverse1 * norm1_gain)
    projected = low_back(low(jnp.einsum('td,jdc->jtc', normed1, mix_weight, precision=HIGH)))
    padded = jnp.pad(projected[:3], ((0, 0), (3, 0), (0, 0)))
    convolved = convolve(padded, conv_weight)
    queries, log_forget, key_rows, values = gates(convolved, decay_gap)
    heads_all = queries.shape[1] // HEAD_DIM
    start_state = jnp.zeros((heads_all, HEAD_DIM, HEAD_DIM), jnp.float32)
    mixed_out, _ = local_mix(split_heads(queries), split_heads(log_forget), split_heads(key_rows), split_heads(values), start_state)
    gated = low(group_gate(mixed_out, projected[3], group_gain))
    hidden = token_rows + low_back(jnp.dot(gated, out_weight, precision=HIGH))
    inverse2 = lax.rsqrt(lax.optimization_barrier(jnp.mean(hidden * hidden, axis=-1, keepdims=True)) + EPS_TOKEN)
    normed2 = low(hidden * inverse2 * norm2_gain)
    lifted = low_back(jnp.einsum('td,jdf->jtf', normed2, up_pair, precision=HIGH))
    inner_act = low(jax.nn.silu(lifted[0]) * lifted[1])
    block_out = hidden + jnp.dot(inner_act, down_weight, precision=HIGH)
    inverse_rms = jnp.stack([inverse1[:, 0], inverse2[:, 0]])
    return (block_out, inverse_rms)

def reference(tokens, norm1_gain, mix_weight, conv_weight, decay_gap, group_gain, out_weight, norm2_gain, up_pair, down_weight, cotangent):
    token_rows = tokens.astype(jnp.float32)
    block_out, back_fn, inverse_rms = jax.vjp(forward, token_rows, norm1_gain.astype(jnp.float32), mix_weight.astype(jnp.float32), conv_weight.astype(jnp.float32), decay_gap.astype(jnp.float32), group_gain.astype(jnp.float32), out_weight.astype(jnp.float32), norm2_gain.astype(jnp.float32), up_pair.astype(jnp.float32), down_weight.astype(jnp.float32), has_aux=True)
    grads = back_fn(cotangent.astype(jnp.float32))
    return (block_out, grads[0], grads[1], grads[2], grads[3], grads[4], grads[5], grads[6], grads[7], grads[8], grads[9], inverse_rms)
```

```python
import functools

import jax
import jax.numpy as jnp
from jax import lax
from jax.experimental import pallas as pl
from jax.experimental.pallas import tpu as pltpu
from jax.sharding import PartitionSpec as P

HEAD_DIM = 128
CHUNK = 128
PAD = 8
EPS_TOKEN = 1e-06
EPS_GROUP = 1e-05
HIGH = lax.Precision.HIGHEST
F32 = jnp.float32
BF16 = jnp.bfloat16
VMEM_LIMIT = 48 * 1024 * 1024


def mul(a, b, ca, cb, precision=HIGH):
    return lax.dot_general(
        a, b, (((ca,), (cb,)), ((), ())), precision=precision, preferred_element_type=F32
    )


def dsilu(v):
    s = jax.nn.sigmoid(v)
    return s * (1.0 + v * (1.0 - s))


def triangle(lower):
    row = lax.broadcasted_iota(jnp.int32, (CHUNK, CHUNK), 0)
    col = lax.broadcasted_iota(jnp.int32, (CHUNK, CHUNK), 1)
    return (row >= col) if lower else (row <= col)


def forward_kernel(
    proj, halo, taps, gap, conv_out, query_out, key_out, total_out, state_out, local_out, last_out, rows
):
    length = proj.shape[0]
    rows[0:PAD, :] = halo[...].astype(F32)
    rows[PAD:, :] = proj[...].astype(F32)
    lower = triangle(True)
    ones = lower.astype(F32)
    state = jnp.zeros((HEAD_DIM, HEAD_DIM), F32)
    before = jnp.zeros((1, HEAD_DIM), F32)
    for c in range(length // CHUNK):
        at = c * CHUNK
        here = slice(at, at + CHUNK)
        conv = []
        for j in range(3):
            cols = slice(j * HEAD_DIM, (j + 1) * HEAD_DIM)
            total = taps[4 * j : 4 * j + 1, :] * rows[PAD + at : PAD + at + CHUNK, cols]
            for d in range(1, 4):
                total = total + taps[4 * j + d : 4 * j + d + 1, :] * rows[PAD + at - d : PAD + at - d + CHUNK, cols]
            conv.append(total)
            conv_out[here, cols] = total
        queries = conv[0] * jax.nn.sigmoid(conv[0])
        open_share = 1.0 - jax.nn.sigmoid(conv[1])
        keys = gap[...] * open_share
        log_forget = jnp.log(1.0 - keys)
        values = conv[2]
        running = mul(ones, log_forget, 1, 0)
        last = running[CHUNK - 1 : CHUNK, :]
        query = queries * jnp.exp(running)
        key = keys * jnp.exp(-running)
        carried = keys * jnp.exp(last - running)
        query_out[here, :] = query
        key_out[here, :] = key
        total_out[c : c + 1, :] = before
        state_out[c] = state
        scores = jnp.where(lower, mul(query, key, 1, 1), 0.0)
        local_out[here, :] = mul(scores, values, 1, 0) + mul(query, state, 1, 1)
        state = state * jnp.exp(last) + mul(values, carried, 0, 0)
        before = before + last
    last_out[0:HEAD_DIM, :] = state
    last_out[HEAD_DIM:, :] = jnp.broadcast_to(jnp.exp(before), (PAD, HEAD_DIM))


def gate_kernel(local, query, total, state, carry, gate, gain, mixed_out, state_out, gated_out):
    length = local.shape[0]
    start = carry[...]
    for c in range(length // CHUNK):
        here = slice(c * CHUNK, (c + 1) * CHUNK)
        grown = start * jnp.exp(total[c : c + 1, :])
        state_out[c] = state[c] + grown
        mixed = local[here, :] + mul(query[here, :], grown, 1, 1)
        mixed_out[here, :] = mixed
        inverse = lax.rsqrt(jnp.mean(mixed * mixed, axis=-1, keepdims=True) + EPS_GROUP)
        g = gate[here, :].astype(F32)
        gated_out[here, :] = (mixed * inverse * gain[...] * (g * jax.nn.sigmoid(g))).astype(BF16)


def gate_back_kernel(
    grad_gated, mixed, gate, gain, query, decay, grad_mixed_out, grad_gate_out, grad_gain_out, start_out
):
    length = mixed.shape[0]
    count = length // CHUNK
    grad_gain = jnp.zeros((1, HEAD_DIM), F32)
    state = jnp.zeros((HEAD_DIM, HEAD_DIM), F32)
    for c in reversed(range(count)):
        here = slice(c * CHUNK, (c + 1) * CHUNK)
        grad = grad_gated[here, :].astype(F32)
        mix = mixed[here, :]
        inverse = lax.rsqrt(jnp.mean(mix * mix, axis=-1, keepdims=True) + EPS_GROUP)
        g = gate[here, :].astype(F32)
        s = jax.nn.sigmoid(g)
        unit = mix * inverse
        w = grad * gain[...] * (g * s)
        grad_gain = grad_gain + jnp.sum(grad * unit * (g * s), axis=0, keepdims=True)
        grad_gate_out[here, :] = (grad * unit * gain[...] * (s * (1.0 + g * (1.0 - s)))).astype(BF16)
        grad_mixed = inverse * w - mix * (inverse * inverse * inverse) * jnp.mean(w * mix, axis=-1, keepdims=True)
        grad_mixed_out[here, :] = grad_mixed
        state = state * decay[c : c + 1, :] + mul(grad_mixed, query[here, :], 0, 0)
    start_out[...] = state
    grad_gain_out[...] = jnp.broadcast_to(grad_gain, (PAD, HEAD_DIM))


def backward_kernel(
    grad_mixed, conv, query, key, states, carry, halo, proj, taps, gap, grad_out, edge_out, small_out, rows, grads
):
    length = grad_mixed.shape[0]
    count = length // CHUNK
    rows[0:PAD, :] = halo[...].astype(F32)
    rows[PAD:, :] = proj[...].astype(F32)
    grads[0:PAD, :] = jnp.zeros((PAD, 3 * HEAD_DIM), F32)
    grads[PAD + length :, :] = jnp.zeros((PAD, 3 * HEAD_DIM), F32)
    lower = triangle(True)
    ones = lower.astype(F32)
    upper = triangle(False).astype(F32)
    last_row = lax.broadcasted_iota(jnp.int32, (CHUNK, HEAD_DIM), 0) == CHUNK - 1
    back = carry[...]
    grad_gap = jnp.zeros((1, HEAD_DIM), F32)
    sums = [jnp.zeros((1, HEAD_DIM), F32) for _ in range(12)]
    for c in reversed(range(count)):
        at = c * CHUNK
        here = slice(at, at + CHUNK)
        c0, c1, values = (conv[here, j * HEAD_DIM : (j + 1) * HEAD_DIM] for j in range(3))
        s1 = jax.nn.sigmoid(c1)
        open_share = 1.0 - s1
        keys = gap[...] * open_share
        forget = 1.0 - keys
        running = mul(ones, jnp.log(forget), 1, 0)
        last = running[CHUNK - 1 : CHUNK, :]
        grown, shrunk, rest = jnp.exp(running), jnp.exp(-running), jnp.exp(last - running)
        q, k, g = query[here, :], key[here, :], grad_mixed[here, :]
        carried = keys * rest
        state = states[c]
        scores = jnp.where(lower, mul(q, k, 1, 1), 0.0)
        grad_scores = jnp.where(lower, mul(g, values, 1, 1), 0.0)
        grad_values = mul(scores, g, 0, 0) + mul(carried, back, 1, 1)
        grad_query = mul(grad_scores, k, 1, 0) + mul(g, state, 1, 0)
        grad_key = mul(grad_scores, q, 0, 0)
        grad_carried = mul(values, back, 1, 0)
        grad_last = jnp.exp(last) * jnp.sum(back * state, axis=0, keepdims=True) + jnp.sum(
            grad_carried * carried, axis=0, keepdims=True
        )
        grad_running = grad_query * q - grad_key * k - grad_carried * carried
        grad_running = grad_running + jnp.where(last_row, grad_last, 0.0)
        grad_keys = grad_key * shrunk + grad_carried * rest
        grad_forget = mul(upper, grad_running, 1, 0) / forget
        inner = grad_forget - grad_keys
        grad_gap = grad_gap - jnp.sum(open_share * inner, axis=0, keepdims=True)
        sigmoid0 = jax.nn.sigmoid(c0)
        new = (
            grad_query * grown * (sigmoid0 * (1.0 + c0 * (1.0 - sigmoid0))),
            gap[...] * s1 * open_share * inner,
            grad_values,
        )
        back = back * jnp.exp(last) + mul(g, q, 0, 0)
        for j in range(3):
            cols = slice(j * HEAD_DIM, (j + 1) * HEAD_DIM)
            grads[PAD + at : PAD + at + CHUNK, cols] = new[j]
            for d in range(4):
                sums[4 * j + d] = sums[4 * j + d] + jnp.sum(
                    new[j] * rows[PAD + at - d : PAD + at - d + CHUNK, cols], axis=0, keepdims=True
                )
            total = taps[4 * j : 4 * j + 1, :] * new[j]
            for d in range(1, 4):
                total = total + taps[4 * j + d : 4 * j + d + 1, :] * grads[PAD + at + d : PAD + at + d + CHUNK, cols]
            grad_out[here, cols] = total
    for j in range(3):
        cols = slice(j * HEAD_DIM, (j + 1) * HEAD_DIM)
        total = taps[4 * j + 1 : 4 * j + 2, :] * grads[1 : 1 + PAD, cols]
        for d in range(2, 4):
            total = total + taps[4 * j + d : 4 * j + d + 1, :] * grads[d : d + PAD, cols]
        edge_out[:, cols] = total
    for i in range(12):
        small_out[i : i + 1, :] = sums[i]
    small_out[12:13, :] = grad_gap
    small_out[13:16, :] = jnp.zeros((3, HEAD_DIM), F32)


def call(kernel, outs, args, scratch=()):
    return pl.pallas_call(
        kernel,
        out_shape=[jax.ShapeDtypeStruct(s, d) for s, d in outs],
        in_specs=[pl.BlockSpec(memory_space=pltpu.VMEM)] * len(args),
        out_specs=[pl.BlockSpec(memory_space=pltpu.VMEM)] * len(outs),
        scratch_shapes=list(scratch),
        compiler_params=pltpu.CompilerParams(vmem_limit_bytes=VMEM_LIMIT),
    )(*args)


class Group:
    def __init__(self, heads):
        self.size = heads
        self.peers = lax.axis_size("seq")
        self.count = self.peers // heads
        self.member = lax.rem(lax.axis_index("seq"), heads)
        self.core = lax.axis_index("head")
        self.lists = [list(range(g * heads, (g + 1) * heads)) for g in range(self.count)]

    def swap(self, value, bits):
        return lax.ppermute(value, "seq", [(s, s ^ bits) for s in range(self.peers)])

    def other_core(self, value):
        return lax.ppermute(value, "head", [(0, 1), (1, 0)])

    def shift(self, value, groups):
        step = groups * self.size
        pairs = [(s, s + step) for s in range(self.peers) if 0 <= s + step < self.peers]
        return lax.ppermute(value, "seq", pairs)

    def carry(self, state, decay, sign):
        total = None
        for k in reversed(range(1, self.count)):
            new = self.shift(state, sign * k)
            total = new if total is None else new + total * self.shift(decay, sign * k)
        return jnp.zeros_like(state) if total is None else total

    def gather(self, half):
        got = {0: half}
        for bits in (1, 2, 4):
            got[bits] = self.swap(half, bits)
        got[3] = self.swap(got[2], 1)
        got[6] = self.swap(got[4], 2)
        got[5] = self.swap(got[4], 1)
        got[7] = self.swap(got[5], 2)
        own = jnp.zeros((self.size,) + half.shape, half.dtype)
        for bits in range(self.size):
            own = lax.dynamic_update_index_in_dim(own, got[bits], self.member ^ bits, 0)
        other = self.other_core(own)
        pair = jnp.where(self.core == 0, jnp.stack([own, other], 1), jnp.stack([other, own], 1))
        return pair.reshape((-1,) + half.shape[1:])

    def scatter(self, partial):
        rows = partial.reshape(self.size, 2, -1, partial.shape[-1])
        other = lax.dynamic_index_in_dim(rows, 1 - self.core, 1, False).astype(BF16)
        mine = lax.dynamic_index_in_dim(rows, self.core, 1, False)
        total = mine + self.other_core(other).astype(F32)
        part = [lax.dynamic_index_in_dim(total, self.member ^ bits, 0, False) for bits in range(self.size)]

        def add(to, source, bits):
            part[to] = part[to] + self.swap(part[source].astype(BF16), bits).astype(F32)

        add(5, 7, 2)
        add(2, 3, 1)
        add(4, 6, 2)
        add(0, 1, 1)
        add(4, 5, 1)
        add(0, 2, 2)
        add(0, 4, 4)
        return part[0]


def to_owners(group, blocks):
    return lax.all_to_all(jnp.concatenate([blocks] * group.count, 0), "seq", 0, 0, tiled=True)


def to_shards(group, blocks):
    got = lax.all_to_all(blocks, "seq", 0, 0, tiled=True)
    return jnp.sum(got.reshape((group.count, group.size) + got.shape[1:]).astype(F32), axis=0)


def inverse_of(rows):
    return lax.rsqrt(jnp.mean(rows * rows, axis=-1, keepdims=True) + EPS_TOKEN)


def norm_back(rows, inverse, gain, grad):
    scaled = grad * gain
    dot_term = jnp.mean(scaled * rows, axis=-1, keepdims=True)
    grad_rows = inverse * scaled - rows * (inverse * inverse * inverse) * dot_term
    return grad_rows, jnp.sum(grad * rows * inverse, axis=0)


def shards(
    tokens,
    norm1_gain,
    mix_weight,
    conv_weight,
    decay_gap,
    group_gain,
    out_weight,
    norm2_gain,
    up_pair,
    down_weight,
    cotangent,
):
    depth = mix_weight.shape[1]
    heads = mix_weight.shape[2] // HEAD_DIM
    units = down_weight.shape[0] // heads
    local, width = tokens.shape
    half = local // 2
    group = Group(heads)
    peers, member, core = group.peers, group.member, group.core
    length = heads * local
    count = length // CHUNK

    def my_half(rows):
        return lax.dynamic_slice_in_dim(rows, core * half, half, 0)

    def own_head(array):
        return lax.dynamic_slice_in_dim(array, member * HEAD_DIM, HEAD_DIM, array.ndim - 1)

    mix_blocks = mix_weight.reshape(4, depth, heads, HEAD_DIM).transpose(2, 1, 0, 3)
    mix_own = to_owners(group, mix_blocks.reshape(heads, depth, 4 * HEAD_DIM)).reshape(width, 4 * HEAD_DIM)
    up_blocks = up_pair.transpose(0, 2, 1).reshape(2, heads, units, depth).transpose(1, 0, 2, 3)
    up_own = to_owners(group, up_blocks.reshape(heads, 2 * units, depth))
    up_own = up_own.transpose(1, 0, 2).reshape(2 * units, width)
    down_own = to_owners(group, down_weight.reshape(heads, units, depth))
    down_own = down_own.transpose(1, 0, 2).reshape(units, width)
    out_all = lax.all_gather(out_weight, "seq", axis=0)
    out_all = out_all.transpose(1, 0, 2).reshape(heads * HEAD_DIM, width)

    taps = own_head(conv_weight).reshape(12, HEAD_DIM)
    gap = own_head(decay_gap).reshape(1, HEAD_DIM)
    gain = own_head(group_gain).reshape(1, HEAD_DIM)

    token_rows = tokens.astype(F32)
    inverse1 = inverse_of(token_rows)
    half_tokens = my_half(token_rows)
    half_inverse1 = my_half(inverse1)
    normed1 = group.gather((half_tokens * half_inverse1 * norm1_gain).astype(BF16))
    projected = mul(normed1, mix_own, 1, 0, None).astype(BF16)
    rows3, gate_rows = projected[:, : 3 * HEAD_DIM], projected[:, 3 * HEAD_DIM :]
    halo = jnp.concatenate(
        [jnp.zeros((PAD - 3, 3 * HEAD_DIM), BF16), group.shift(rows3[length - 3 :], 1)], axis=0
    )

    def wide(n, dtype=F32):
        return ((length, n * HEAD_DIM), dtype)

    square = ((HEAD_DIM, HEAD_DIM), F32)
    conv, query, key, totals, states, mixed_here, last = call(
        forward_kernel,
        [
            wide(3),
            wide(1),
            wide(1),
            ((count, HEAD_DIM), F32),
            ((count, HEAD_DIM, HEAD_DIM), F32),
            wide(1),
            ((HEAD_DIM + PAD, HEAD_DIM), F32),
        ],
        (rows3, halo, taps, gap),
        [pltpu.VMEM((length + PAD, 3 * HEAD_DIM), F32)],
    )
    own_decay = last[HEAD_DIM : HEAD_DIM + 1]
    carry = group.carry(last[:HEAD_DIM], own_decay, 1)
    mixed, states, gated = call(
        gate_kernel,
        [wide(1), ((count, HEAD_DIM, HEAD_DIM), F32), wide(1, BF16)],
        (mixed_here, query, totals, states, carry, gate_rows, gain),
    )

    def by_head(rows):
        got = lax.all_to_all(rows.reshape(heads, local, HEAD_DIM), "seq", 0, 0, axis_index_groups=group.lists, tiled=True)
        return got.transpose(1, 0, 2).reshape(local, heads * HEAD_DIM)

    def by_token(rows):
        blocks = rows.reshape(local, heads, HEAD_DIM).transpose(1, 0, 2)
        got = lax.all_to_all(blocks, "seq", 0, 0, axis_index_groups=group.lists, tiled=True)
        return got.reshape(length, HEAD_DIM)

    branch = mul(by_head(gated), out_all, 1, 0, None)
    away = lax.dynamic_slice_in_dim(branch, (1 - core) * half, half, 0)
    hidden = half_tokens + my_half(branch) + group.other_core(away)

    inverse2 = inverse_of(hidden)
    normed2 = group.gather((hidden * inverse2 * norm2_gain).astype(BF16))
    cot_half = my_half(cotangent)
    cot_all = group.gather(cot_half)

    lifted = mul(normed2, up_own, 1, 1, None)
    gate_in, up_in = lifted[:, :units], lifted[:, units:]
    gate_act = gate_in * jax.nn.sigmoid(gate_in)
    inner = (gate_act * up_in).astype(BF16)
    grad_inner = mul(cot_all, down_own, 1, 1, None)
    grad_lifted = jnp.concatenate(
        [grad_inner * up_in * dsilu(gate_in), grad_inner * gate_act], axis=1
    ).astype(BF16)
    grad_normed2 = group.scatter(mul(grad_lifted, up_own, 1, 0, None))
    grad_hidden_norm, grad_norm2 = norm_back(hidden, inverse2, norm2_gain, grad_normed2)
    grad_hidden = cot_half.astype(F32) + grad_hidden_norm
    grad_branch_half = grad_hidden.astype(BF16)

    other_branch = group.other_core(grad_branch_half)
    grad_branch = jnp.where(
        core == 0,
        jnp.concatenate([grad_branch_half, other_branch], 0),
        jnp.concatenate([other_branch, grad_branch_half], 0),
    )
    grad_gated = by_token(mul(grad_branch, out_all, 1, 1, None).astype(BF16))
    decays = jnp.exp(jnp.concatenate([totals[1:] - totals[:-1], jnp.log(own_decay) - totals[-1:]], axis=0))
    grad_mixed, grad_gate_rows, grad_group, start_grad = call(
        gate_back_kernel,
        [wide(1), wide(1, BF16), ((PAD, HEAD_DIM), F32), square],
        (grad_gated, mixed, gate_rows, gain, query, decays),
    )
    back_carry = group.carry(start_grad, own_decay, -1)
    grad_rows3, edge, small = call(
        backward_kernel,
        [wide(3), ((PAD, 3 * HEAD_DIM), F32), ((16, HEAD_DIM), F32)],
        (grad_mixed, conv, query, key, states, back_carry, halo, rows3, taps, gap),
        [
            pltpu.VMEM((length + PAD, 3 * HEAD_DIM), F32),
            pltpu.VMEM((length + 2 * PAD, 3 * HEAD_DIM), F32),
        ],
    )
    later = group.shift(edge, -1)
    grad_rows3 = jnp.concatenate([grad_rows3[: length - PAD], grad_rows3[length - PAD :] + later], axis=0)
    grad_projected = jnp.concatenate([grad_rows3.astype(BF16), grad_gate_rows], axis=1)

    grad_mix = mul(normed1, grad_projected, 0, 0, None).astype(BF16)
    mix_total = to_shards(group, grad_mix.reshape(peers, depth, 4 * HEAD_DIM))
    mix_total = mix_total.reshape(heads, depth, 4, HEAD_DIM).transpose(2, 1, 0, 3).reshape(4, depth, heads * HEAD_DIM)

    grad_normed1 = group.scatter(mul(grad_projected, mix_own, 1, 1, None))
    grad_rows1, grad_norm1 = norm_back(half_tokens, half_inverse1, norm1_gain, grad_normed1)
    grad_tokens = grad_hidden + grad_rows1

    def columns(rows):
        return rows.astype(BF16).reshape(-1, peers, depth).transpose(1, 0, 2)

    up_total = to_shards(group, columns(mul(grad_lifted, normed2, 0, 0, None)))
    up_total = up_total.reshape(heads, 2, units, depth).transpose(1, 3, 0, 2).reshape(2, depth, heads * units)
    down_total = to_shards(group, columns(mul(inner, cot_all, 0, 0, None)))
    down_total = down_total.reshape(heads * units, depth)
    branch_all = group.gather(grad_branch_half)
    out_total = to_shards(group, columns(mul(gated, branch_all, 0, 0, None))).reshape(heads * HEAD_DIM, depth)

    block_half = hidden + group.scatter(mul(inner, down_own, 1, 0, None))

    def both_halves(rows):
        other = group.other_core(rows)
        return jnp.where(core == 0, jnp.concatenate([rows, other], 0), jnp.concatenate([other, rows], 0))

    block_out = both_halves(block_half)
    grad_tokens = both_halves(grad_tokens)
    inverse2 = both_halves(inverse2)

    own_small = jnp.concatenate([small[:13], grad_group[:1]], axis=0)
    placed = lax.dynamic_update_slice(jnp.zeros((14, heads * HEAD_DIM), F32), own_small, (0, member * HEAD_DIM))
    small_total, norms = lax.psum((placed, jnp.stack([grad_norm1, grad_norm2])), "seq")
    norms = norms + group.other_core(norms)
    inverse_rms = jnp.stack([inverse1[:, 0], inverse2[:, 0]])
    return (
        block_out,
        grad_tokens,
        norms[0],
        mix_total,
        small_total[:12].reshape(3, 4, heads * HEAD_DIM),
        small_total[12],
        small_total[13],
        out_total,
        norms[1],
        up_total,
        down_total,
        inverse_rms,
    )


def solution(mesh):
    in_specs = (
        P("seq", None),
        P(),
        P(None, "seq", "head"),
        P(None, None, "head"),
        P("head"),
        P("head"),
        P("head", "seq"),
        P(),
        P(None, "seq", "head"),
        P("head", "seq"),
        P("seq", None),
    )
    out_specs = (
        P("seq", None),
        P("seq", None),
        P(),
        P(None, "seq", "head"),
        P(None, None, "head"),
        P("head"),
        P("head"),
        P("head", "seq"),
        P(),
        P(None, "seq", "head"),
        P("head", "seq"),
        P(None, "seq"),
    )
    return jax.shard_map(shards, mesh=mesh, in_specs=in_specs, out_specs=out_specs, check_vma=False)
```

```python
import functools

import jax
import jax.numpy as jnp
from jax import lax
from jax.experimental import pallas as pl
from jax.experimental.pallas import tpu as pltpu
from jax.sharding import PartitionSpec as P

HEAD_DIM = 128
CHUNK = 128
PAD = 8
STEP = 4
EPS_TOKEN = 1e-06
EPS_GROUP = 1e-05
HIGH = lax.Precision.HIGHEST
F32 = jnp.float32
BF16 = jnp.bfloat16
VMEM_LIMIT = 48 * 1024 * 1024


def mul(a, b, ca, cb, precision=HIGH):
    return lax.dot_general(
        a, b, (((ca,), (cb,)), ((), ())), precision=precision, preferred_element_type=F32
    )


def dsilu(v):
    s = jax.nn.sigmoid(v)
    return s * (1.0 + v * (1.0 - s))


def triangle(lower):
    row = lax.broadcasted_iota(jnp.int32, (CHUNK, CHUNK), 0)
    col = lax.broadcasted_iota(jnp.int32, (CHUNK, CHUNK), 1)
    return (row >= col) if lower else (row <= col)


def forward_kernel(
    proj, halo, taps, gap, conv_out, query_out, key_out, total_out, state_out, local_out, last_out, rows
):
    length = proj.shape[0]
    rows[0:16, :] = halo[...].astype(F32)
    rows[16:, :] = proj[:, : 3 * HEAD_DIM].astype(F32)
    lower = triangle(True)
    ones = lower.astype(F32)
    state = jnp.zeros((HEAD_DIM, HEAD_DIM), F32)
    before = jnp.zeros((1, HEAD_DIM), F32)
    for c in range(length // CHUNK):
        at = c * CHUNK
        here = slice(at, at + CHUNK)
        conv = []
        for j in range(3):
            cols = slice(j * HEAD_DIM, (j + 1) * HEAD_DIM)
            total = taps[4 * j : 4 * j + 1, :] * rows[16 + at : 16 + at + CHUNK, cols]
            for d in range(1, 4):
                total = total + taps[4 * j + d : 4 * j + d + 1, :] * rows[16 + at - d : 16 + at - d + CHUNK, cols]
            conv.append(total)
            conv_out[here, cols] = total
        queries = conv[0] * jax.nn.sigmoid(conv[0])
        open_share = 1.0 - jax.nn.sigmoid(conv[1])
        keys = gap[...] * open_share
        log_forget = jnp.log(1.0 - keys)
        values = conv[2]
        running = mul(ones, log_forget, 1, 0)
        last = running[CHUNK - 1 : CHUNK, :]
        query = queries * jnp.exp(running)
        key = keys * jnp.exp(-running)
        carried = keys * jnp.exp(last - running)
        query_out[here, :] = query
        key_out[here, :] = key
        total_out[c : c + 1, :] = before
        state_out[c] = state
        scores = jnp.where(lower, mul(query, key, 1, 1), 0.0)
        local_out[here, :] = mul(scores, values, 1, 0) + mul(query, state, 1, 1)
        state = state * jnp.exp(last) + mul(values, carried, 0, 0)
        before = before + last
    last_out[0:HEAD_DIM, :] = state
    last_out[HEAD_DIM:, :] = jnp.broadcast_to(jnp.exp(before), (PAD, HEAD_DIM))


def gate_kernel(
    ids, local, query, total, state, carry, gate, gain, weights, mixed_out, state_out, turned_out, mine, away, gated
):
    length = local.shape[0]
    members, half, _ = mine.shape
    start = carry[...]
    for c in range(length // CHUNK):
        here = slice(c * CHUNK, (c + 1) * CHUNK)
        grown = start * jnp.exp(total[c : c + 1, :])
        state_out[c] = state[c] + grown
        mixed = local[here, :] + mul(query[here, :], grown, 1, 1)
        mixed_out[here, :] = mixed
        inverse = lax.rsqrt(jnp.mean(mixed * mixed, axis=-1, keepdims=True) + EPS_GROUP)
        g = gate[here, 3 * HEAD_DIM :].astype(F32)
        gated[here, :] = (mixed * inverse * gain[...] * (g * jax.nn.sigmoid(g))).astype(BF16)
    parts = []
    for k, b, block in blocks_of(ids, members):
        parts.append(gated[pl.ds(pl.multiple_of(block * half, half), half), :])
        if len(parts) == STEP:
            x = jnp.concatenate(parts, axis=0)
            at = (k * members + b + 1 - STEP) * half
            turned_out[:, at : at + STEP * half] = x.astype(F32).T.astype(BF16)
            result = mul(x, weights[:, 4 * HEAD_DIM :], 1, 1, None).astype(BF16)
            (mine, away)[k][b + 1 - STEP : b + 1] = result.reshape(STEP, half, -1)
            parts = []


def gate_back_kernel(
    ids, *refs, members
):
    own, other = refs[:members], refs[members : 2 * members]
    weights, mixed, gate, gain, query, decay = refs[2 * members : 2 * members + 6]
    grad_mixed_out, grad_gate_out, grad_gain_out, start_out, grad_gated = refs[2 * members + 6 :]
    half = own[0].shape[0]
    at = 0
    blocks = list(blocks_of(ids, members))
    for at in range(0, len(blocks), STEP):
        k, b, _ = blocks[at]
        result = mul(rows_of((own, other)[k], b), weights[:, 4 * HEAD_DIM :], 1, 0, None)
        for i in range(STEP):
            to = pl.multiple_of(blocks[at + i][2] * half, half)
            grad_gated[pl.ds(to, half), :] = result[i * half : (i + 1) * half]
    length = mixed.shape[0]
    count = length // CHUNK
    grad_gain = jnp.zeros((1, HEAD_DIM), F32)
    state = jnp.zeros((HEAD_DIM, HEAD_DIM), F32)
    for c in reversed(range(count)):
        here = slice(c * CHUNK, (c + 1) * CHUNK)
        grad = grad_gated[here, :]
        mix = mixed[here, :]
        inverse = lax.rsqrt(jnp.mean(mix * mix, axis=-1, keepdims=True) + EPS_GROUP)
        g = gate[here, 3 * HEAD_DIM :].astype(F32)
        s = jax.nn.sigmoid(g)
        unit = mix * inverse
        w = grad * gain[...] * (g * s)
        grad_gain = grad_gain + jnp.sum(grad * unit * (g * s), axis=0, keepdims=True)
        grad_gate_out[here, :] = (grad * unit * gain[...] * (s * (1.0 + g * (1.0 - s)))).astype(BF16)
        grad_mixed = inverse * w - mix * (inverse * inverse * inverse) * jnp.mean(w * mix, axis=-1, keepdims=True)
        grad_mixed_out[here, :] = grad_mixed
        state = state * decay[c : c + 1, :] + mul(grad_mixed, query[here, :], 0, 0)
    start_out[...] = state
    grad_gain_out[...] = jnp.broadcast_to(grad_gain, (PAD, HEAD_DIM))


def backward_kernel(
    grad_mixed,
    conv,
    query,
    key,
    states,
    carry,
    halo,
    proj,
    taps,
    gap,
    grad_out,
    tail_out,
    edge_out,
    small_out,
    rows,
    grads,
):
    length = grad_mixed.shape[0]
    count = length // CHUNK
    rows[0:16, :] = halo[...].astype(F32)
    rows[16:, :] = proj[:, : 3 * HEAD_DIM].astype(F32)
    grads[0:PAD, :] = jnp.zeros((PAD, 3 * HEAD_DIM), F32)
    grads[PAD + length :, :] = jnp.zeros((PAD, 3 * HEAD_DIM), F32)
    lower = triangle(True)
    ones = lower.astype(F32)
    upper = triangle(False).astype(F32)
    last_row = lax.broadcasted_iota(jnp.int32, (CHUNK, HEAD_DIM), 0) == CHUNK - 1
    back = carry[...]
    grad_gap = jnp.zeros((1, HEAD_DIM), F32)
    sums = [jnp.zeros((1, HEAD_DIM), F32) for _ in range(12)]
    for c in reversed(range(count)):
        at = c * CHUNK
        here = slice(at, at + CHUNK)
        c0, c1, values = (conv[here, j * HEAD_DIM : (j + 1) * HEAD_DIM] for j in range(3))
        s1 = jax.nn.sigmoid(c1)
        open_share = 1.0 - s1
        keys = gap[...] * open_share
        forget = 1.0 - keys
        running = mul(ones, jnp.log(forget), 1, 0)
        last = running[CHUNK - 1 : CHUNK, :]
        grown, shrunk, rest = jnp.exp(running), jnp.exp(-running), jnp.exp(last - running)
        q, k, g = query[here, :], key[here, :], grad_mixed[here, :]
        carried = keys * rest
        state = states[c]
        scores = jnp.where(lower, mul(q, k, 1, 1), 0.0)
        grad_scores = jnp.where(lower, mul(g, values, 1, 1), 0.0)
        grad_values = mul(scores, g, 0, 0) + mul(carried, back, 1, 1)
        grad_query = mul(grad_scores, k, 1, 0) + mul(g, state, 1, 0)
        grad_key = mul(grad_scores, q, 0, 0)
        grad_carried = mul(values, back, 1, 0)
        grad_last = jnp.exp(last) * jnp.sum(back * state, axis=0, keepdims=True) + jnp.sum(
            grad_carried * carried, axis=0, keepdims=True
        )
        grad_running = grad_query * q - grad_key * k - grad_carried * carried
        grad_running = grad_running + jnp.where(last_row, grad_last, 0.0)
        grad_keys = grad_key * shrunk + grad_carried * rest
        grad_forget = mul(upper, grad_running, 1, 0) / forget
        inner = grad_forget - grad_keys
        grad_gap = grad_gap - jnp.sum(open_share * inner, axis=0, keepdims=True)
        sigmoid0 = jax.nn.sigmoid(c0)
        new = (
            grad_query * grown * (sigmoid0 * (1.0 + c0 * (1.0 - sigmoid0))),
            gap[...] * s1 * open_share * inner,
            grad_values,
        )
        back = back * jnp.exp(last) + mul(g, q, 0, 0)
        for j in range(3):
            cols = slice(j * HEAD_DIM, (j + 1) * HEAD_DIM)
            grads[PAD + at : PAD + at + CHUNK, cols] = new[j]
            for d in range(4):
                sums[4 * j + d] = sums[4 * j + d] + jnp.sum(
                    new[j] * rows[16 + at - d : 16 + at - d + CHUNK, cols], axis=0, keepdims=True
                )
            total = taps[4 * j : 4 * j + 1, :] * new[j]
            for d in range(1, 4):
                total = total + taps[4 * j + d : 4 * j + d + 1, :] * grads[PAD + at + d : PAD + at + d + CHUNK, cols]
            grad_out[here, cols] = total.astype(BF16)
            if c == count - 1:
                tail_out[:, cols] = total[CHUNK - 16 :]
    for j in range(3):
        cols = slice(j * HEAD_DIM, (j + 1) * HEAD_DIM)
        total = taps[4 * j + 1 : 4 * j + 2, :] * grads[1 : 1 + PAD, cols]
        for d in range(2, 4):
            total = total + taps[4 * j + d : 4 * j + d + 1, :] * grads[d : d + PAD, cols]
        edge_out[:, cols] = total
    for i in range(12):
        small_out[i : i + 1, :] = sums[i]
    small_out[12:13, :] = grad_gap
    small_out[13:16, :] = jnp.zeros((3, HEAD_DIM), F32)


def blocks_of(ids, count):
    member, core = ids[0], ids[1]
    for k in range(2):
        for b in range(count):
            yield k, b, (member ^ b) * 2 + (core ^ k)


def rows_of(blocks, first, count=STEP, cols=slice(None)):
    if isinstance(blocks, (tuple, list)):
        return jnp.concatenate([blocks[first + i][:, cols] for i in range(count)], axis=0)
    part = blocks[first : first + count, :, cols]
    return part.reshape(-1, part.shape[-1])


def fill_columns(weights, source, first, target, rows):
    groups, members, _, depth = source.shape
    per = max(1, 128 // depth)
    for at in range(0, groups * members, per):
        parts = [source[(at + i) // members, (at + i) % members, first : first + rows, :] for i in range(per)]
        part = parts[0] if per == 1 else jnp.concatenate(parts, axis=1)
        weights[target : target + rows, at * depth : (at + per) * depth] = part


def mix_blocks_kernel(mix, out_weight, out):
    groups, heads, depth, _ = out.shape
    for m in range(heads):
        cols = slice(m * HEAD_DIM, (m + 1) * HEAD_DIM)
        turned = out_weight[cols, :].astype(F32).T.astype(BF16)
        for g in range(groups):
            for j in range(4):
                out[g, m, :, j * HEAD_DIM : (j + 1) * HEAD_DIM] = mix[j, :, cols]
            out[g, m, :, 4 * HEAD_DIM :] = turned


def up_blocks_kernel(up, out, turned):
    _, _, units = up.shape
    groups, heads, rows, _ = out.shape
    rows = rows // 2
    for j in range(2):
        for t in range(units // 128):
            block = up[j, :, t * 128 : (t + 1) * 128].astype(F32)
            turned[t * 128 : (t + 1) * 128, :] = block.T.astype(BF16)
        for g in range(groups):
            for m in range(heads):
                out[g, m, j * rows : (j + 1) * rows, :] = turned[m * rows : (m + 1) * rows, :]


def project_kernel(ids, *refs, members):
    own, other = refs[:members], refs[members : 2 * members]
    weights, out, tail = refs[2 * members :]
    half = own[0].shape[0]
    blocks = list(blocks_of(ids, members))
    for at in range(0, len(blocks), STEP):
        k, b, _ = blocks[at]
        result = mul(rows_of((own, other)[k], b), weights[:, : 4 * HEAD_DIM], 1, 0, None).astype(BF16)
        for i in range(STEP):
            to = pl.multiple_of(blocks[at + i][2] * half, half)
            out[pl.ds(to, half), :] = result[i * half : (i + 1) * half]
    tail[...] = out[out.shape[0] - 16 :, : tail.shape[1]]


def feed_kernel(*refs, members):
    own, other, cot_own, cot_other = (refs[i * members : (i + 1) * members] for i in range(4))
    up, down, turned, inner_out, mine, away, weights = refs[4 * members :]
    half, width = own[0].shape
    units = down.shape[2]
    wide = turned.shape[0] // 3
    for j in range(3):
        weights[j * wide + units : (j + 1) * wide, :] = jnp.zeros((wide - units, width), BF16)
        fill_columns(weights, *((up, 0), (up, units), (down, 0))[j], j * wide, units)
    for k in range(2):
        for b in range(0, members, STEP):
            x = rows_of((own, other)[k], b)
            c = rows_of((cot_own, cot_other)[k], b)
            lifted = mul(x, weights[: 2 * wide], 1, 1, None)
            gate, up_in = lifted[:, :wide], lifted[:, wide:]
            grad = mul(c, weights[2 * wide :], 1, 1, None)
            s = jax.nn.sigmoid(gate)
            act = gate * s
            inner = act * up_in
            grad_gate = grad * up_in * (s * (1.0 + gate * (1.0 - s)))
            grad_up = grad * act
            at = (k * members + b) * half
            cols = slice(at, at + STEP * half)
            turned[0:wide, cols] = grad_gate.T.astype(BF16)
            turned[wide : 2 * wide, cols] = grad_up.T.astype(BF16)
            turned[2 * wide :, cols] = inner.T.astype(BF16)
            inner_out[cols, :] = inner.astype(BF16)
            lift = jnp.concatenate([grad_gate.astype(BF16), grad_up.astype(BF16)], axis=1)
            (mine, away)[k][b : b + STEP] = (
                mul(lift, weights[: 2 * wide], 1, 0, None).astype(BF16).reshape(STEP, half, width)
            )


def block_kernel(ids, inner, down, mine, away, weights):
    members, half, width = mine.shape
    units, wide = down.shape[2], inner.shape[1]
    weights[units:, :] = jnp.zeros((wide - units, width), BF16)
    fill_columns(weights, down, 0, 0, units)
    for k in range(2):
        for b in range(0, members, STEP):
            at = (k * members + b) * half
            result = mul(inner[at : at + STEP * half, :], weights[...], 1, 0, None).astype(BF16)
            for i in range(STEP):
                (mine, away)[k][ids[0] ^ (b + i)] = result[i * half : (i + 1) * half]


def store_shards(out, at, first, result):
    depth = out.shape[3]
    for i in range(result.shape[1] // depth):
        part = result[:, i * depth : (i + 1) * depth].astype(BF16)
        out[(at + i) // out.shape[1], (at + i) % out.shape[1], first : first + part.shape[0], :] = part


def product_into(out, first, turned, spans, own, other, members):
    rows = turned.shape[1] // 2
    width = out.shape[0] * out.shape[1] * out.shape[3]
    low, high = spans[0][0], spans[-1][1]
    for at in range(0, width, 256):
        cols = slice(at, at + 256)
        result = mul(turned[low:high, :rows], rows_of(own, 0, members, cols), 1, 0, None)
        result += mul(turned[low:high, rows:], rows_of(other, 0, members, cols), 1, 0, None)
        to = first
        for start, stop in spans:
            store_shards(out, at // out.shape[3], to, result[start - low : stop - low])
            to += stop - start


def feed_grad_kernel(*refs, members):
    own, other, cot_own, cot_other = (refs[i * members : (i + 1) * members] for i in range(4))
    turned, out = refs[4 * members :]
    units, wide = out.shape[2] // 3, turned.shape[0] // 3
    product_into(out, 0, turned, [(0, units), (wide, wide + units)], own, other, members)
    product_into(out, 2 * units, turned, [(2 * wide, 2 * wide + units)], cot_own, cot_other, members)


def mix_grad_kernel(*refs, members):
    own, other, branch_own, branch_other = (refs[i * members : (i + 1) * members] for i in range(4))
    turned, turned_gated, sums, out = refs[4 * members :]
    groups, heads, rows, _ = out.shape
    for g in range(groups):
        for m in range(heads):
            out[g, m, 5 * HEAD_DIM :, :] = sums[...]
    product_into(out, 0, turned, [(0, 4 * HEAD_DIM)], own, other, members)
    product_into(out, 4 * HEAD_DIM, turned_gated, [(0, HEAD_DIM)], branch_own, branch_other, members)


def project_back_kernel(ids, *refs, members):
    own, other = refs[:members], refs[members : 2 * members]
    grad3, tail, later, grad_gate, weights, norm_gain, turned, mine_out, away_out, norm_out, grads = refs[2 * members :]
    length = grad3.shape[0]
    members, half, width = mine_out.shape
    three = grad3.shape[1]
    grads[:, :three] = grad3[...]
    end = tail.shape[0]
    edge = jnp.concatenate([jnp.zeros((end - later.shape[0], three), F32), later[...]], axis=0)
    grads[length - end :, :three] = (tail[...] + edge).astype(BF16)
    grads[:, three:] = grad_gate[...]
    grad_norm = jnp.zeros((1, width), F32)
    parts = []
    for k, b, block in blocks_of(ids, members):
        parts.append(grads[pl.ds(pl.multiple_of(block * half, half), half), :])
        if len(parts) == STEP:
            x = jnp.concatenate(parts, axis=0)
            at = (k * members + b + 1 - STEP) * half
            turned[:, at : at + STEP * half] = x.astype(F32).T.astype(BF16)
            result = mul(x, weights[:, : 4 * HEAD_DIM], 1, 1, None)
            normed = rows_of((own, other)[k], b + 1 - STEP).astype(F32)
            grad_norm = grad_norm + jnp.sum(result * normed, axis=0, keepdims=True)
            (mine_out, away_out)[k][b + 1 - STEP : b + 1] = result.astype(BF16).reshape(STEP, half, width)
            parts = []
    norm_out[...] = jnp.broadcast_to(grad_norm / norm_gain[...], norm_out.shape)


def add_kernel(ids, blocks, got, out):
    for m in range(out.shape[0]):
        out[m] = (blocks[ids[0], m].astype(F32) + got[ids[1], m].astype(F32)).astype(BF16)


def mix_total_kernel(got, mix_out, out_out):
    groups, heads, _, depth = got.shape

    def total(i, rows):
        result = got[0, i, rows, :].astype(F32)
        for g in range(1, groups):
            result = result + got[g, i, rows, :].astype(F32)
        return result

    for i in range(heads):
        cols = slice(i * HEAD_DIM, (i + 1) * HEAD_DIM)
        for j in range(4):
            mix_out[j, :, cols] = total(i, slice(j * HEAD_DIM, (j + 1) * HEAD_DIM)).T
        out_out[cols, :] = total(i, slice(4 * HEAD_DIM, 5 * HEAD_DIM))


def feed_total_kernel(got, up_out, down_out, rows):
    heads, three, depth = got.shape
    units = three // 3
    for j in range(2):
        for i in range(heads):
            rows[i * units : (i + 1) * units, :] = got[i, j * units : (j + 1) * units, :].astype(F32)
        for t in range(heads * units // 128):
            up_out[j, :, t * 128 : (t + 1) * 128] = rows[t * 128 : (t + 1) * 128, :].T
    for i in range(heads):
        down_out[i * units : (i + 1) * units, :] = got[i, 2 * units :, :].astype(F32)


def call(kernel, outs, args, scratch=(), ids=None, behind=(), us=5):
    specs = [pl.BlockSpec(memory_space=pltpu.VMEM)] * len(args)
    if ids is not None:
        specs = [pl.BlockSpec(memory_space=pltpu.SMEM)] + specs
        args = (ids,) + tuple(args)
    real = len(args)

    def body(*refs):
        kernel(*refs[:real], *refs[real + len(behind) :])

    return pl.pallas_call(
        body,
        out_shape=[jax.ShapeDtypeStruct(s, d) for s, d in outs],
        in_specs=specs + [pl.BlockSpec(memory_space=pl.ANY)] * len(behind),
        out_specs=[pl.BlockSpec(memory_space=pltpu.VMEM)] * len(outs),
        scratch_shapes=list(scratch),
        compiler_params=pltpu.CompilerParams(vmem_limit_bytes=VMEM_LIMIT),
        cost_estimate=pl.CostEstimate(flops=0, bytes_accessed=us * 3000000, transcendentals=0),
    )(*args, *behind)


class Group:
    def __init__(self, heads):
        self.size = heads
        self.peers = lax.axis_size("seq")
        self.count = self.peers // heads
        self.member = lax.rem(lax.axis_index("seq"), heads)
        self.index = lax.div(lax.axis_index("seq"), heads)
        self.core = lax.axis_index("head")
        self.ids = jnp.stack([self.member, self.core]).astype(jnp.int32)
        self.lists = [list(range(g * heads, (g + 1) * heads)) for g in range(self.count)]
        self.columns = [list(range(m, self.peers, heads)) for m in range(heads)]

    def swap(self, value, bits):
        return lax.ppermute(value, "seq", [(s, s ^ bits) for s in range(self.peers)])

    def other_core(self, value):
        return lax.ppermute(value, "head", [(0, 1), (1, 0)])

    def shift(self, value, groups):
        step = groups * self.size
        pairs = [(s, s + step) for s in range(self.peers) if 0 <= s + step < self.peers]
        return lax.ppermute(value, "seq", pairs)

    def carry(self, state, decay, sign):
        total = None
        for k in reversed(range(1, self.count)):
            new = self.shift(state, sign * k)
            total = new if total is None else new + total * self.shift(decay, sign * k)
        return jnp.zeros_like(state) if total is None else total

    def gather(self, half):
        got = {0: half}
        for bits in (4, 1, 2):
            got[bits] = self.swap(half, bits)
        got[6] = self.swap(got[4], 2)
        got[5] = self.swap(got[4], 1)
        got[3] = self.swap(got[2], 1)
        got[7] = self.swap(got[5], 2)
        own = [got[bits] for bits in range(self.size)]
        return own, [self.other_core(block) for block in own]

    def scatter(self, mine, away, meanwhile=None):
        other = self.other_core(away)
        part = [mine[b].astype(F32) + other[b].astype(F32) for b in range(self.size)]

        def add(to, source, bits):
            part[to] = part[to] + self.swap(part[source].astype(BF16), bits).astype(F32)

        add(5, 7, 2)
        add(2, 3, 1)
        add(4, 6, 2)
        add(0, 1, 1)
        if meanwhile is not None:
            part[5] = after(part[5], meanwhile)
        add(4, 5, 1)
        add(0, 2, 2)
        add(0, 4, 4)
        return part[0]

    def spread(self, blocks):
        return lax.all_to_all(blocks, "seq", 0, 0, axis_index_groups=self.lists, tiled=True)

    def all_groups(self, value):
        return lax.all_gather(value, "seq", axis_index_groups=self.columns)

    def over_groups(self, blocks, behind):
        if self.count == 2:
            away = lax.dynamic_index_in_dim(blocks, 1 - self.index, 0, False)
            (total,) = call(
                add_kernel,
                [(away.shape, BF16)],
                (blocks, self.all_groups(away)),
                (),
                jnp.stack([self.index, 1 - self.index]).astype(jnp.int32),
                behind,
            )
            return total
        return lax.psum_scatter(blocks, "seq", axis_index_groups=self.columns)


def inverse_of(rows):
    return lax.rsqrt(jnp.mean(rows * rows, axis=-1, keepdims=True) + EPS_TOKEN)


def norm_back(rows, inverse, gain, grad):
    scaled = grad * gain
    dot_term = jnp.mean(scaled * rows, axis=-1, keepdims=True)
    grad_rows = inverse * scaled - rows * (inverse * inverse * inverse) * dot_term
    return grad_rows, jnp.sum(grad * rows * inverse, axis=0)


def after(value, *earlier):
    return lax.optimization_barrier((value,) + earlier)[0]


def shards(
    tokens,
    norm1_gain,
    mix_weight,
    conv_weight,
    decay_gap,
    group_gain,
    out_weight,
    norm2_gain,
    up_pair,
    down_weight,
    cotangent,
):
    depth = mix_weight.shape[1]
    heads = mix_weight.shape[2] // HEAD_DIM
    units = down_weight.shape[0] // heads
    wide = -(-units // 128) * 128
    local, width = tokens.shape
    half = local // 2
    group = Group(heads)
    ids, member, core = group.ids, group.member, group.core
    length = heads * local
    count = length // CHUNK
    groups, peers = group.count, group.peers

    def my_half(rows):
        return lax.dynamic_slice_in_dim(rows, core * half, half, 0)

    def own_head(array):
        return lax.dynamic_slice_in_dim(array, member * HEAD_DIM, HEAD_DIM, array.ndim - 1)

    taps = own_head(conv_weight).reshape(12, HEAD_DIM)
    gap = own_head(decay_gap).reshape(1, HEAD_DIM)
    gain = own_head(group_gain).reshape(1, HEAD_DIM)

    token_rows = tokens.astype(F32)
    inverse1 = inverse_of(token_rows)
    half_tokens = my_half(token_rows)
    half_inverse1 = my_half(inverse1)
    cot_half = my_half(cotangent)
    down_here = group.spread(down_weight.reshape(heads, units, depth))
    normed1, normed1_other = group.gather((half_tokens * half_inverse1 * norm1_gain).astype(BF16))
    cot, cot_other = group.gather(cot_half)
    (mix_blocks,) = call(
        mix_blocks_kernel,
        [((groups, heads, depth, 5 * HEAD_DIM), BF16)],
        (mix_weight, out_weight),
        (),
        None,
        (normed1[5], cot[5], down_here),
    )
    mix_own = lax.all_to_all(mix_blocks.reshape(peers, depth, 5 * HEAD_DIM), "seq", 0, 0, tiled=True)
    mix_own = mix_own.reshape(width, 5 * HEAD_DIM)
    (up_blocks,) = call(
        up_blocks_kernel,
        [((groups, heads, 2 * units, depth), BF16)],
        (up_pair,),
        [pltpu.VMEM((heads * units, depth), BF16)],
        None,
        (mix_blocks,),
        3,
    )
    down_own = group.all_groups(down_here)
    projected, tail = call(
        functools.partial(project_kernel, members=heads),
        [((length, 4 * HEAD_DIM), BF16), ((16, 3 * HEAD_DIM), BF16)],
        (*normed1, *normed1_other, mix_own),
        (),
        ids,
    )
    halo = group.shift(tail, 1)

    def many(n, dtype=F32):
        return ((length, n * HEAD_DIM), dtype)

    square = ((HEAD_DIM, HEAD_DIM), F32)
    all_rows = ((heads, half, width), BF16)
    conv, query, key, totals, states, mixed_here, last = call(
        forward_kernel,
        [
            many(3),
            many(1),
            many(1),
            ((count, HEAD_DIM), F32),
            ((count, HEAD_DIM, HEAD_DIM), F32),
            many(1),
            ((HEAD_DIM + PAD, HEAD_DIM), F32),
        ],
        (projected, halo, taps, gap),
        [pltpu.VMEM((length + 16, 3 * HEAD_DIM), F32)],
        None,
        cot_other,
    )
    own_decay = last[HEAD_DIM : HEAD_DIM + 1]
    carry = group.carry(last[:HEAD_DIM], own_decay, 1)
    up_own = lax.all_to_all(
        after(up_blocks.reshape(peers, 2 * units, depth), carry), "seq", 0, 0, tiled=True
    )
    up_own = up_own.reshape(groups, heads, 2 * units, depth)
    mixed, states, turned_gated, mine, away = call(
        gate_kernel,
        [many(1), ((count, HEAD_DIM, HEAD_DIM), F32), ((HEAD_DIM, length), BF16), all_rows, all_rows],
        (mixed_here, query, totals, states, carry, projected, gain, mix_own),
        [pltpu.VMEM((length, HEAD_DIM), BF16)],
        ids,
    )
    hidden = half_tokens + group.scatter(mine, away, up_own)
    inverse2 = inverse_of(hidden)
    normed2, normed2_other = group.gather((hidden * inverse2 * norm2_gain).astype(BF16))

    turned, inner, mine, away = call(
        functools.partial(feed_kernel, members=heads),
        [((3 * wide, length), BF16), ((length, wide), BF16), all_rows, all_rows],
        (*normed2, *normed2_other, *cot, *cot_other, up_own, down_own),
        [pltpu.VMEM((3 * wide, width), BF16)],
        us=17,
    )
    (grad_feed,) = call(
        functools.partial(feed_grad_kernel, members=heads),
        [((groups, heads, 3 * units, depth), BF16)],
        (*normed2, *normed2_other, *cot, *cot_other, turned),
        us=10,
    )
    grad_normed2 = group.scatter(mine, away, grad_feed)
    grad_hidden_norm, grad_norm2 = norm_back(hidden, inverse2, norm2_gain, grad_normed2)
    grad_hidden = cot_half.astype(F32) + grad_hidden_norm
    branch, branch_other = group.gather(grad_hidden.astype(BF16))

    decays = jnp.exp(jnp.concatenate([totals[1:] - totals[:-1], jnp.log(own_decay) - totals[-1:]], axis=0))
    grad_mixed, grad_gate_rows, grad_group, start_grad = call(
        functools.partial(gate_back_kernel, members=heads),
        [many(1), many(1, BF16), ((PAD, HEAD_DIM), F32), square],
        (*branch, *branch_other, mix_own, mixed, projected, gain, query, decays),
        [pltpu.VMEM((length, HEAD_DIM), F32)],
        ids,
    )
    back_carry = group.carry(start_grad, own_decay, -1)
    grad_rows3, grad_tail, edge, small = call(
        backward_kernel,
        [many(3, BF16), ((16, 3 * HEAD_DIM), F32), ((PAD, 3 * HEAD_DIM), F32), ((16, HEAD_DIM), F32)],
        (grad_mixed, conv, query, key, states, back_carry, halo, projected, taps, gap),
        [
            pltpu.VMEM((length + 16, 3 * HEAD_DIM), F32),
            pltpu.VMEM((length + 2 * PAD, 3 * HEAD_DIM), F32),
        ],
    )
    later = group.shift(edge, -1)
    turned_mix, mine, away, grad_norm1 = call(
        functools.partial(project_back_kernel, members=heads),
        [((4 * HEAD_DIM, length), BF16), all_rows, all_rows, ((PAD, width), F32)],
        (
            *normed1,
            *normed1_other,
            grad_rows3,
            grad_tail,
            later,
            grad_gate_rows,
            mix_own,
            norm1_gain.reshape(1, width),
        ),
        [pltpu.VMEM((length, 4 * HEAD_DIM), BF16)],
        ids,
    )
    sums = jnp.concatenate([small[:13].reshape(-1), grad_group[0], grad_norm1[0], grad_norm2]).astype(BF16)
    extra = -(-sums.shape[0] // (16 * depth)) * 16
    sums = jnp.pad(sums, (0, extra * depth - sums.shape[0])).reshape(extra, depth)
    (grad_mix,) = call(
        functools.partial(mix_grad_kernel, members=heads),
        [((groups, heads, 5 * HEAD_DIM + extra, depth), BF16)],
        (*normed1, *normed1_other, *branch, *branch_other, turned_mix, turned_gated, sums),
        us=7,
    )
    feed_total = group.over_groups(grad_feed, (grad_mix,))
    grad_mix = after(grad_mix.reshape(peers, 5 * HEAD_DIM + extra, depth), feed_total)
    mix_got = lax.all_to_all(grad_mix, "seq", 0, 0, tiled=True)
    grad_normed1 = group.scatter(mine, after(away, grad_mix))
    feed_got = group.spread(after(feed_total, mix_got))
    mix_total, out_total = call(
        mix_total_kernel,
        [((4, depth, heads * HEAD_DIM), F32), ((heads * HEAD_DIM, depth), F32)],
        (mix_got.reshape(groups, heads, 5 * HEAD_DIM + extra, depth),),
    )
    grad_rows1 = norm_back(half_tokens, half_inverse1, norm1_gain, grad_normed1)[0]
    grad_tokens = grad_hidden + grad_rows1

    up_total, down_total = call(
        feed_total_kernel,
        [((2, depth, heads * units), F32), ((heads * units, depth), F32)],
        (feed_got,),
        [pltpu.VMEM((heads * units, depth), F32)],
    )
    (block_mine, block_away) = call(
        block_kernel, [all_rows, all_rows], (inner, down_own), [pltpu.VMEM((wide, width), BF16)], ids, (grad_mix,)
    )
    block = (block_mine.astype(F32) + group.other_core(block_away).astype(F32)).astype(BF16)
    block_half = hidden + lax.psum_scatter(block, "seq", axis_index_groups=group.lists).astype(F32)

    def both_halves(rows):
        other = group.other_core(rows)
        return jnp.where(core == 0, jnp.concatenate([rows, other], 0), jnp.concatenate([other, rows], 0))

    block_out = both_halves(block_half)
    grad_tokens = both_halves(grad_tokens)
    inverse2 = both_halves(inverse2)

    sums = mix_got[:, 5 * HEAD_DIM :].reshape(groups, heads, -1).astype(F32).sum(0)
    own_sums = sums[:, : 14 * HEAD_DIM].reshape(heads, 14, HEAD_DIM).transpose(1, 0, 2).reshape(14, heads * HEAD_DIM)
    norms = sums[:, 14 * HEAD_DIM : 14 * HEAD_DIM + 2 * width].sum(0).reshape(2, width)
    norms = norms + group.other_core(norms)
    inverse_rms = jnp.stack([inverse1[:, 0], inverse2[:, 0]])
    return (
        block_out,
        grad_tokens,
        norms[0],
        mix_total,
        own_sums[:12].reshape(3, 4, heads * HEAD_DIM),
        own_sums[12],
        own_sums[13],
        out_total,
        norms[1],
        up_total,
        down_total,
        inverse_rms,
    )


def solution(mesh):
    in_specs = (
        P("seq", None),
        P(),
        P(None, "seq", "head"),
        P(None, None, "head"),
        P("head"),
        P("head"),
        P("head", "seq"),
        P(),
        P(None, "seq", "head"),
        P("head", "seq"),
        P("seq", None),
    )
    out_specs = (
        P("seq", None),
        P("seq", None),
        P(),
        P(None, "seq", "head"),
        P(None, None, "head"),
        P("head"),
        P("head"),
        P("head", "seq"),
        P(),
        P(None, "seq", "head"),
        P("head", "seq"),
        P(None, "seq"),
    )
    return jax.shard_map(shards, mesh=mesh, in_specs=in_specs, out_specs=out_specs, check_vma=False)
```

```python
import functools

import jax
import jax.numpy as jnp
from jax import lax
from jax.experimental import pallas as pl
from jax.experimental.pallas import tpu as pltpu
from jax.sharding import PartitionSpec as P

HEAD_DIM = 128
CHUNK = 128
PAD = 8
STEP = 4
EPS_TOKEN = 1e-06
EPS_GROUP = 1e-05
HIGH = lax.Precision.HIGHEST
F32 = jnp.float32
BF16 = jnp.bfloat16
MIB = 1024 * 1024


def mul(a, b, ca, cb, precision=HIGH):
    return lax.dot_general(
        a, b, (((ca,), (cb,)), ((), ())), precision=precision, preferred_element_type=F32
    )


def dsilu(v):
    s = jax.nn.sigmoid(v)
    return s * (1.0 + v * (1.0 - s))


def triangle(lower):
    row = lax.broadcasted_iota(jnp.int32, (CHUNK, CHUNK), 0)
    col = lax.broadcasted_iota(jnp.int32, (CHUNK, CHUNK), 1)
    return (row >= col) if lower else (row <= col)


def forward_kernel(
    proj, halo, taps, gap, conv_out, query_out, key_out, total_out, state_out, local_out, last_out, rows
):
    length = proj.shape[0]
    rows[0:16, :] = halo[...].astype(F32)
    rows[16:, :] = proj[:, : 3 * HEAD_DIM].astype(F32)
    lower = triangle(True)
    ones = lower.astype(F32)
    state = jnp.zeros((HEAD_DIM, HEAD_DIM), F32)
    before = jnp.zeros((1, HEAD_DIM), F32)
    for c in range(length // CHUNK):
        at = c * CHUNK
        here = slice(at, at + CHUNK)
        conv = []
        for j in range(3):
            cols = slice(j * HEAD_DIM, (j + 1) * HEAD_DIM)
            total = taps[4 * j : 4 * j + 1, :] * rows[16 + at : 16 + at + CHUNK, cols]
            for d in range(1, 4):
                total = total + taps[4 * j + d : 4 * j + d + 1, :] * rows[16 + at - d : 16 + at - d + CHUNK, cols]
            conv.append(total)
            conv_out[here, cols] = total
        queries = conv[0] * jax.nn.sigmoid(conv[0])
        open_share = 1.0 - jax.nn.sigmoid(conv[1])
        keys = gap[...] * open_share
        log_forget = jnp.log(1.0 - keys)
        values = conv[2]
        running = mul(ones, log_forget, 1, 0)
        last = running[CHUNK - 1 : CHUNK, :]
        query = queries * jnp.exp(running)
        key = keys * jnp.exp(-running)
        carried = keys * jnp.exp(last - running)
        query_out[here, :] = query
        key_out[here, :] = key
        total_out[c : c + 1, :] = before
        state_out[c] = state
        scores = jnp.where(lower, mul(query, key, 1, 1), 0.0)
        local_out[here, :] = mul(scores, values, 1, 0) + mul(query, state, 1, 1)
        state = state * jnp.exp(last) + mul(values, carried, 0, 0)
        before = before + last
    last_out[0:HEAD_DIM, :] = state
    last_out[HEAD_DIM:, :] = jnp.broadcast_to(jnp.exp(before), (PAD, HEAD_DIM))


def gate_kernel(
    ids, local, query, total, state, carry, gate, gain, weights, mixed_out, state_out, turned_out, mine, away, gated
):
    length = local.shape[0]
    members, half, _ = mine.shape
    start = carry[...]
    for c in range(length // CHUNK):
        here = slice(c * CHUNK, (c + 1) * CHUNK)
        grown = start * jnp.exp(total[c : c + 1, :])
        state_out[c] = state[c] + grown
        mixed = local[here, :] + mul(query[here, :], grown, 1, 1)
        mixed_out[here, :] = mixed
        inverse = lax.rsqrt(jnp.mean(mixed * mixed, axis=-1, keepdims=True) + EPS_GROUP)
        g = gate[here, 3 * HEAD_DIM :].astype(F32)
        gated[here, :] = (mixed * inverse * gain[...] * (g * jax.nn.sigmoid(g))).astype(BF16)
    parts = []
    for k, b, block in blocks_of(ids, members):
        parts.append(gated[pl.ds(pl.multiple_of(block * half, half), half), :])
        if len(parts) == STEP:
            x = jnp.concatenate(parts, axis=0)
            at = (k * members + b + 1 - STEP) * half
            turned_out[:, at : at + STEP * half] = x.astype(F32).T.astype(BF16)
            result = mul(x, weights[:, 4 * HEAD_DIM :], 1, 1, None).astype(BF16)
            (mine, away)[k][b + 1 - STEP : b + 1] = result.reshape(STEP, half, -1)
            parts = []


def gate_back_kernel(
    ids, *refs, members
):
    own, other = refs[:members], refs[members : 2 * members]
    weights, mixed, gate, gain, query, decay = refs[2 * members : 2 * members + 6]
    grad_mixed_out, grad_gate_out, grad_gain_out, start_out, grad_gated = refs[2 * members + 6 :]
    half = own[0].shape[0]
    at = 0
    blocks = list(blocks_of(ids, members))
    for at in range(0, len(blocks), STEP):
        k, b, _ = blocks[at]
        result = mul(rows_of((own, other)[k], b), weights[:, 4 * HEAD_DIM :], 1, 0, None)
        for i in range(STEP):
            to = pl.multiple_of(blocks[at + i][2] * half, half)
            grad_gated[pl.ds(to, half), :] = result[i * half : (i + 1) * half]
    length = mixed.shape[0]
    count = length // CHUNK
    grad_gain = jnp.zeros((1, HEAD_DIM), F32)
    state = jnp.zeros((HEAD_DIM, HEAD_DIM), F32)
    for c in reversed(range(count)):
        here = slice(c * CHUNK, (c + 1) * CHUNK)
        grad = grad_gated[here, :]
        mix = mixed[here, :]
        inverse = lax.rsqrt(jnp.mean(mix * mix, axis=-1, keepdims=True) + EPS_GROUP)
        g = gate[here, 3 * HEAD_DIM :].astype(F32)
        s = jax.nn.sigmoid(g)
        unit = mix * inverse
        w = grad * gain[...] * (g * s)
        grad_gain = grad_gain + jnp.sum(grad * unit * (g * s), axis=0, keepdims=True)
        grad_gate_out[here, :] = (grad * unit * gain[...] * (s * (1.0 + g * (1.0 - s)))).astype(BF16)
        grad_mixed = inverse * w - mix * (inverse * inverse * inverse) * jnp.mean(w * mix, axis=-1, keepdims=True)
        grad_mixed_out[here, :] = grad_mixed
        state = state * decay[c : c + 1, :] + mul(grad_mixed, query[here, :], 0, 0)
    start_out[...] = state
    grad_gain_out[...] = jnp.broadcast_to(grad_gain, (PAD, HEAD_DIM))


def backward_kernel(
    grad_mixed,
    conv,
    query,
    key,
    states,
    carry,
    halo,
    proj,
    taps,
    gap,
    grad_out,
    tail_out,
    edge_out,
    small_out,
    rows,
    grads,
):
    length = grad_mixed.shape[0]
    count = length // CHUNK
    rows[0:16, :] = halo[...].astype(F32)
    rows[16:, :] = proj[:, : 3 * HEAD_DIM].astype(F32)
    grads[0:PAD, :] = jnp.zeros((PAD, 3 * HEAD_DIM), F32)
    grads[PAD + length :, :] = jnp.zeros((PAD, 3 * HEAD_DIM), F32)
    lower = triangle(True)
    ones = lower.astype(F32)
    upper = triangle(False).astype(F32)
    last_row = lax.broadcasted_iota(jnp.int32, (CHUNK, HEAD_DIM), 0) == CHUNK - 1
    back = carry[...]
    grad_gap = jnp.zeros((1, HEAD_DIM), F32)
    sums = [jnp.zeros((1, HEAD_DIM), F32) for _ in range(12)]
    for c in reversed(range(count)):
        at = c * CHUNK
        here = slice(at, at + CHUNK)
        c0, c1, values = (conv[here, j * HEAD_DIM : (j + 1) * HEAD_DIM] for j in range(3))
        s1 = jax.nn.sigmoid(c1)
        open_share = 1.0 - s1
        keys = gap[...] * open_share
        forget = 1.0 - keys
        running = mul(ones, jnp.log(forget), 1, 0)
        last = running[CHUNK - 1 : CHUNK, :]
        grown, shrunk, rest = jnp.exp(running), jnp.exp(-running), jnp.exp(last - running)
        q, k, g = query[here, :], key[here, :], grad_mixed[here, :]
        carried = keys * rest
        state = states[c]
        scores = jnp.where(lower, mul(q, k, 1, 1), 0.0)
        grad_scores = jnp.where(lower, mul(g, values, 1, 1), 0.0)
        grad_values = mul(scores, g, 0, 0) + mul(carried, back, 1, 1)
        grad_query = mul(grad_scores, k, 1, 0) + mul(g, state, 1, 0)
        grad_key = mul(grad_scores, q, 0, 0)
        grad_carried = mul(values, back, 1, 0)
        grad_last = jnp.exp(last) * jnp.sum(back * state, axis=0, keepdims=True) + jnp.sum(
            grad_carried * carried, axis=0, keepdims=True
        )
        grad_running = grad_query * q - grad_key * k - grad_carried * carried
        grad_running = grad_running + jnp.where(last_row, grad_last, 0.0)
        grad_keys = grad_key * shrunk + grad_carried * rest
        grad_forget = mul(upper, grad_running, 1, 0) / forget
        inner = grad_forget - grad_keys
        grad_gap = grad_gap - jnp.sum(open_share * inner, axis=0, keepdims=True)
        sigmoid0 = jax.nn.sigmoid(c0)
        new = (
            grad_query * grown * (sigmoid0 * (1.0 + c0 * (1.0 - sigmoid0))),
            gap[...] * s1 * open_share * inner,
            grad_values,
        )
        back = back * jnp.exp(last) + mul(g, q, 0, 0)
        for j in range(3):
            cols = slice(j * HEAD_DIM, (j + 1) * HEAD_DIM)
            grads[PAD + at : PAD + at + CHUNK, cols] = new[j]
            for d in range(4):
                sums[4 * j + d] = sums[4 * j + d] + jnp.sum(
                    new[j] * rows[16 + at - d : 16 + at - d + CHUNK, cols], axis=0, keepdims=True
                )
            total = taps[4 * j : 4 * j + 1, :] * new[j]
            for d in range(1, 4):
                total = total + taps[4 * j + d : 4 * j + d + 1, :] * grads[PAD + at + d : PAD + at + d + CHUNK, cols]
            grad_out[here, cols] = total.astype(BF16)
            if c == count - 1:
                tail_out[:, cols] = total[CHUNK - 16 :]
    for j in range(3):
        cols = slice(j * HEAD_DIM, (j + 1) * HEAD_DIM)
        total = taps[4 * j + 1 : 4 * j + 2, :] * grads[1 : 1 + PAD, cols]
        for d in range(2, 4):
            total = total + taps[4 * j + d : 4 * j + d + 1, :] * grads[d : d + PAD, cols]
        edge_out[:, cols] = total
    for i in range(12):
        small_out[i : i + 1, :] = sums[i]
    small_out[12:13, :] = grad_gap
    small_out[13:16, :] = jnp.zeros((3, HEAD_DIM), F32)


def blocks_of(ids, count):
    member, core = ids[0], ids[1]
    for k in range(2):
        for b in range(count):
            yield k, b, (member ^ b) * 2 + (core ^ k)


def rows_of(blocks, first, count=STEP, cols=slice(None)):
    if isinstance(blocks, (tuple, list)):
        return jnp.concatenate([blocks[first + i][:, cols] for i in range(count)], axis=0)
    part = blocks[first : first + count, :, cols]
    return part.reshape(-1, part.shape[-1])


def fill_columns(weights, source, first, target, rows):
    groups, members, _, depth = source.shape
    per = max(1, 128 // depth)
    for at in range(0, groups * members, per):
        parts = [source[(at + i) // members, (at + i) % members, first : first + rows, :] for i in range(per)]
        part = parts[0] if per == 1 else jnp.concatenate(parts, axis=1)
        weights[target : target + rows, at * depth : (at + per) * depth] = part


def mix_blocks_kernel(mix, out_weight, out):
    heads, depth, _ = out.shape
    for m in range(heads):
        cols = slice(m * HEAD_DIM, (m + 1) * HEAD_DIM)
        for j in range(4):
            out[m, :, j * HEAD_DIM : (j + 1) * HEAD_DIM] = mix[j, :, cols]
        out[m, :, 4 * HEAD_DIM :] = out_weight[cols, :].astype(F32).T.astype(BF16)


def feed_blocks_kernel(up, down, out, turned):
    _, _, units = up.shape
    heads = out.shape[0]
    rows = units // heads
    for j in range(2):
        for t in range(units // 128):
            block = up[j, :, t * 128 : (t + 1) * 128].astype(F32)
            turned[t * 128 : (t + 1) * 128, :] = block.T.astype(BF16)
        for m in range(heads):
            out[m, j * rows : (j + 1) * rows, :] = turned[m * rows : (m + 1) * rows, :]
    for m in range(heads):
        out[m, 2 * rows :, :] = down[m * rows : (m + 1) * rows, :]


def project_kernel(ids, *refs, members):
    own, other = refs[:members], refs[members : 2 * members]
    weights, out, tail = refs[2 * members :]
    half = own[0].shape[0]
    blocks = list(blocks_of(ids, members))
    for at in range(0, len(blocks), STEP):
        k, b, _ = blocks[at]
        result = mul(rows_of((own, other)[k], b), weights[:, : 4 * HEAD_DIM], 1, 0, None).astype(BF16)
        for i in range(STEP):
            to = pl.multiple_of(blocks[at + i][2] * half, half)
            out[pl.ds(to, half), :] = result[i * half : (i + 1) * half]
    tail[...] = out[out.shape[0] - 16 :, : tail.shape[1]]


def feed_kernel(*refs, members):
    own, other, cot_own, cot_other = (refs[i * members : (i + 1) * members] for i in range(4))
    feed, turned, inner_out, mine, away, weights = refs[4 * members :]
    half, width = own[0].shape
    units = feed.shape[2] // 3
    wide = turned.shape[0] // 3
    for j in range(3):
        weights[j * wide + units : (j + 1) * wide, :] = jnp.zeros((wide - units, width), BF16)
        fill_columns(weights, feed, j * units, j * wide, units)
    for k in range(2):
        for b in range(0, members, STEP):
            x = rows_of((own, other)[k], b)
            c = rows_of((cot_own, cot_other)[k], b)
            lifted = mul(x, weights[: 2 * wide], 1, 1, None)
            gate, up_in = lifted[:, :wide], lifted[:, wide:]
            grad = mul(c, weights[2 * wide :], 1, 1, None)
            s = jax.nn.sigmoid(gate)
            act = gate * s
            inner = act * up_in
            grad_gate = grad * up_in * (s * (1.0 + gate * (1.0 - s)))
            grad_up = grad * act
            at = (k * members + b) * half
            cols = slice(at, at + STEP * half)
            turned[0:wide, cols] = grad_gate.T.astype(BF16)
            turned[wide : 2 * wide, cols] = grad_up.T.astype(BF16)
            turned[2 * wide :, cols] = inner.T.astype(BF16)
            inner_out[cols, :] = inner.astype(BF16)
            lift = jnp.concatenate([grad_gate.astype(BF16), grad_up.astype(BF16)], axis=1)
            (mine, away)[k][b : b + STEP] = (
                mul(lift, weights[: 2 * wide], 1, 0, None).astype(BF16).reshape(STEP, half, width)
            )


def block_kernel(inner, feed, mine, away, weights):
    members, half, width = mine.shape
    units, wide = feed.shape[2] // 3, inner.shape[1]
    weights[units:, :] = jnp.zeros((wide - units, width), BF16)
    fill_columns(weights, feed, 2 * units, 0, units)
    for k in range(2):
        for b in range(0, members, STEP):
            at = (k * members + b) * half
            result = mul(inner[at : at + STEP * half, :], weights[...], 1, 0, None)
            (mine, away)[k][b : b + STEP] = result.astype(BF16).reshape(STEP, half, width)


def product_into(ids, out, first, turned, spans, own, other, members, got=None):
    rows = turned.shape[1] // 2
    shards, _, depth = out.shape
    low, high = spans[0][0], spans[-1][1]
    for at in range(0, shards * depth, 256):
        cols = pl.ds(pl.multiple_of(ids[2] * (shards * depth) + at, 128), 256)
        result = mul(turned[low:high, :rows], rows_of(own, 0, members, cols), 1, 0, None)
        result += mul(turned[low:high, rows:], rows_of(other, 0, members, cols), 1, 0, None)
        to = first
        for start, stop in spans:
            here = slice(to, to + stop - start)
            for i in range(256 // depth):
                part = result[start - low : stop - low, i * depth : (i + 1) * depth]
                if got is not None:
                    part = part + got[ids[3], at // depth + i, here, :].astype(F32)
                out[at // depth + i, here, :] = part.astype(BF16)
            to += stop - start


def feed_grad_kernel(ids, *refs, members):
    own, other, cot_own, cot_other = (refs[i * members : (i + 1) * members] for i in range(4))
    turned, *got, out = refs[4 * members :]
    got = got[0] if got else None
    units, wide = out.shape[1] // 3, turned.shape[0] // 3
    product_into(ids, out, 0, turned, [(0, units), (wide, wide + units)], own, other, members, got)
    product_into(ids, out, 2 * units, turned, [(2 * wide, 2 * wide + units)], cot_own, cot_other, members, got)


def mix_grad_kernel(ids, *refs, members):
    own, other, branch_own, branch_other = (refs[i * members : (i + 1) * members] for i in range(4))
    turned, turned_gated, sums, *got, out = refs[4 * members :]
    got = got[0] if got else None
    for m in range(out.shape[0]):
        total = sums[...]
        if got is not None:
            total = total + got[ids[3], m, 5 * HEAD_DIM :, :].astype(F32)
        out[m, 5 * HEAD_DIM :, :] = total.astype(BF16)
    product_into(ids, out, 0, turned, [(0, 4 * HEAD_DIM)], own, other, members, got)
    product_into(ids, out, 4 * HEAD_DIM, turned_gated, [(0, HEAD_DIM)], branch_own, branch_other, members, got)


def project_back_kernel(ids, *refs, members):
    own, other = refs[:members], refs[members : 2 * members]
    grad3, tail, later, grad_gate, weights, norm_gain, turned, mine_out, away_out, norm_out, grads = refs[2 * members :]
    length = grad3.shape[0]
    members, half, width = mine_out.shape
    three = grad3.shape[1]
    grads[:, :three] = grad3[...]
    end = tail.shape[0]
    edge = jnp.concatenate([jnp.zeros((end - later.shape[0], three), F32), later[...]], axis=0)
    grads[length - end :, :three] = (tail[...] + edge).astype(BF16)
    grads[:, three:] = grad_gate[...]
    grad_norm = jnp.zeros((1, width), F32)
    parts = []
    for k, b, block in blocks_of(ids, members):
        parts.append(grads[pl.ds(pl.multiple_of(block * half, half), half), :])
        if len(parts) == STEP:
            x = jnp.concatenate(parts, axis=0)
            at = (k * members + b + 1 - STEP) * half
            turned[:, at : at + STEP * half] = x.astype(F32).T.astype(BF16)
            result = mul(x, weights[:, : 4 * HEAD_DIM], 1, 1, None)
            normed = rows_of((own, other)[k], b + 1 - STEP).astype(F32)
            grad_norm = grad_norm + jnp.sum(result * normed, axis=0, keepdims=True)
            for i in range(STEP):
                to = ids[0] ^ (b + 1 - STEP + i)
                (mine_out, away_out)[k][to] = result[i * half : (i + 1) * half].astype(BF16)
            parts = []
    norm_out[...] = jnp.broadcast_to(grad_norm / norm_gain[...], norm_out.shape)


def mix_total_kernel(got, mix_out, out_out):
    groups, heads, _, depth = got.shape

    def total(i, rows):
        result = got[0, i, rows, :].astype(F32)
        for g in range(1, groups):
            result = result + got[g, i, rows, :].astype(F32)
        return result

    for i in range(heads):
        cols = slice(i * HEAD_DIM, (i + 1) * HEAD_DIM)
        for j in range(4):
            mix_out[j, :, cols] = total(i, slice(j * HEAD_DIM, (j + 1) * HEAD_DIM)).T
        out_out[cols, :] = total(i, slice(4 * HEAD_DIM, 5 * HEAD_DIM))


def feed_total_kernel(got, up_out, down_out, rows):
    heads, three, depth = got.shape
    units = three // 3
    for j in range(2):
        for i in range(heads):
            rows[i * units : (i + 1) * units, :] = got[i, j * units : (j + 1) * units, :].astype(F32)
        for t in range(heads * units // 128):
            up_out[j, :, t * 128 : (t + 1) * 128] = rows[t * 128 : (t + 1) * 128, :].T
    for i in range(heads):
        down_out[i * units : (i + 1) * units, :] = got[i, 2 * units :, :].astype(F32)


def call(kernel, outs, args, scratch=(), ids=None, behind=(), us=5, mib=20):
    specs = [pl.BlockSpec(memory_space=pltpu.VMEM)] * len(args)
    if ids is not None:
        specs = [pl.BlockSpec(memory_space=pltpu.SMEM)] + specs
        args = (ids,) + tuple(args)
    real = len(args)

    def body(*refs):
        kernel(*refs[:real], *refs[real + len(behind) :])

    return pl.pallas_call(
        body,
        out_shape=[jax.ShapeDtypeStruct(s, d) for s, d in outs],
        in_specs=specs + [pl.BlockSpec(memory_space=pl.ANY)] * len(behind),
        out_specs=[pl.BlockSpec(memory_space=pltpu.VMEM)] * len(outs),
        scratch_shapes=list(scratch),
        compiler_params=pltpu.CompilerParams(vmem_limit_bytes=mib * MIB),
        cost_estimate=pl.CostEstimate(flops=0, bytes_accessed=us * 3000000, transcendentals=0),
    )(*args, *behind)


class Group:
    def __init__(self, heads):
        self.size = heads
        self.peers = lax.axis_size("seq")
        self.count = self.peers // heads
        self.member = lax.rem(lax.axis_index("seq"), heads)
        self.index = lax.div(lax.axis_index("seq"), heads)
        self.core = lax.axis_index("head")
        self.ids = jnp.stack([self.member, self.core]).astype(jnp.int32)
        self.lists = [list(range(g * heads, (g + 1) * heads)) for g in range(self.count)]
        self.columns = [list(range(m, self.peers, heads)) for m in range(heads)]

    def swap(self, value, bits):
        return lax.ppermute(value, "seq", [(s, s ^ bits) for s in range(self.peers)])

    def other_core(self, value):
        return lax.ppermute(value, "head", [(0, 1), (1, 0)])

    def shift(self, value, groups):
        step = groups * self.size
        pairs = [(s, s + step) for s in range(self.peers) if 0 <= s + step < self.peers]
        return lax.ppermute(value, "seq", pairs)

    def carry(self, state, decay, sign):
        total = None
        for k in reversed(range(1, self.count)):
            new = self.shift(state, sign * k)
            total = new if total is None else new + total * self.shift(decay, sign * k)
        return jnp.zeros_like(state) if total is None else total

    def gather(self, half):
        got = {0: half}
        for bits in (4, 1, 2):
            got[bits] = self.swap(half, bits)
        got[6] = self.swap(got[4], 2)
        got[5] = self.swap(got[4], 1)
        got[3] = self.swap(got[2], 1)
        got[7] = self.swap(got[5], 2)
        own = [got[bits] for bits in range(self.size)]
        return own, [self.other_core(block) for block in own]

    def scatter(self, mine, away, meanwhile=None):
        other = self.other_core(away)
        part = [mine[b].astype(F32) + other[b].astype(F32) for b in range(self.size)]

        def add(to, source, bits):
            part[to] = part[to] + self.swap(part[source].astype(BF16), bits).astype(F32)

        add(5, 7, 2)
        add(2, 3, 1)
        add(4, 6, 2)
        add(0, 1, 1)
        if meanwhile is not None:
            part[5] = after(part[5], meanwhile)
        add(4, 5, 1)
        add(0, 2, 2)
        add(0, 4, 4)
        return part[0]

    def spread(self, blocks):
        return lax.all_to_all(blocks, "seq", 0, 0, axis_index_groups=self.lists, tiled=True)

    def all_groups(self, value):
        return lax.all_gather(value, "seq", axis_index_groups=self.columns)

    def away(self, kernel, rows, depth, args, us):
        count = 1 if self.count == 2 else self.count
        ids = jnp.stack([self.member, self.core, (1 - self.index) * (count == 1), 0 * self.core]).astype(jnp.int32)
        (out,) = call(kernel, [((count * self.size, rows, depth), BF16)], args, (), ids, us=us, mib=28)
        if count == 1:
            return self.all_groups(out)
        out = out.reshape(count, self.size, rows, depth)
        return lax.psum_scatter(out, "seq", axis_index_groups=self.columns)

    def over_groups(self, kernel, args, got, behind, us):
        if self.count != 2:
            return got
        ids = jnp.stack([self.member, self.core, self.index, 1 - self.index]).astype(jnp.int32)
        return call(kernel, [(got.shape[1:], BF16)], (*args, got), (), ids, behind, us, 28)[0]


def inverse_of(rows):
    return lax.rsqrt(jnp.mean(rows * rows, axis=-1, keepdims=True) + EPS_TOKEN)


def norm_back(rows, inverse, gain, grad):
    scaled = grad * gain
    dot_term = jnp.mean(scaled * rows, axis=-1, keepdims=True)
    grad_rows = inverse * scaled - rows * (inverse * inverse * inverse) * dot_term
    return grad_rows, jnp.sum(grad * rows * inverse, axis=0)


def together(steps, *args):
    shapes = jax.eval_shape(steps, *args)
    always = lax.axis_index("seq") < 2 * lax.axis_size("seq")

    def never(*_):
        return jax.tree.map(lambda leaf: jnp.zeros(leaf.shape, leaf.dtype), shapes)

    return lax.cond(always, steps, never, *args)


def after(value, *earlier):
    return lax.optimization_barrier((value,) + earlier)[0]


def shards(
    tokens,
    norm1_gain,
    mix_weight,
    conv_weight,
    decay_gap,
    group_gain,
    out_weight,
    norm2_gain,
    up_pair,
    down_weight,
    cotangent,
):
    depth = mix_weight.shape[1]
    heads = mix_weight.shape[2] // HEAD_DIM
    units = down_weight.shape[0] // heads
    wide = -(-units // 128) * 128
    local, width = tokens.shape
    half = local // 2
    group = Group(heads)
    ids, member, core = group.ids, group.member, group.core
    length = heads * local
    count = length // CHUNK
    groups, peers = group.count, group.peers

    def my_half(rows):
        return lax.dynamic_slice_in_dim(rows, core * half, half, 0)

    def own_head(array):
        return lax.dynamic_slice_in_dim(array, member * HEAD_DIM, HEAD_DIM, array.ndim - 1)

    taps = own_head(conv_weight).reshape(12, HEAD_DIM)
    gap = own_head(decay_gap).reshape(1, HEAD_DIM)
    gain = own_head(group_gain).reshape(1, HEAD_DIM)

    everything = jnp.stack([member, core, 0 * core, 0 * core]).astype(jnp.int32)
    square = ((HEAD_DIM, HEAD_DIM), F32)
    all_rows = ((heads, half, width), BF16)

    def many(n, dtype=F32):
        return ((length, n * HEAD_DIM), dtype)

    token_rows = tokens.astype(F32)
    inverse1 = inverse_of(token_rows)
    half_tokens = my_half(token_rows)
    half_inverse1 = my_half(inverse1)
    cot_half = my_half(cotangent)
    (mix_blocks,) = call(
        mix_blocks_kernel, [((heads, depth, 5 * HEAD_DIM), BF16)], (mix_weight, out_weight), us=2
    )
    mix_all = group.all_groups(mix_blocks)

    def start_steps(rows, blocks, up, down):
        own, other = group.gather(rows)
        (feed_blocks,) = call(
            feed_blocks_kernel,
            [((heads, 3 * units, depth), BF16)],
            (up, down),
            [pltpu.VMEM((heads * units, depth), BF16)],
            us=3,
        )
        here = group.spread(after(blocks, *other))
        feed = group.spread(after(feed_blocks, here))
        return own, other, feed, here

    normed1, normed1_other, feed_here, mix_here = together(
        start_steps,
        after((half_tokens * half_inverse1 * norm1_gain).astype(BF16), mix_blocks),
        mix_blocks,
        up_pair,
        down_weight,
    )
    feed_own = group.all_groups(feed_here)

    def forward_steps(mix_all, mix_here, normed1, normed1_other):
        if groups == 2:
            far = group.spread(lax.dynamic_index_in_dim(mix_all, 1 - group.index, 0, False))
            mix_own = jnp.where(group.index == 0, jnp.stack([mix_here, far]), jnp.stack([far, mix_here]))
        else:
            mix_own = jnp.moveaxis(group.spread(jnp.moveaxis(mix_all, 0, 1)), 0, 1)
        mix_own = mix_own.reshape(width, 5 * HEAD_DIM)
        projected, tail = call(
            functools.partial(project_kernel, members=heads),
            [((length, 4 * HEAD_DIM), BF16), ((16, 3 * HEAD_DIM), BF16)],
            (*normed1, *normed1_other, mix_own),
            (),
            ids,
        )
        halo = group.shift(tail, 1)
        conv, query, key, totals, states, mixed_here, last = call(
            forward_kernel,
            [
                many(3),
                many(1),
                many(1),
                ((count, HEAD_DIM), F32),
                ((count, HEAD_DIM, HEAD_DIM), F32),
                many(1),
                ((HEAD_DIM + PAD, HEAD_DIM), F32),
            ],
            (projected, halo, taps, gap),
            [pltpu.VMEM((length + 16, 3 * HEAD_DIM), F32)],
        )
        cot, cot_other = group.gather(after(cot_half, halo))
        own_decay = last[HEAD_DIM : HEAD_DIM + 1]
        carry = group.carry(last[:HEAD_DIM], own_decay, 1)
        mixed, states, turned_gated, mine, away = call(
            gate_kernel,
            [many(1), ((count, HEAD_DIM, HEAD_DIM), F32), ((HEAD_DIM, length), BF16), all_rows, all_rows],
            (mixed_here, query, totals, states, carry, projected, gain, mix_own),
            [pltpu.VMEM((length, HEAD_DIM), BF16)],
            ids,
            tuple(cot),
        )
        hidden = half_tokens + group.scatter(mine, away)
        inverse2 = inverse_of(hidden)
        normed2, normed2_other = group.gather((hidden * inverse2 * norm2_gain).astype(BF16))
        decays = jnp.exp(jnp.concatenate([totals[1:] - totals[:-1], jnp.log(own_decay) - totals[-1:]], axis=0))
        kept = (mix_own, projected, halo, conv, query, key, states, mixed, own_decay, decays)
        return kept, (normed2, normed2_other, cot, cot_other), (turned_gated, hidden, inverse2)

    kept, feed_rows, (turned_gated, hidden, inverse2) = together(
        forward_steps, mix_all, mix_here, normed1, normed1_other
    )
    feed_rows = tuple(block for blocks in feed_rows for block in blocks)
    turned, inner, mine, away = call(
        functools.partial(feed_kernel, members=heads),
        [((3 * wide, length), BF16), ((length, wide), BF16), all_rows, all_rows],
        (*feed_rows, feed_own),
        [pltpu.VMEM((3 * wide, width), BF16)],
        us=17,
        mib=38,
    )
    feed_grad = functools.partial(feed_grad_kernel, members=heads)
    feed_args = (*feed_rows, turned)
    feed_away = group.away(feed_grad, 3 * units, depth, feed_args, 5)

    def backward_steps(mine, away, kept, hidden, inverse2, normed1, normed1_other, turned_gated):
        mix_own, projected, halo, conv, query, key, states, mixed, own_decay, decays = kept
        grad_normed2 = group.scatter(mine, away)
        grad_hidden_norm, grad_norm2 = norm_back(hidden, inverse2, norm2_gain, grad_normed2)
        grad_hidden = cot_half.astype(F32) + grad_hidden_norm
        branch, branch_other = group.gather(grad_hidden.astype(BF16))
        grad_mixed, grad_gate_rows, grad_group, start_grad = call(
            functools.partial(gate_back_kernel, members=heads),
            [many(1), many(1, BF16), ((PAD, HEAD_DIM), F32), square],
            (*branch, *branch_other, mix_own, mixed, projected, gain, query, decays),
            [pltpu.VMEM((length, HEAD_DIM), F32)],
            ids,
        )
        back_carry = group.carry(start_grad, own_decay, -1)
        grad_rows3, grad_tail, edge, small = call(
            backward_kernel,
            [many(3, BF16), ((16, 3 * HEAD_DIM), F32), ((PAD, 3 * HEAD_DIM), F32), ((16, HEAD_DIM), F32)],
            (grad_mixed, conv, query, key, states, back_carry, halo, projected, taps, gap),
            [
                pltpu.VMEM((length + 16, 3 * HEAD_DIM), F32),
                pltpu.VMEM((length + 2 * PAD, 3 * HEAD_DIM), F32),
            ],
            us=8,
        )
        later = group.shift(edge, -1)
        turned_mix, mine, away, grad_norm1 = call(
            functools.partial(project_back_kernel, members=heads),
            [((4 * HEAD_DIM, length), BF16), all_rows, all_rows, ((PAD, width), F32)],
            (
                *normed1,
                *normed1_other,
                grad_rows3,
                grad_tail,
                later,
                grad_gate_rows,
                mix_own,
                norm1_gain.reshape(1, width),
            ),
            [pltpu.VMEM((length, 4 * HEAD_DIM), BF16)],
            ids,
            us=7,
            mib=28,
        )
        sums = jnp.concatenate([small[:13].reshape(-1), grad_group[0], grad_norm1[0], grad_norm2]).astype(BF16)
        sums = jnp.pad(sums, (0, extra * depth - sums.shape[0])).reshape(extra, depth)
        (grad_mix,) = call(
            functools.partial(mix_grad_kernel, members=heads),
            [((peers, 5 * HEAD_DIM + extra, depth), BF16)],
            (*normed1, *normed1_other, *branch, *branch_other, turned_mix, turned_gated, sums),
            (),
            everything,
            us=7,
            mib=28,
        )
        both = (mine.astype(F32) + group.other_core(away).astype(F32)).astype(BF16)
        return grad_hidden, grad_mix, both

    extra = -(-(14 * HEAD_DIM + 2 * width) // (16 * depth)) * 16
    grad_hidden, grad_mix, both = together(
        backward_steps, mine, away, kept, hidden, inverse2, normed1, normed1_other, turned_gated
    )
    grad_normed1 = lax.psum_scatter(both, "seq", axis_index_groups=group.lists).astype(F32)
    mix_got = lax.all_to_all(after(grad_mix, feed_away), "seq", 0, 0, tiled=True)
    (block_mine, block_away) = call(
        block_kernel, [all_rows, all_rows], (inner, feed_own), [pltpu.VMEM((wide, width), BF16)], None, (grad_mix,)
    )
    block_half = hidden + group.scatter(block_mine, block_away)
    feed_total = group.over_groups(feed_grad, feed_args, feed_away, (grad_mix,), 8)
    feed_got = group.spread(after(feed_total, mix_got))
    mix_total, out_total = call(
        mix_total_kernel,
        [((4, depth, heads * HEAD_DIM), F32), ((heads * HEAD_DIM, depth), F32)],
        (mix_got.reshape(groups, heads, 5 * HEAD_DIM + extra, depth),),
        us=4,
    )
    grad_rows1 = norm_back(half_tokens, half_inverse1, norm1_gain, grad_normed1)[0]
    grad_tokens = grad_hidden + grad_rows1
    up_total, down_total = call(
        feed_total_kernel,
        [((2, depth, heads * units), F32), ((heads * units, depth), F32)],
        (feed_got,),
        [pltpu.VMEM((heads * units, depth), F32)],
    )
    def both_halves(rows):
        other = group.other_core(rows)
        return jnp.where(core == 0, jnp.concatenate([rows, other], 0), jnp.concatenate([other, rows], 0))

    block_out = both_halves(block_half)
    grad_tokens = both_halves(grad_tokens)
    inverse2 = both_halves(inverse2)

    sums = mix_got[:, 5 * HEAD_DIM :].reshape(groups, heads, -1).astype(F32).sum(0)
    own_sums = sums[:, : 14 * HEAD_DIM].reshape(heads, 14, HEAD_DIM).transpose(1, 0, 2).reshape(14, heads * HEAD_DIM)
    norms = sums[:, 14 * HEAD_DIM : 14 * HEAD_DIM + 2 * width].sum(0).reshape(2, width)
    norms = norms + group.other_core(norms)
    inverse_rms = jnp.stack([inverse1[:, 0], inverse2[:, 0]])
    return (
        block_out,
        grad_tokens,
        norms[0],
        mix_total,
        own_sums[:12].reshape(3, 4, heads * HEAD_DIM),
        own_sums[12],
        own_sums[13],
        out_total,
        norms[1],
        up_total,
        down_total,
        inverse_rms,
    )


def solution(mesh):
    in_specs = (
        P("seq", None),
        P(),
        P(None, "seq", "head"),
        P(None, None, "head"),
        P("head"),
        P("head"),
        P("head", "seq"),
        P(),
        P(None, "seq", "head"),
        P("head", "seq"),
        P("seq", None),
    )
    out_specs = (
        P("seq", None),
        P("seq", None),
        P(),
        P(None, "seq", "head"),
        P(None, None, "head"),
        P("head"),
        P("head"),
        P("head", "seq"),
        P(),
        P(None, "seq", "head"),
        P("head", "seq"),
        P(None, "seq"),
    )
    return jax.shard_map(shards, mesh=mesh, in_specs=in_specs, out_specs=out_specs, check_vma=False)
```

```python
import functools

import jax
import jax.numpy as jnp
from jax import lax
from jax.experimental import pallas as pl
from jax.experimental.pallas import tpu as pltpu
from jax.sharding import PartitionSpec as P

HEAD_DIM = 128
CHUNK = 128
PAD = 8
STEP = 4
EPS_TOKEN = 1e-06
EPS_GROUP = 1e-05
HIGH = lax.Precision.HIGHEST
F32 = jnp.float32
BF16 = jnp.bfloat16
MIB = 1024 * 1024


def mul(a, b, ca, cb, precision=HIGH):
    return lax.dot_general(
        a, b, (((ca,), (cb,)), ((), ())), precision=precision, preferred_element_type=F32
    )


def dsilu(v):
    s = jax.nn.sigmoid(v)
    return s * (1.0 + v * (1.0 - s))


def triangle(lower):
    row = lax.broadcasted_iota(jnp.int32, (CHUNK, CHUNK), 0)
    col = lax.broadcasted_iota(jnp.int32, (CHUNK, CHUNK), 1)
    return (row >= col) if lower else (row <= col)


def forward_kernel(
    proj, halo, taps, gap, conv_out, query_out, key_out, total_out, state_out, local_out, last_out, rows
):
    length = proj.shape[0]
    rows[0:16, :] = halo[...].astype(F32)
    rows[16:, :] = proj[:, : 3 * HEAD_DIM].astype(F32)
    lower = triangle(True)
    ones = lower.astype(F32)
    state = jnp.zeros((HEAD_DIM, HEAD_DIM), F32)
    before = jnp.zeros((1, HEAD_DIM), F32)
    for c in range(length // CHUNK):
        at = c * CHUNK
        here = slice(at, at + CHUNK)
        conv = []
        for j in range(3):
            cols = slice(j * HEAD_DIM, (j + 1) * HEAD_DIM)
            total = taps[4 * j : 4 * j + 1, :] * rows[16 + at : 16 + at + CHUNK, cols]
            for d in range(1, 4):
                total = total + taps[4 * j + d : 4 * j + d + 1, :] * rows[16 + at - d : 16 + at - d + CHUNK, cols]
            conv.append(total)
            conv_out[here, cols] = total
        queries = conv[0] * jax.nn.sigmoid(conv[0])
        open_share = 1.0 - jax.nn.sigmoid(conv[1])
        keys = gap[...] * open_share
        log_forget = jnp.log(1.0 - keys)
        values = conv[2]
        running = mul(ones, log_forget, 1, 0)
        last = running[CHUNK - 1 : CHUNK, :]
        query = queries * jnp.exp(running)
        key = keys * jnp.exp(-running)
        carried = keys * jnp.exp(last - running)
        query_out[here, :] = query
        key_out[here, :] = key
        total_out[c : c + 1, :] = before
        state_out[c] = state
        scores = jnp.where(lower, mul(query, key, 1, 1), 0.0)
        local_out[here, :] = mul(scores, values, 1, 0) + mul(query, state, 1, 1)
        state = state * jnp.exp(last) + mul(values, carried, 0, 0)
        before = before + last
    last_out[0:HEAD_DIM, :] = state
    last_out[HEAD_DIM:, :] = jnp.broadcast_to(jnp.exp(before), (PAD, HEAD_DIM))


def gate_kernel(
    ids, local, query, total, state, carry, gate, gain, weights, mixed_out, state_out, turned_out, mine, away, gated
):
    length = local.shape[0]
    members, half, _ = mine.shape
    start = carry[...]
    for c in range(length // CHUNK):
        here = slice(c * CHUNK, (c + 1) * CHUNK)
        grown = start * jnp.exp(total[c : c + 1, :])
        state_out[c] = state[c] + grown
        mixed = local[here, :] + mul(query[here, :], grown, 1, 1)
        mixed_out[here, :] = mixed
        inverse = lax.rsqrt(jnp.mean(mixed * mixed, axis=-1, keepdims=True) + EPS_GROUP)
        g = gate[here, 3 * HEAD_DIM :].astype(F32)
        gated[here, :] = (mixed * inverse * gain[...] * (g * jax.nn.sigmoid(g))).astype(BF16)
    parts = []
    for k, b, block in blocks_of(ids, members):
        parts.append(gated[pl.ds(pl.multiple_of(block * half, half), half), :])
        if len(parts) == STEP:
            x = jnp.concatenate(parts, axis=0)
            at = (k * members + b + 1 - STEP) * half
            turned_out[:, at : at + STEP * half] = x.astype(F32).T.astype(BF16)
            result = mul(x, weights[:, 4 * HEAD_DIM :], 1, 1, None).astype(BF16)
            (mine, away)[k][b + 1 - STEP : b + 1] = result.reshape(STEP, half, -1)
            parts = []


def gate_back_kernel(
    ids, *refs, members
):
    own, other = refs[:members], refs[members : 2 * members]
    weights, mixed, gate, gain, query, decay = refs[2 * members : 2 * members + 6]
    grad_mixed_out, grad_gate_out, grad_gain_out, start_out, grad_gated = refs[2 * members + 6 :]
    half = own[0].shape[0]
    at = 0
    blocks = list(blocks_of(ids, members))
    for at in range(0, len(blocks), STEP):
        k, b, _ = blocks[at]
        result = mul(rows_of((own, other)[k], b), weights[:, 4 * HEAD_DIM :], 1, 0, None)
        for i in range(STEP):
            to = pl.multiple_of(blocks[at + i][2] * half, half)
            grad_gated[pl.ds(to, half), :] = result[i * half : (i + 1) * half]
    length = mixed.shape[0]
    count = length // CHUNK
    grad_gain = jnp.zeros((1, HEAD_DIM), F32)
    state = jnp.zeros((HEAD_DIM, HEAD_DIM), F32)
    for c in reversed(range(count)):
        here = slice(c * CHUNK, (c + 1) * CHUNK)
        grad = grad_gated[here, :]
        mix = mixed[here, :]
        inverse = lax.rsqrt(jnp.mean(mix * mix, axis=-1, keepdims=True) + EPS_GROUP)
        g = gate[here, 3 * HEAD_DIM :].astype(F32)
        s = jax.nn.sigmoid(g)
        unit = mix * inverse
        w = grad * gain[...] * (g * s)
        grad_gain = grad_gain + jnp.sum(grad * unit * (g * s), axis=0, keepdims=True)
        grad_gate_out[here, :] = (grad * unit * gain[...] * (s * (1.0 + g * (1.0 - s)))).astype(BF16)
        grad_mixed = inverse * w - mix * (inverse * inverse * inverse) * jnp.mean(w * mix, axis=-1, keepdims=True)
        grad_mixed_out[here, :] = grad_mixed
        state = state * decay[c : c + 1, :] + mul(grad_mixed, query[here, :], 0, 0)
    start_out[...] = state
    grad_gain_out[...] = jnp.broadcast_to(grad_gain, (PAD, HEAD_DIM))


def backward_kernel(
    grad_mixed,
    conv,
    query,
    key,
    states,
    carry,
    halo,
    proj,
    taps,
    gap,
    grad_out,
    tail_out,
    edge_out,
    small_out,
    rows,
    grads,
):
    length = grad_mixed.shape[0]
    count = length // CHUNK
    rows[0:16, :] = halo[...].astype(F32)
    rows[16:, :] = proj[:, : 3 * HEAD_DIM].astype(F32)
    grads[0:PAD, :] = jnp.zeros((PAD, 3 * HEAD_DIM), F32)
    grads[PAD + length :, :] = jnp.zeros((PAD, 3 * HEAD_DIM), F32)
    lower = triangle(True)
    ones = lower.astype(F32)
    upper = triangle(False).astype(F32)
    last_row = lax.broadcasted_iota(jnp.int32, (CHUNK, HEAD_DIM), 0) == CHUNK - 1
    back = carry[...]
    grad_gap = jnp.zeros((1, HEAD_DIM), F32)
    sums = [jnp.zeros((1, HEAD_DIM), F32) for _ in range(12)]
    for c in reversed(range(count)):
        at = c * CHUNK
        here = slice(at, at + CHUNK)
        c0, c1, values = (conv[here, j * HEAD_DIM : (j + 1) * HEAD_DIM] for j in range(3))
        s1 = jax.nn.sigmoid(c1)
        open_share = 1.0 - s1
        keys = gap[...] * open_share
        forget = 1.0 - keys
        running = mul(ones, jnp.log(forget), 1, 0)
        last = running[CHUNK - 1 : CHUNK, :]
        grown, shrunk, rest = jnp.exp(running), jnp.exp(-running), jnp.exp(last - running)
        q, k, g = query[here, :], key[here, :], grad_mixed[here, :]
        carried = keys * rest
        state = states[c]
        scores = jnp.where(lower, mul(q, k, 1, 1), 0.0)
        grad_scores = jnp.where(lower, mul(g, values, 1, 1), 0.0)
        grad_values = mul(scores, g, 0, 0) + mul(carried, back, 1, 1)
        grad_query = mul(grad_scores, k, 1, 0) + mul(g, state, 1, 0)
        grad_key = mul(grad_scores, q, 0, 0)
        grad_carried = mul(values, back, 1, 0)
        grad_last = jnp.exp(last) * jnp.sum(back * state, axis=0, keepdims=True) + jnp.sum(
            grad_carried * carried, axis=0, keepdims=True
        )
        grad_running = grad_query * q - grad_key * k - grad_carried * carried
        grad_running = grad_running + jnp.where(last_row, grad_last, 0.0)
        grad_keys = grad_key * shrunk + grad_carried * rest
        grad_forget = mul(upper, grad_running, 1, 0) / forget
        inner = grad_forget - grad_keys
        grad_gap = grad_gap - jnp.sum(open_share * inner, axis=0, keepdims=True)
        sigmoid0 = jax.nn.sigmoid(c0)
        new = (
            grad_query * grown * (sigmoid0 * (1.0 + c0 * (1.0 - sigmoid0))),
            gap[...] * s1 * open_share * inner,
            grad_values,
        )
        back = back * jnp.exp(last) + mul(g, q, 0, 0)
        for j in range(3):
            cols = slice(j * HEAD_DIM, (j + 1) * HEAD_DIM)
            grads[PAD + at : PAD + at + CHUNK, cols] = new[j]
            for d in range(4):
                sums[4 * j + d] = sums[4 * j + d] + jnp.sum(
                    new[j] * rows[16 + at - d : 16 + at - d + CHUNK, cols], axis=0, keepdims=True
                )
            total = taps[4 * j : 4 * j + 1, :] * new[j]
            for d in range(1, 4):
                total = total + taps[4 * j + d : 4 * j + d + 1, :] * grads[PAD + at + d : PAD + at + d + CHUNK, cols]
            grad_out[here, cols] = total.astype(BF16)
            if c == count - 1:
                tail_out[:, cols] = total[CHUNK - 16 :]
    for j in range(3):
        cols = slice(j * HEAD_DIM, (j + 1) * HEAD_DIM)
        total = taps[4 * j + 1 : 4 * j + 2, :] * grads[1 : 1 + PAD, cols]
        for d in range(2, 4):
            total = total + taps[4 * j + d : 4 * j + d + 1, :] * grads[d : d + PAD, cols]
        edge_out[:, cols] = total
    for i in range(12):
        small_out[i : i + 1, :] = sums[i]
    small_out[12:13, :] = grad_gap
    small_out[13:16, :] = jnp.zeros((3, HEAD_DIM), F32)


def blocks_of(ids, count):
    member, core = ids[0], ids[1]
    for k in range(2):
        for b in range(count):
            yield k, b, (member ^ b) * 2 + (core ^ k)


def rows_of(blocks, first, count=STEP, cols=slice(None)):
    if isinstance(blocks, (tuple, list)):
        return jnp.concatenate([blocks[first + i][:, cols] for i in range(count)], axis=0)
    part = blocks[first : first + count, :, cols]
    return part.reshape(-1, part.shape[-1])


def fill_columns(weights, source, first, target, rows):
    groups, members, _, depth = source.shape
    per = max(1, 128 // depth)
    for at in range(0, groups * members, per):
        parts = [source[(at + i) // members, (at + i) % members, first : first + rows, :] for i in range(per)]
        part = parts[0] if per == 1 else jnp.concatenate(parts, axis=1)
        weights[target : target + rows, at * depth : (at + per) * depth] = part


def mix_blocks_kernel(mix, out_weight, out):
    groups, heads, depth, _ = out.shape
    for m in range(heads):
        cols = slice(m * HEAD_DIM, (m + 1) * HEAD_DIM)
        turned = out_weight[cols, :].astype(F32).T.astype(BF16)
        for g in range(groups):
            for j in range(4):
                out[g, m, :, j * HEAD_DIM : (j + 1) * HEAD_DIM] = mix[j, :, cols]
            out[g, m, :, 4 * HEAD_DIM :] = turned


def feed_blocks_kernel(up, down, out, turned):
    _, _, units = up.shape
    heads = out.shape[0]
    rows = units // heads
    for j in range(2):
        for t in range(units // 128):
            block = up[j, :, t * 128 : (t + 1) * 128].astype(F32)
            turned[t * 128 : (t + 1) * 128, :] = block.T.astype(BF16)
        for m in range(heads):
            out[m, j * rows : (j + 1) * rows, :] = turned[m * rows : (m + 1) * rows, :]
    for m in range(heads):
        out[m, 2 * rows :, :] = down[m * rows : (m + 1) * rows, :]


def project_kernel(ids, *refs, members):
    own, other = refs[:members], refs[members : 2 * members]
    weights, out, tail = refs[2 * members :]
    half = own[0].shape[0]
    blocks = list(blocks_of(ids, members))
    for at in range(0, len(blocks), STEP):
        k, b, _ = blocks[at]
        result = mul(rows_of((own, other)[k], b), weights[:, : 4 * HEAD_DIM], 1, 0, None).astype(BF16)
        for i in range(STEP):
            to = pl.multiple_of(blocks[at + i][2] * half, half)
            out[pl.ds(to, half), :] = result[i * half : (i + 1) * half]
    tail[...] = out[out.shape[0] - 16 :, : tail.shape[1]]


def feed_kernel(*refs, members):
    own, other, cot_own, cot_other = (refs[i * members : (i + 1) * members] for i in range(4))
    feed, turned, inner_out, mine, away, weights = refs[4 * members :]
    half, width = own[0].shape
    units = feed.shape[2] // 3
    wide = turned.shape[0] // 3
    for j in range(3):
        weights[j * wide + units : (j + 1) * wide, :] = jnp.zeros((wide - units, width), BF16)
        fill_columns(weights, feed, j * units, j * wide, units)
    for k in range(2):
        for b in range(0, members, STEP):
            x = rows_of((own, other)[k], b)
            c = rows_of((cot_own, cot_other)[k], b)
            lifted = mul(x, weights[: 2 * wide], 1, 1, None)
            gate, up_in = lifted[:, :wide], lifted[:, wide:]
            grad = mul(c, weights[2 * wide :], 1, 1, None)
            s = jax.nn.sigmoid(gate)
            act = gate * s
            inner = act * up_in
            grad_gate = grad * up_in * (s * (1.0 + gate * (1.0 - s)))
            grad_up = grad * act
            at = (k * members + b) * half
            cols = slice(at, at + STEP * half)
            turned[0:wide, cols] = grad_gate.T.astype(BF16)
            turned[wide : 2 * wide, cols] = grad_up.T.astype(BF16)
            turned[2 * wide :, cols] = inner.T.astype(BF16)
            inner_out[cols, :] = inner.astype(BF16)
            lift = jnp.concatenate([grad_gate.astype(BF16), grad_up.astype(BF16)], axis=1)
            (mine, away)[k][b : b + STEP] = (
                mul(lift, weights[: 2 * wide], 1, 0, None).astype(BF16).reshape(STEP, half, width)
            )


def block_kernel(inner, feed, mine, away, weights):
    members, half, width = mine.shape
    units, wide = feed.shape[2] // 3, inner.shape[1]
    weights[units:, :] = jnp.zeros((wide - units, width), BF16)
    fill_columns(weights, feed, 2 * units, 0, units)
    for k in range(2):
        for b in range(0, members, STEP):
            at = (k * members + b) * half
            result = mul(inner[at : at + STEP * half, :], weights[...], 1, 0, None)
            (mine, away)[k][b : b + STEP] = result.astype(BF16).reshape(STEP, half, width)


def product_into(ids, out, first, turned, spans, own, other, members, got=None):
    rows = turned.shape[1] // 2
    shards, _, depth = out.shape
    low, high = spans[0][0], spans[-1][1]
    for at in range(0, shards * depth, 256):
        cols = pl.ds(pl.multiple_of(ids[2] * (shards * depth) + at, 128), 256)
        result = mul(turned[low:high, :rows], rows_of(own, 0, members, cols), 1, 0, None)
        result += mul(turned[low:high, rows:], rows_of(other, 0, members, cols), 1, 0, None)
        to = first
        for start, stop in spans:
            here = slice(to, to + stop - start)
            for i in range(256 // depth):
                part = result[start - low : stop - low, i * depth : (i + 1) * depth]
                if got is not None:
                    part = part + got[ids[3], at // depth + i, here, :].astype(F32)
                out[at // depth + i, here, :] = part.astype(BF16)
            to += stop - start


def feed_grad_kernel(ids, *refs, members):
    own, other, cot_own, cot_other = (refs[i * members : (i + 1) * members] for i in range(4))
    turned, *got, out = refs[4 * members :]
    got = got[0] if got else None
    units, wide = out.shape[1] // 3, turned.shape[0] // 3
    product_into(ids, out, 0, turned, [(0, units), (wide, wide + units)], own, other, members, got)
    product_into(ids, out, 2 * units, turned, [(2 * wide, 2 * wide + units)], cot_own, cot_other, members, got)


def mix_grad_kernel(ids, *refs, members):
    own, other, branch_own, branch_other = (refs[i * members : (i + 1) * members] for i in range(4))
    turned, turned_gated, sums, *got, out = refs[4 * members :]
    got = got[0] if got else None
    for m in range(out.shape[0]):
        total = sums[...]
        if got is not None:
            total = total + got[ids[3], m, 5 * HEAD_DIM :, :].astype(F32)
        out[m, 5 * HEAD_DIM :, :] = total.astype(BF16)
    product_into(ids, out, 0, turned, [(0, 4 * HEAD_DIM)], own, other, members, got)
    product_into(ids, out, 4 * HEAD_DIM, turned_gated, [(0, HEAD_DIM)], branch_own, branch_other, members, got)


def project_back_kernel(ids, *refs, members):
    own, other = refs[:members], refs[members : 2 * members]
    grad3, tail, later, grad_gate, weights, norm_gain, turned, mine_out, away_out, norm_out, grads = refs[2 * members :]
    length = grad3.shape[0]
    members, half, width = mine_out.shape
    three = grad3.shape[1]
    grads[:, :three] = grad3[...]
    end = tail.shape[0]
    edge = jnp.concatenate([jnp.zeros((end - later.shape[0], three), F32), later[...]], axis=0)
    grads[length - end :, :three] = (tail[...] + edge).astype(BF16)
    grads[:, three:] = grad_gate[...]
    grad_norm = jnp.zeros((1, width), F32)
    parts = []
    for k, b, block in blocks_of(ids, members):
        parts.append(grads[pl.ds(pl.multiple_of(block * half, half), half), :])
        if len(parts) == STEP:
            x = jnp.concatenate(parts, axis=0)
            at = (k * members + b + 1 - STEP) * half
            turned[:, at : at + STEP * half] = x.astype(F32).T.astype(BF16)
            result = mul(x, weights[:, : 4 * HEAD_DIM], 1, 1, None)
            normed = rows_of((own, other)[k], b + 1 - STEP).astype(F32)
            grad_norm = grad_norm + jnp.sum(result * normed, axis=0, keepdims=True)
            for i in range(STEP):
                to = ids[0] ^ (b + 1 - STEP + i)
                (mine_out, away_out)[k][to] = result[i * half : (i + 1) * half].astype(BF16)
            parts = []
    norm_out[...] = jnp.broadcast_to(grad_norm / norm_gain[...], norm_out.shape)


def mix_total_kernel(got, mix_out, out_out):
    groups, heads, _, depth = got.shape

    def total(i, rows):
        result = got[0, i, rows, :].astype(F32)
        for g in range(1, groups):
            result = result + got[g, i, rows, :].astype(F32)
        return result

    for i in range(heads):
        cols = slice(i * HEAD_DIM, (i + 1) * HEAD_DIM)
        for j in range(4):
            mix_out[j, :, cols] = total(i, slice(j * HEAD_DIM, (j + 1) * HEAD_DIM)).T
        out_out[cols, :] = total(i, slice(4 * HEAD_DIM, 5 * HEAD_DIM))


def feed_total_kernel(got, up_out, down_out, rows):
    heads, three, depth = got.shape
    units = three // 3
    for j in range(2):
        for i in range(heads):
            rows[i * units : (i + 1) * units, :] = got[i, j * units : (j + 1) * units, :].astype(F32)
        for t in range(heads * units // 128):
            up_out[j, :, t * 128 : (t + 1) * 128] = rows[t * 128 : (t + 1) * 128, :].T
    for i in range(heads):
        down_out[i * units : (i + 1) * units, :] = got[i, 2 * units :, :].astype(F32)


def call(kernel, outs, args, scratch=(), ids=None, behind=(), us=5, mib=20):
    specs = [pl.BlockSpec(memory_space=pltpu.VMEM)] * len(args)
    if ids is not None:
        specs = [pl.BlockSpec(memory_space=pltpu.SMEM)] + specs
        args = (ids,) + tuple(args)
    real = len(args)

    def body(*refs):
        kernel(*refs[:real], *refs[real + len(behind) :])

    return pl.pallas_call(
        body,
        out_shape=[jax.ShapeDtypeStruct(s, d) for s, d in outs],
        in_specs=specs + [pl.BlockSpec(memory_space=pl.ANY)] * len(behind),
        out_specs=[pl.BlockSpec(memory_space=pltpu.VMEM)] * len(outs),
        scratch_shapes=list(scratch),
        compiler_params=pltpu.CompilerParams(vmem_limit_bytes=mib * MIB),
        cost_estimate=pl.CostEstimate(flops=0, bytes_accessed=us * 3000000, transcendentals=0),
    )(*args, *behind)


class Group:
    def __init__(self, heads):
        self.size = heads
        self.peers = lax.axis_size("seq")
        self.count = self.peers // heads
        self.member = lax.rem(lax.axis_index("seq"), heads)
        self.index = lax.div(lax.axis_index("seq"), heads)
        self.core = lax.axis_index("head")
        self.ids = jnp.stack([self.member, self.core]).astype(jnp.int32)
        self.lists = [list(range(g * heads, (g + 1) * heads)) for g in range(self.count)]
        self.columns = [list(range(m, self.peers, heads)) for m in range(heads)]

    def swap(self, value, bits):
        return lax.ppermute(value, "seq", [(s, s ^ bits) for s in range(self.peers)])

    def other_core(self, value):
        return lax.ppermute(value, "head", [(0, 1), (1, 0)])

    def shift(self, value, groups):
        step = groups * self.size
        pairs = [(s, s + step) for s in range(self.peers) if 0 <= s + step < self.peers]
        return lax.ppermute(value, "seq", pairs)

    def carry(self, state, decay, sign):
        total = None
        for k in reversed(range(1, self.count)):
            new = self.shift(state, sign * k)
            total = new if total is None else new + total * self.shift(decay, sign * k)
        return jnp.zeros_like(state) if total is None else total

    def gather(self, half):
        got = {0: half}
        for bits in (4, 1, 2):
            got[bits] = self.swap(half, bits)
        got[6] = self.swap(got[4], 2)
        got[5] = self.swap(got[4], 1)
        got[3] = self.swap(got[2], 1)
        got[7] = self.swap(got[5], 2)
        own = [got[bits] for bits in range(self.size)]
        return own, [self.other_core(block) for block in own]

    def over_members(self, part, before_last=()):
        def add(to, source, bits):
            part[to] = part[to] + self.swap(part[source].astype(BF16), bits).astype(F32)

        add(5, 7, 2)
        add(2, 3, 1)
        add(4, 6, 2)
        add(0, 1, 1)
        add(4, 5, 1)
        add(0, 2, 2)
        part[4] = after(part[4], *before_last)
        add(0, 4, 4)
        return part[0]

    def scatter(self, mine, other, before_last=()):
        part = [mine[b].astype(F32) + other[b].astype(F32) for b in range(self.size)]
        return self.over_members(part, before_last)

    def spread(self, blocks):
        return lax.all_to_all(blocks, "seq", 0, 0, axis_index_groups=self.lists, tiled=True)

    def all_groups(self, value):
        return lax.all_gather(value, "seq", axis_index_groups=self.columns)

    def away(self, kernel, rows, depth, args, us):
        count = 1 if self.count == 2 else self.count
        ids = jnp.stack([self.member, self.core, (1 - self.index) * (count == 1), 0 * self.core]).astype(jnp.int32)
        (out,) = call(kernel, [((count * self.size, rows, depth), BF16)], args, (), ids, us=us, mib=28)
        if count == 1:
            return self.all_groups(out)
        out = out.reshape(count, self.size, rows, depth)
        return lax.psum_scatter(out, "seq", axis_index_groups=self.columns)

    def over_groups(self, kernel, args, got, behind, us):
        if self.count != 2:
            return got
        ids = jnp.stack([self.member, self.core, self.index, 1 - self.index]).astype(jnp.int32)
        return call(kernel, [(got.shape[1:], BF16)], (*args, got), (), ids, behind, us, 28)[0]


def inverse_of(rows):
    return lax.rsqrt(jnp.mean(rows * rows, axis=-1, keepdims=True) + EPS_TOKEN)


def norm_back(rows, inverse, gain, grad):
    scaled = grad * gain
    dot_term = jnp.mean(scaled * rows, axis=-1, keepdims=True)
    grad_rows = inverse * scaled - rows * (inverse * inverse * inverse) * dot_term
    return grad_rows, jnp.sum(grad * rows * inverse, axis=0)


def together(steps, *args):
    shapes = jax.eval_shape(steps, *args)
    always = lax.axis_index("seq") < 2 * lax.axis_size("seq")

    def never(*_):
        return jax.tree.map(lambda leaf: jnp.zeros(leaf.shape, leaf.dtype), shapes)

    return lax.cond(always, steps, never, *args)


def after(value, *earlier):
    return lax.optimization_barrier((value,) + earlier)[0]


def shards(
    tokens,
    norm1_gain,
    mix_weight,
    conv_weight,
    decay_gap,
    group_gain,
    out_weight,
    norm2_gain,
    up_pair,
    down_weight,
    cotangent,
):
    depth = mix_weight.shape[1]
    heads = mix_weight.shape[2] // HEAD_DIM
    units = down_weight.shape[0] // heads
    wide = -(-units // 128) * 128
    local, width = tokens.shape
    half = local // 2
    group = Group(heads)
    ids, member, core = group.ids, group.member, group.core
    length = heads * local
    count = length // CHUNK
    groups, peers = group.count, group.peers

    def my_half(rows):
        return lax.dynamic_slice_in_dim(rows, core * half, half, 0)

    def own_head(array):
        return lax.dynamic_slice_in_dim(array, member * HEAD_DIM, HEAD_DIM, array.ndim - 1)

    taps = own_head(conv_weight).reshape(12, HEAD_DIM)
    gap = own_head(decay_gap).reshape(1, HEAD_DIM)
    gain = own_head(group_gain).reshape(1, HEAD_DIM)

    everything = jnp.stack([member, core, 0 * core, 0 * core]).astype(jnp.int32)
    square = ((HEAD_DIM, HEAD_DIM), F32)
    all_rows = ((heads, half, width), BF16)

    def many(n, dtype=F32):
        return ((length, n * HEAD_DIM), dtype)

    token_rows = tokens.astype(F32)
    inverse1 = inverse_of(token_rows)
    half_tokens = my_half(token_rows)
    half_inverse1 = my_half(inverse1)
    cot_half = my_half(cotangent)

    def start_steps(rows, mix_weight, out_weight, up, down):
        own, other = group.gather(rows)
        (mix_blocks,) = call(
            mix_blocks_kernel, [((groups, heads, depth, 5 * HEAD_DIM), BF16)], (mix_weight, out_weight), us=2
        )
        mix_blocks = after(mix_blocks.reshape(peers, depth, 5 * HEAD_DIM), *other)
        mix_own = lax.all_to_all(mix_blocks, "seq", 0, 0, tiled=True).reshape(width, 5 * HEAD_DIM)
        (feed_blocks,) = call(
            feed_blocks_kernel,
            [((heads, 3 * units, depth), BF16)],
            (up, down),
            [pltpu.VMEM((heads * units, depth), BF16)],
            us=3,
        )
        feed = group.spread(after(feed_blocks, mix_own))
        projected, tail = call(
            functools.partial(project_kernel, members=heads),
            [((length, 4 * HEAD_DIM), BF16), ((16, 3 * HEAD_DIM), BF16)],
            (*own, *other, mix_own),
            (),
            ids,
        )
        halo = group.shift(tail, 1)
        conv, query, key, totals, states, mixed_here, last = call(
            forward_kernel,
            [
                many(3),
                many(1),
                many(1),
                ((count, HEAD_DIM), F32),
                ((count, HEAD_DIM, HEAD_DIM), F32),
                many(1),
                ((HEAD_DIM + PAD, HEAD_DIM), F32),
            ],
            (projected, halo, taps, gap),
            [pltpu.VMEM((length + 16, 3 * HEAD_DIM), F32)],
        )
        own_decay = last[HEAD_DIM : HEAD_DIM + 1]
        carry = group.carry(last[:HEAD_DIM], own_decay, 1)
        decays = jnp.exp(jnp.concatenate([totals[1:] - totals[:-1], jnp.log(own_decay) - totals[-1:]], axis=0))
        kept = (mix_own, projected, halo, conv, query, key)
        return own, other, feed, kept, (own_decay, decays), (mixed_here, totals, states, carry)

    normed1, normed1_other, feed_here, kept, decay_rows, here = together(
        start_steps,
        (half_tokens * half_inverse1 * norm1_gain).astype(BF16),
        mix_weight,
        out_weight,
        up_pair,
        down_weight,
    )
    feed_own = group.all_groups(feed_here)

    def both_halves(rows):
        other = group.other_core(rows)
        return jnp.where(core == 0, jnp.concatenate([rows, other], 0), jnp.concatenate([other, rows], 0))

    def forward_steps(kept, here, cot_half):
        mix_own, projected, _, _, query, _ = kept
        mixed_here, totals, states, carry = here
        cot, cot_other = group.gather(cot_half)
        mixed, states, turned_gated, mine, away = call(
            gate_kernel,
            [many(1), ((count, HEAD_DIM, HEAD_DIM), F32), ((HEAD_DIM, length), BF16), all_rows, all_rows],
            (mixed_here, query, totals, states, carry, projected, gain, mix_own),
            [pltpu.VMEM((length, HEAD_DIM), BF16)],
            ids,
        )
        hidden = half_tokens + group.scatter(mine, group.other_core(away))
        inverse2 = inverse_of(hidden)
        normed2, normed2_other = group.gather((hidden * inverse2 * norm2_gain).astype(BF16))
        return (states, mixed), (*normed2, *normed2_other, *cot, *cot_other), (turned_gated, hidden, inverse2, both_halves(inverse2))

    mixed_rows, feed_rows, (turned_gated, hidden, inverse2, inverse2_all) = together(
        forward_steps, kept, here, cot_half
    )
    kept = (*kept, *mixed_rows, *decay_rows)
    turned, inner, mine, away = call(
        functools.partial(feed_kernel, members=heads),
        [((3 * wide, length), BF16), ((length, wide), BF16), all_rows, all_rows],
        (*feed_rows, feed_own),
        [pltpu.VMEM((3 * wide, width), BF16)],
        us=17,
        mib=38,
    )
    feed_grad = functools.partial(feed_grad_kernel, members=heads)
    feed_args = (*feed_rows, turned)
    other = group.other_core(away)
    feed_away = group.away(feed_grad, 3 * units, depth, feed_args, 7)

    def backward_steps(mine, other, kept, hidden, inverse2, normed1, normed1_other, turned_gated):
        mix_own, projected, halo, conv, query, key, states, mixed, own_decay, decays = kept
        grad_normed2 = group.scatter(mine, other)
        grad_hidden_norm, grad_norm2 = norm_back(hidden, inverse2, norm2_gain, grad_normed2)
        grad_hidden = cot_half.astype(F32) + grad_hidden_norm
        branch, branch_other = group.gather(grad_hidden.astype(BF16))
        grad_mixed, grad_gate_rows, grad_group, start_grad = call(
            functools.partial(gate_back_kernel, members=heads),
            [many(1), many(1, BF16), ((PAD, HEAD_DIM), F32), square],
            (*branch, *branch_other, mix_own, mixed, projected, gain, query, decays),
            [pltpu.VMEM((length, HEAD_DIM), F32)],
            ids,
        )
        back_carry = group.carry(start_grad, own_decay, -1)
        grad_rows3, grad_tail, edge, small = call(
            backward_kernel,
            [many(3, BF16), ((16, 3 * HEAD_DIM), F32), ((PAD, 3 * HEAD_DIM), F32), ((16, HEAD_DIM), F32)],
            (grad_mixed, conv, query, key, states, back_carry, halo, projected, taps, gap),
            [
                pltpu.VMEM((length + 16, 3 * HEAD_DIM), F32),
                pltpu.VMEM((length + 2 * PAD, 3 * HEAD_DIM), F32),
            ],
            us=8,
        )
        later = group.shift(edge, -1)
        turned_mix, mine, away, grad_norm1 = call(
            functools.partial(project_back_kernel, members=heads),
            [((4 * HEAD_DIM, length), BF16), all_rows, all_rows, ((PAD, width), F32)],
            (
                *normed1,
                *normed1_other,
                grad_rows3,
                grad_tail,
                later,
                grad_gate_rows,
                mix_own,
                norm1_gain.reshape(1, width),
            ),
            [pltpu.VMEM((length, 4 * HEAD_DIM), BF16)],
            ids,
            us=7,
            mib=28,
        )
        sums = jnp.concatenate([small[:13].reshape(-1), grad_group[0], grad_norm1[0], grad_norm2]).astype(BF16)
        sums = jnp.pad(sums, (0, extra * depth - sums.shape[0])).reshape(extra, depth)
        (grad_mix,) = call(
            functools.partial(mix_grad_kernel, members=heads),
            [((peers, 5 * HEAD_DIM + extra, depth), BF16)],
            (*normed1, *normed1_other, *branch, *branch_other, turned_mix, turned_gated, sums),
            (),
            everything,
            us=7,
            mib=28,
        )
        both = (mine.astype(F32) + group.other_core(away).astype(F32)).astype(BF16)
        return grad_hidden, grad_mix, both

    extra = -(-(14 * HEAD_DIM + 2 * width) // (16 * depth)) * 16
    grad_hidden, grad_mix, both = together(
        backward_steps, mine, other, kept, hidden, inverse2, normed1, normed1_other, turned_gated
    )
    grad_normed1 = lax.psum_scatter(both, "seq", axis_index_groups=group.lists)
    mix_got = lax.all_to_all(after(grad_mix, feed_away), "seq", 0, 0, tiled=True)
    feed_total = group.over_groups(feed_grad, feed_args, feed_away, (grad_mix,), 8)
    (block_mine, block_away) = call(
        block_kernel, [all_rows, all_rows], (inner, feed_own), [pltpu.VMEM((wide, width), BF16)], None, (feed_total,)
    )
    feed_got = group.spread(after(feed_total, mix_got))
    mix_total, out_total = call(
        mix_total_kernel,
        [((4, depth, heads * HEAD_DIM), F32), ((heads * HEAD_DIM, depth), F32)],
        (mix_got.reshape(groups, heads, 5 * HEAD_DIM + extra, depth),),
        us=4,
    )
    sums = mix_got[:, 5 * HEAD_DIM :].reshape(groups, heads, -1).astype(F32).sum(0)
    own_sums = sums[:, : 14 * HEAD_DIM].reshape(heads, 14, HEAD_DIM).transpose(1, 0, 2).reshape(14, heads * HEAD_DIM)
    norms = sums[:, 14 * HEAD_DIM : 14 * HEAD_DIM + 2 * width].sum(0).reshape(2, width)
    norms = norms + group.other_core(norms)
    block_half = hidden + group.scatter(
        block_mine, group.other_core(block_away), (mix_total, out_total, own_sums, norms)
    )
    grad_normed1 = after(grad_normed1, block_half).astype(F32)
    grad_rows1 = norm_back(half_tokens, half_inverse1, norm1_gain, grad_normed1)[0]
    grad_tokens = grad_hidden + grad_rows1
    up_total, down_total = call(
        feed_total_kernel,
        [((2, depth, heads * units), F32), ((heads * units, depth), F32)],
        (feed_got,),
        [pltpu.VMEM((heads * units, depth), F32)],
    )
    block_out = both_halves(block_half)
    grad_tokens = both_halves(grad_tokens)

    inverse_rms = jnp.stack([inverse1[:, 0], inverse2_all[:, 0]])
    return (
        block_out,
        grad_tokens,
        norms[0],
        mix_total,
        own_sums[:12].reshape(3, 4, heads * HEAD_DIM),
        own_sums[12],
        own_sums[13],
        out_total,
        norms[1],
        up_total,
        down_total,
        inverse_rms,
    )


def solution(mesh):
    in_specs = (
        P("seq", None),
        P(),
        P(None, "seq", "head"),
        P(None, None, "head"),
        P("head"),
        P("head"),
        P("head", "seq"),
        P(),
        P(None, "seq", "head"),
        P("head", "seq"),
        P("seq", None),
    )
    out_specs = (
        P("seq", None),
        P("seq", None),
        P(),
        P(None, "seq", "head"),
        P(None, None, "head"),
        P("head"),
        P("head"),
        P("head", "seq"),
        P(),
        P(None, "seq", "head"),
        P("head", "seq"),
        P(None, "seq"),
    )
    return jax.shard_map(shards, mesh=mesh, in_specs=in_specs, out_specs=out_specs, check_vma=False)
```

```python
import functools

import jax
import jax.numpy as jnp
from jax import lax
from jax.experimental import pallas as pl
from jax.experimental.pallas import tpu as pltpu
from jax.sharding import PartitionSpec as P

HEAD_DIM = 128
CHUNK = 128
PAD = 8
STEP = 4
EPS_TOKEN = 1e-06
EPS_GROUP = 1e-05
HIGH = lax.Precision.HIGHEST
F32 = jnp.float32
BF16 = jnp.bfloat16
MIB = 1024 * 1024


def mul(a, b, ca, cb, precision=HIGH):
    return lax.dot_general(
        a, b, (((ca,), (cb,)), ((), ())), precision=precision, preferred_element_type=F32
    )


def dsilu(v):
    s = jax.nn.sigmoid(v)
    return s * (1.0 + v * (1.0 - s))


def triangle(lower):
    row = lax.broadcasted_iota(jnp.int32, (CHUNK, CHUNK), 0)
    col = lax.broadcasted_iota(jnp.int32, (CHUNK, CHUNK), 1)
    return (row >= col) if lower else (row <= col)


def forward_kernel(
    proj, halo, taps, gap, conv_out, query_out, key_out, total_out, state_out, local_out, last_out, rows
):
    length = proj.shape[0]
    rows[0:16, :] = halo[...].astype(F32)
    rows[16:, :] = proj[:, : 3 * HEAD_DIM].astype(F32)
    lower = triangle(True)
    ones = lower.astype(F32)
    state = jnp.zeros((HEAD_DIM, HEAD_DIM), F32)
    before = jnp.zeros((1, HEAD_DIM), F32)
    for c in range(length // CHUNK):
        at = c * CHUNK
        here = slice(at, at + CHUNK)
        conv = []
        for j in range(3):
            cols = slice(j * HEAD_DIM, (j + 1) * HEAD_DIM)
            total = taps[4 * j : 4 * j + 1, :] * rows[16 + at : 16 + at + CHUNK, cols]
            for d in range(1, 4):
                total = total + taps[4 * j + d : 4 * j + d + 1, :] * rows[16 + at - d : 16 + at - d + CHUNK, cols]
            conv.append(total)
            conv_out[here, cols] = total
        queries = conv[0] * jax.nn.sigmoid(conv[0])
        open_share = 1.0 - jax.nn.sigmoid(conv[1])
        keys = gap[...] * open_share
        log_forget = jnp.log(1.0 - keys)
        values = conv[2]
        running = mul(ones, log_forget, 1, 0)
        last = running[CHUNK - 1 : CHUNK, :]
        query = queries * jnp.exp(running)
        key = keys * jnp.exp(-running)
        carried = keys * jnp.exp(last - running)
        query_out[here, :] = query
        key_out[here, :] = key
        total_out[c : c + 1, :] = before
        state_out[c] = state
        scores = jnp.where(lower, mul(query, key, 1, 1), 0.0)
        local_out[here, :] = mul(scores, values, 1, 0) + mul(query, state, 1, 1)
        state = state * jnp.exp(last) + mul(values, carried, 0, 0)
        before = before + last
    last_out[0:HEAD_DIM, :] = state
    last_out[HEAD_DIM:, :] = jnp.broadcast_to(jnp.exp(before), (PAD, HEAD_DIM))


def gate_kernel(
    ids, local, query, total, state, carry, gate, gain, weights, mixed_out, state_out, turned_out, mine, away, gated
):
    length = local.shape[0]
    members, half, _ = mine.shape
    start = carry[...]
    for c in range(length // CHUNK):
        here = slice(c * CHUNK, (c + 1) * CHUNK)
        grown = start * jnp.exp(total[c : c + 1, :])
        state_out[c] = state[c] + grown
        mixed = local[here, :] + mul(query[here, :], grown, 1, 1)
        mixed_out[here, :] = mixed
        inverse = lax.rsqrt(jnp.mean(mixed * mixed, axis=-1, keepdims=True) + EPS_GROUP)
        g = gate[here, 3 * HEAD_DIM :].astype(F32)
        gated[here, :] = (mixed * inverse * gain[...] * (g * jax.nn.sigmoid(g))).astype(BF16)
    parts = []
    for k, b, block in blocks_of(ids, members):
        parts.append(gated[pl.ds(pl.multiple_of(block * half, half), half), :])
        if len(parts) == STEP:
            x = jnp.concatenate(parts, axis=0)
            at = (k * members + b + 1 - STEP) * half
            turned_out[:, at : at + STEP * half] = x.astype(F32).T.astype(BF16)
            result = mul(x, weights[:, 4 * HEAD_DIM :], 1, 1, None).astype(BF16)
            (mine, away)[k][b + 1 - STEP : b + 1] = result.reshape(STEP, half, -1)
            parts = []


def gate_back_kernel(
    ids, *refs, members
):
    own, other = refs[:members], refs[members : 2 * members]
    weights, mixed, gate, gain, query, decay = refs[2 * members : 2 * members + 6]
    grad_mixed_out, grad_gate_out, grad_gain_out, start_out, grad_gated = refs[2 * members + 6 :]
    half = own[0].shape[0]
    at = 0
    blocks = list(blocks_of(ids, members))
    for at in range(0, len(blocks), STEP):
        k, b, _ = blocks[at]
        result = mul(rows_of((own, other)[k], b), weights[:, 4 * HEAD_DIM :], 1, 0, None)
        for i in range(STEP):
            to = pl.multiple_of(blocks[at + i][2] * half, half)
            grad_gated[pl.ds(to, half), :] = result[i * half : (i + 1) * half]
    length = mixed.shape[0]
    count = length // CHUNK
    grad_gain = jnp.zeros((1, HEAD_DIM), F32)
    state = jnp.zeros((HEAD_DIM, HEAD_DIM), F32)
    for c in reversed(range(count)):
        here = slice(c * CHUNK, (c + 1) * CHUNK)
        grad = grad_gated[here, :]
        mix = mixed[here, :]
        inverse = lax.rsqrt(jnp.mean(mix * mix, axis=-1, keepdims=True) + EPS_GROUP)
        g = gate[here, 3 * HEAD_DIM :].astype(F32)
        s = jax.nn.sigmoid(g)
        unit = mix * inverse
        w = grad * gain[...] * (g * s)
        grad_gain = grad_gain + jnp.sum(grad * unit * (g * s), axis=0, keepdims=True)
        grad_gate_out[here, :] = (grad * unit * gain[...] * (s * (1.0 + g * (1.0 - s)))).astype(BF16)
        grad_mixed = inverse * w - mix * (inverse * inverse * inverse) * jnp.mean(w * mix, axis=-1, keepdims=True)
        grad_mixed_out[here, :] = grad_mixed
        state = state * decay[c : c + 1, :] + mul(grad_mixed, query[here, :], 0, 0)
    start_out[...] = state
    grad_gain_out[...] = jnp.broadcast_to(grad_gain, (PAD, HEAD_DIM))


def backward_kernel(
    grad_mixed,
    conv,
    query,
    key,
    states,
    carry,
    halo,
    proj,
    taps,
    gap,
    grad_out,
    tail_out,
    edge_out,
    small_out,
    rows,
    grads,
):
    length = grad_mixed.shape[0]
    count = length // CHUNK
    rows[0:16, :] = halo[...].astype(F32)
    rows[16:, :] = proj[:, : 3 * HEAD_DIM].astype(F32)
    grads[0:PAD, :] = jnp.zeros((PAD, 3 * HEAD_DIM), F32)
    grads[PAD + length :, :] = jnp.zeros((PAD, 3 * HEAD_DIM), F32)
    lower = triangle(True)
    ones = lower.astype(F32)
    upper = triangle(False).astype(F32)
    last_row = lax.broadcasted_iota(jnp.int32, (CHUNK, HEAD_DIM), 0) == CHUNK - 1
    back = carry[...]
    grad_gap = jnp.zeros((1, HEAD_DIM), F32)
    sums = [jnp.zeros((1, HEAD_DIM), F32) for _ in range(12)]
    for c in reversed(range(count)):
        at = c * CHUNK
        here = slice(at, at + CHUNK)
        c0, c1, values = (conv[here, j * HEAD_DIM : (j + 1) * HEAD_DIM] for j in range(3))
        s1 = jax.nn.sigmoid(c1)
        open_share = 1.0 - s1
        keys = gap[...] * open_share
        forget = 1.0 - keys
        running = mul(ones, jnp.log(forget), 1, 0)
        last = running[CHUNK - 1 : CHUNK, :]
        grown, shrunk, rest = jnp.exp(running), jnp.exp(-running), jnp.exp(last - running)
        q, k, g = query[here, :], key[here, :], grad_mixed[here, :]
        carried = keys * rest
        state = states[c]
        scores = jnp.where(lower, mul(q, k, 1, 1), 0.0)
        grad_scores = jnp.where(lower, mul(g, values, 1, 1), 0.0)
        grad_values = mul(scores, g, 0, 0) + mul(carried, back, 1, 1)
        grad_query = mul(grad_scores, k, 1, 0) + mul(g, state, 1, 0)
        grad_key = mul(grad_scores, q, 0, 0)
        grad_carried = mul(values, back, 1, 0)
        grad_last = jnp.exp(last) * jnp.sum(back * state, axis=0, keepdims=True) + jnp.sum(
            grad_carried * carried, axis=0, keepdims=True
        )
        grad_running = grad_query * q - grad_key * k - grad_carried * carried
        grad_running = grad_running + jnp.where(last_row, grad_last, 0.0)
        grad_keys = grad_key * shrunk + grad_carried * rest
        grad_forget = mul(upper, grad_running, 1, 0) / forget
        inner = grad_forget - grad_keys
        grad_gap = grad_gap - jnp.sum(open_share * inner, axis=0, keepdims=True)
        sigmoid0 = jax.nn.sigmoid(c0)
        new = (
            grad_query * grown * (sigmoid0 * (1.0 + c0 * (1.0 - sigmoid0))),
            gap[...] * s1 * open_share * inner,
            grad_values,
        )
        back = back * jnp.exp(last) + mul(g, q, 0, 0)
        for j in range(3):
            cols = slice(j * HEAD_DIM, (j + 1) * HEAD_DIM)
            grads[PAD + at : PAD + at + CHUNK, cols] = new[j]
            for d in range(4):
                sums[4 * j + d] = sums[4 * j + d] + jnp.sum(
                    new[j] * rows[16 + at - d : 16 + at - d + CHUNK, cols], axis=0, keepdims=True
                )
            total = taps[4 * j : 4 * j + 1, :] * new[j]
            for d in range(1, 4):
                total = total + taps[4 * j + d : 4 * j + d + 1, :] * grads[PAD + at + d : PAD + at + d + CHUNK, cols]
            grad_out[here, cols] = total.astype(BF16)
            if c == count - 1:
                tail_out[:, cols] = total[CHUNK - 16 :]
    for j in range(3):
        cols = slice(j * HEAD_DIM, (j + 1) * HEAD_DIM)
        total = taps[4 * j + 1 : 4 * j + 2, :] * grads[1 : 1 + PAD, cols]
        for d in range(2, 4):
            total = total + taps[4 * j + d : 4 * j + d + 1, :] * grads[d : d + PAD, cols]
        edge_out[:, cols] = total
    for i in range(12):
        small_out[i : i + 1, :] = sums[i]
    small_out[12:13, :] = grad_gap
    small_out[13:16, :] = jnp.zeros((3, HEAD_DIM), F32)


def blocks_of(ids, count):
    member, core = ids[0], ids[1]
    for k in range(2):
        for b in range(count):
            yield k, b, (member ^ b) * 2 + (core ^ k)


def rows_of(blocks, first, count=STEP, cols=slice(None)):
    if isinstance(blocks, (tuple, list)):
        return jnp.concatenate([blocks[first + i][:, cols] for i in range(count)], axis=0)
    part = blocks[first : first + count, :, cols]
    return part.reshape(-1, part.shape[-1])


def fill_columns(weights, source, first, target, rows):
    groups, members, _, depth = source.shape
    per = max(1, 128 // depth)
    for at in range(0, groups * members, per):
        parts = [source[(at + i) // members, (at + i) % members, first : first + rows, :] for i in range(per)]
        part = parts[0] if per == 1 else jnp.concatenate(parts, axis=1)
        weights[target : target + rows, at * depth : (at + per) * depth] = part


def mix_blocks_kernel(mix, out_weight, out):
    groups, heads, depth, _ = out.shape
    for m in range(heads):
        cols = slice(m * HEAD_DIM, (m + 1) * HEAD_DIM)
        turned = out_weight[cols, :].astype(F32).T.astype(BF16)
        for g in range(groups):
            for j in range(4):
                out[g, m, :, j * HEAD_DIM : (j + 1) * HEAD_DIM] = mix[j, :, cols]
            out[g, m, :, 4 * HEAD_DIM :] = turned


def feed_blocks_kernel(up, down, out, turned):
    _, _, units = up.shape
    heads = out.shape[0]
    rows = units // heads
    for j in range(2):
        for t in range(units // 128):
            block = up[j, :, t * 128 : (t + 1) * 128].astype(F32)
            turned[t * 128 : (t + 1) * 128, :] = block.T.astype(BF16)
        for m in range(heads):
            out[m, j * rows : (j + 1) * rows, :] = turned[m * rows : (m + 1) * rows, :]
    for m in range(heads):
        out[m, 2 * rows :, :] = down[m * rows : (m + 1) * rows, :]


def project_kernel(ids, *refs, members):
    own, other = refs[:members], refs[members : 2 * members]
    weights, out, tail = refs[2 * members :]
    half = own[0].shape[0]
    blocks = list(blocks_of(ids, members))
    for at in range(0, len(blocks), STEP):
        k, b, _ = blocks[at]
        result = mul(rows_of((own, other)[k], b), weights[:, : 4 * HEAD_DIM], 1, 0, None).astype(BF16)
        for i in range(STEP):
            to = pl.multiple_of(blocks[at + i][2] * half, half)
            out[pl.ds(to, half), :] = result[i * half : (i + 1) * half]
    tail[...] = out[out.shape[0] - 16 :, : tail.shape[1]]


def feed_kernel(*refs, members):
    own, other, cot_own, cot_other = (refs[i * members : (i + 1) * members] for i in range(4))
    feed, turned, inner_out, mine, away, weights = refs[4 * members :]
    half, width = own[0].shape
    units = feed.shape[2] // 3
    wide = turned.shape[0] // 3
    for j in range(3):
        weights[j * wide + units : (j + 1) * wide, :] = jnp.zeros((wide - units, width), BF16)
        fill_columns(weights, feed, j * units, j * wide, units)
    for k in range(2):
        for b in range(0, members, STEP):
            x = rows_of((own, other)[k], b)
            c = rows_of((cot_own, cot_other)[k], b)
            lifted = mul(x, weights[: 2 * wide], 1, 1, None)
            gate, up_in = lifted[:, :wide], lifted[:, wide:]
            grad = mul(c, weights[2 * wide :], 1, 1, None)
            s = jax.nn.sigmoid(gate)
            act = gate * s
            inner = act * up_in
            grad_gate = grad * up_in * (s * (1.0 + gate * (1.0 - s)))
            grad_up = grad * act
            at = (k * members + b) * half
            cols = slice(at, at + STEP * half)
            turned[0:wide, cols] = grad_gate.T.astype(BF16)
            turned[wide : 2 * wide, cols] = grad_up.T.astype(BF16)
            turned[2 * wide :, cols] = inner.T.astype(BF16)
            inner_out[cols, :] = inner.astype(BF16)
            lift = jnp.concatenate([grad_gate.astype(BF16), grad_up.astype(BF16)], axis=1)
            (mine, away)[k][b : b + STEP] = (
                mul(lift, weights[: 2 * wide], 1, 0, None).astype(BF16).reshape(STEP, half, width)
            )


def block_kernel(inner, feed, mine, away, weights):
    members, half, width = mine.shape
    units, wide = feed.shape[2] // 3, inner.shape[1]
    weights[units:, :] = jnp.zeros((wide - units, width), BF16)
    fill_columns(weights, feed, 2 * units, 0, units)
    for k in range(2):
        for b in range(0, members, STEP):
            at = (k * members + b) * half
            result = mul(inner[at : at + STEP * half, :], weights[...], 1, 0, None)
            (mine, away)[k][b : b + STEP] = result.astype(BF16).reshape(STEP, half, width)


def product_into(ids, out, first, turned, spans, own, other, members, got=None):
    rows = turned.shape[1] // 2
    shards, _, depth = out.shape
    low, high = spans[0][0], spans[-1][1]
    for at in range(0, shards * depth, 256):
        cols = pl.ds(pl.multiple_of(ids[2] * (shards * depth) + at, 128), 256)
        result = mul(turned[low:high, :rows], rows_of(own, 0, members, cols), 1, 0, None)
        result += mul(turned[low:high, rows:], rows_of(other, 0, members, cols), 1, 0, None)
        to = first
        for start, stop in spans:
            here = slice(to, to + stop - start)
            for i in range(256 // depth):
                part = result[start - low : stop - low, i * depth : (i + 1) * depth]
                if got is not None:
                    part = part + got[ids[3], at // depth + i, here, :].astype(F32)
                out[at // depth + i, here, :] = part.astype(BF16)
            to += stop - start


def feed_grad_kernel(ids, *refs, members):
    own, other, cot_own, cot_other = (refs[i * members : (i + 1) * members] for i in range(4))
    turned, *got, out = refs[4 * members :]
    got = got[0] if got else None
    units, wide = out.shape[1] // 3, turned.shape[0] // 3
    product_into(ids, out, 0, turned, [(0, units), (wide, wide + units)], own, other, members, got)
    product_into(ids, out, 2 * units, turned, [(2 * wide, 2 * wide + units)], cot_own, cot_other, members, got)


def mix_grad_kernel(ids, *refs, members):
    own, other, branch_own, branch_other = (refs[i * members : (i + 1) * members] for i in range(4))
    turned, turned_gated, sums, *got, out = refs[4 * members :]
    got = got[0] if got else None
    for m in range(out.shape[0]):
        total = sums[...]
        if got is not None:
            total = total + got[ids[3], m, 5 * HEAD_DIM :, :].astype(F32)
        out[m, 5 * HEAD_DIM :, :] = total.astype(BF16)
    product_into(ids, out, 0, turned, [(0, 4 * HEAD_DIM)], own, other, members, got)
    product_into(ids, out, 4 * HEAD_DIM, turned_gated, [(0, HEAD_DIM)], branch_own, branch_other, members, got)


def project_back_kernel(ids, *refs, members):
    own, other = refs[:members], refs[members : 2 * members]
    grad3, tail, later, grad_gate, weights, norm_gain, turned, mine_out, away_out, norm_out, grads = refs[2 * members :]
    length = grad3.shape[0]
    members, half, width = mine_out.shape
    three = grad3.shape[1]
    grads[:, :three] = grad3[...]
    end = tail.shape[0]
    edge = jnp.concatenate([jnp.zeros((end - later.shape[0], three), F32), later[...]], axis=0)
    grads[length - end :, :three] = (tail[...] + edge).astype(BF16)
    grads[:, three:] = grad_gate[...]
    grad_norm = jnp.zeros((1, width), F32)
    parts = []
    for k, b, block in blocks_of(ids, members):
        parts.append(grads[pl.ds(pl.multiple_of(block * half, half), half), :])
        if len(parts) == STEP:
            x = jnp.concatenate(parts, axis=0)
            at = (k * members + b + 1 - STEP) * half
            turned[:, at : at + STEP * half] = x.astype(F32).T.astype(BF16)
            result = mul(x, weights[:, : 4 * HEAD_DIM], 1, 1, None)
            normed = rows_of((own, other)[k], b + 1 - STEP).astype(F32)
            grad_norm = grad_norm + jnp.sum(result * normed, axis=0, keepdims=True)
            for i in range(STEP):
                to = ids[0] ^ (b + 1 - STEP + i)
                (mine_out, away_out)[k][to] = result[i * half : (i + 1) * half].astype(BF16)
            parts = []
    norm_out[...] = jnp.broadcast_to(grad_norm / norm_gain[...], norm_out.shape)


def mix_total_kernel(got, mix_out, out_out):
    groups, heads, _, depth = got.shape

    def total(i, rows):
        result = got[0, i, rows, :].astype(F32)
        for g in range(1, groups):
            result = result + got[g, i, rows, :].astype(F32)
        return result

    for i in range(heads):
        cols = slice(i * HEAD_DIM, (i + 1) * HEAD_DIM)
        for j in range(4):
            mix_out[j, :, cols] = total(i, slice(j * HEAD_DIM, (j + 1) * HEAD_DIM)).T
        out_out[cols, :] = total(i, slice(4 * HEAD_DIM, 5 * HEAD_DIM))


def feed_total_kernel(got, up_out, down_out, rows):
    heads, three, depth = got.shape
    units = three // 3
    for j in range(2):
        for i in range(heads):
            rows[i * units : (i + 1) * units, :] = got[i, j * units : (j + 1) * units, :].astype(F32)
        for t in range(heads * units // 128):
            up_out[j, :, t * 128 : (t + 1) * 128] = rows[t * 128 : (t + 1) * 128, :].T
    for i in range(heads):
        down_out[i * units : (i + 1) * units, :] = got[i, 2 * units :, :].astype(F32)


def call(kernel, outs, args, scratch=(), ids=None, behind=(), us=5, mib=20):
    specs = [pl.BlockSpec(memory_space=pltpu.VMEM)] * len(args)
    if ids is not None:
        specs = [pl.BlockSpec(memory_space=pltpu.SMEM)] + specs
        args = (ids,) + tuple(args)
    real = len(args)

    def body(*refs):
        kernel(*refs[:real], *refs[real + len(behind) :])

    return pl.pallas_call(
        body,
        out_shape=[jax.ShapeDtypeStruct(s, d) for s, d in outs],
        in_specs=specs + [pl.BlockSpec(memory_space=pl.ANY)] * len(behind),
        out_specs=[pl.BlockSpec(memory_space=pltpu.VMEM)] * len(outs),
        scratch_shapes=list(scratch),
        compiler_params=pltpu.CompilerParams(vmem_limit_bytes=mib * MIB),
        cost_estimate=pl.CostEstimate(flops=0, bytes_accessed=us * 3000000, transcendentals=0),
    )(*args, *behind)


class Group:
    def __init__(self, heads):
        self.size = heads
        self.peers = lax.axis_size("seq")
        self.count = self.peers // heads
        self.member = lax.rem(lax.axis_index("seq"), heads)
        self.index = lax.div(lax.axis_index("seq"), heads)
        self.core = lax.axis_index("head")
        self.ids = jnp.stack([self.member, self.core]).astype(jnp.int32)
        self.lists = [list(range(g * heads, (g + 1) * heads)) for g in range(self.count)]
        self.columns = [list(range(m, self.peers, heads)) for m in range(heads)]

    def swap(self, value, bits):
        return lax.ppermute(value, "seq", [(s, s ^ bits) for s in range(self.peers)])

    def other_core(self, value):
        return lax.ppermute(value, "head", [(0, 1), (1, 0)])

    def shift(self, value, groups):
        step = groups * self.size
        pairs = [(s, s + step) for s in range(self.peers) if 0 <= s + step < self.peers]
        return lax.ppermute(value, "seq", pairs)

    def carry(self, state, decay, sign):
        total = None
        for k in reversed(range(1, self.count)):
            new = self.shift(state, sign * k)
            total = new if total is None else new + total * self.shift(decay, sign * k)
        return jnp.zeros_like(state) if total is None else total

    def gather(self, half):
        got = {0: half}
        for bits in (4, 1, 2):
            got[bits] = self.swap(half, bits)
        got[6] = self.swap(got[4], 2)
        got[5] = self.swap(got[4], 1)
        got[3] = self.swap(got[2], 1)
        got[7] = self.swap(got[5], 2)
        own = [got[bits] for bits in range(self.size)]
        return own, [self.other_core(block) for block in own]

    def over_members(self, part, before_last=()):
        def add(to, source, bits):
            part[to] = part[to] + self.swap(part[source].astype(BF16), bits).astype(F32)

        add(5, 7, 2)
        add(2, 3, 1)
        add(4, 6, 2)
        add(0, 1, 1)
        add(4, 5, 1)
        add(0, 2, 2)
        part[4] = after(part[4], *before_last)
        add(0, 4, 4)
        return part[0]

    def scatter(self, mine, other, before_last=()):
        part = [mine[b].astype(F32) + other[b].astype(F32) for b in range(self.size)]
        return self.over_members(part, before_last)

    def spread(self, blocks):
        return lax.all_to_all(blocks, "seq", 0, 0, axis_index_groups=self.lists, tiled=True)

    def all_groups(self, value):
        return lax.all_gather(value, "seq", axis_index_groups=self.columns)

    def away(self, kernel, rows, depth, args, us):
        count = 1 if self.count == 2 else self.count
        ids = jnp.stack([self.member, self.core, (1 - self.index) * (count == 1), 0 * self.core]).astype(jnp.int32)
        (out,) = call(kernel, [((count * self.size, rows, depth), BF16)], args, (), ids, us=us, mib=28)
        if count == 1:
            return self.all_groups(out)
        out = out.reshape(count, self.size, rows, depth)
        return lax.psum_scatter(out, "seq", axis_index_groups=self.columns)

    def over_groups(self, kernel, args, got, behind, us):
        if self.count != 2:
            return got
        ids = jnp.stack([self.member, self.core, self.index, 1 - self.index]).astype(jnp.int32)
        return call(kernel, [(got.shape[1:], BF16)], (*args, got), (), ids, behind, us, 28)[0]


def inverse_of(rows):
    return lax.rsqrt(jnp.mean(rows * rows, axis=-1, keepdims=True) + EPS_TOKEN)


def norm_back(rows, inverse, gain, grad):
    scaled = grad * gain
    dot_term = jnp.mean(scaled * rows, axis=-1, keepdims=True)
    grad_rows = inverse * scaled - rows * (inverse * inverse * inverse) * dot_term
    return grad_rows, jnp.sum(grad * rows * inverse, axis=0)


def together(steps, *args):
    shapes = jax.eval_shape(steps, *args)
    always = lax.axis_index("seq") < 2 * lax.axis_size("seq")

    def never(*_):
        return jax.tree.map(lambda leaf: jnp.zeros(leaf.shape, leaf.dtype), shapes)

    return lax.cond(always, steps, never, *args)


def after(value, *earlier):
    return lax.optimization_barrier((value,) + earlier)[0]


def shards(
    tokens,
    norm1_gain,
    mix_weight,
    conv_weight,
    decay_gap,
    group_gain,
    out_weight,
    norm2_gain,
    up_pair,
    down_weight,
    cotangent,
):
    depth = mix_weight.shape[1]
    heads = mix_weight.shape[2] // HEAD_DIM
    units = down_weight.shape[0] // heads
    wide = -(-units // 128) * 128
    local, width = tokens.shape
    half = local // 2
    group = Group(heads)
    ids, member, core = group.ids, group.member, group.core
    length = heads * local
    count = length // CHUNK
    groups, peers = group.count, group.peers

    def my_half(rows):
        return lax.dynamic_slice_in_dim(rows, core * half, half, 0)

    def own_head(array):
        return lax.dynamic_slice_in_dim(array, member * HEAD_DIM, HEAD_DIM, array.ndim - 1)

    taps = own_head(conv_weight).reshape(12, HEAD_DIM)
    gap = own_head(decay_gap).reshape(1, HEAD_DIM)
    gain = own_head(group_gain).reshape(1, HEAD_DIM)

    everything = jnp.stack([member, core, 0 * core, 0 * core]).astype(jnp.int32)
    square = ((HEAD_DIM, HEAD_DIM), F32)
    all_rows = ((heads, half, width), BF16)

    def many(n, dtype=F32):
        return ((length, n * HEAD_DIM), dtype)

    token_rows = tokens.astype(F32)
    inverse1 = inverse_of(token_rows)
    half_tokens = my_half(token_rows)
    half_inverse1 = my_half(inverse1)
    cot_half = my_half(cotangent)

    def start_steps(rows, mix_weight, out_weight, up, down):
        own, other = group.gather(rows)
        (mix_blocks,) = call(
            mix_blocks_kernel, [((groups, heads, depth, 5 * HEAD_DIM), BF16)], (mix_weight, out_weight), us=2
        )
        mix_blocks = mix_blocks.reshape(peers, depth, 5 * HEAD_DIM)
        mix_own = lax.all_to_all(mix_blocks, "seq", 0, 0, tiled=True).reshape(width, 5 * HEAD_DIM)
        (feed_blocks,) = call(
            feed_blocks_kernel,
            [((heads, 3 * units, depth), BF16)],
            (up, down),
            [pltpu.VMEM((heads * units, depth), BF16)],
            us=3,
        )
        projected, tail = call(
            functools.partial(project_kernel, members=heads),
            [((length, 4 * HEAD_DIM), BF16), ((16, 3 * HEAD_DIM), BF16)],
            (*own, *other, mix_own),
            (),
            ids,
        )
        halo = group.shift(tail, 1)
        feed = group.spread(after(feed_blocks, halo))
        conv, query, key, totals, states, mixed_here, last = call(
            forward_kernel,
            [
                many(3),
                many(1),
                many(1),
                ((count, HEAD_DIM), F32),
                ((count, HEAD_DIM, HEAD_DIM), F32),
                many(1),
                ((HEAD_DIM + PAD, HEAD_DIM), F32),
            ],
            (projected, halo, taps, gap),
            [pltpu.VMEM((length + 16, 3 * HEAD_DIM), F32)],
        )
        own_decay = last[HEAD_DIM : HEAD_DIM + 1]
        carry = group.carry(last[:HEAD_DIM], own_decay, 1)
        decays = jnp.exp(jnp.concatenate([totals[1:] - totals[:-1], jnp.log(own_decay) - totals[-1:]], axis=0))
        kept = (mix_own, projected, halo, conv, query, key)
        return own, other, feed, kept, (own_decay, decays), (mixed_here, totals, states, carry)

    normed1, normed1_other, feed_here, kept, decay_rows, here = together(
        start_steps,
        (half_tokens * half_inverse1 * norm1_gain).astype(BF16),
        mix_weight,
        out_weight,
        up_pair,
        down_weight,
    )
    feed_own = group.all_groups(feed_here)

    def both_halves(rows):
        other = group.other_core(rows)
        return jnp.where(core == 0, jnp.concatenate([rows, other], 0), jnp.concatenate([other, rows], 0))

    def forward_steps(kept, here, cot_half):
        mix_own, projected, _, _, query, _ = kept
        mixed_here, totals, states, carry = here
        cot, cot_other = group.gather(cot_half)
        mixed, states, turned_gated, mine, away = call(
            gate_kernel,
            [many(1), ((count, HEAD_DIM, HEAD_DIM), F32), ((HEAD_DIM, length), BF16), all_rows, all_rows],
            (mixed_here, query, totals, states, carry, projected, gain, mix_own),
            [pltpu.VMEM((length, HEAD_DIM), BF16)],
            ids,
        )
        hidden = half_tokens + group.scatter(mine, group.other_core(away))
        inverse2 = inverse_of(hidden)
        normed2, normed2_other = group.gather((hidden * inverse2 * norm2_gain).astype(BF16))
        return (states, mixed), (*normed2, *normed2_other, *cot, *cot_other), (turned_gated, hidden, inverse2, both_halves(inverse2))

    mixed_rows, feed_rows, (turned_gated, hidden, inverse2, inverse2_all) = together(
        forward_steps, kept, here, cot_half
    )
    kept = (*kept, *mixed_rows, *decay_rows)
    turned, inner, mine, away = call(
        functools.partial(feed_kernel, members=heads),
        [((3 * wide, length), BF16), ((length, wide), BF16), all_rows, all_rows],
        (*feed_rows, feed_own),
        [pltpu.VMEM((3 * wide, width), BF16)],
        us=17,
        mib=38,
    )
    feed_grad = functools.partial(feed_grad_kernel, members=heads)
    feed_args = (*feed_rows, turned)
    other = group.other_core(away)
    feed_away = group.away(feed_grad, 3 * units, depth, feed_args, 7)

    def backward_steps(mine, other, kept, hidden, inverse2, normed1, normed1_other, turned_gated):
        mix_own, projected, halo, conv, query, key, states, mixed, own_decay, decays = kept
        grad_normed2 = group.scatter(mine, other)
        grad_hidden_norm, grad_norm2 = norm_back(hidden, inverse2, norm2_gain, grad_normed2)
        grad_hidden = cot_half.astype(F32) + grad_hidden_norm
        branch, branch_other = group.gather(grad_hidden.astype(BF16))
        grad_mixed, grad_gate_rows, grad_group, start_grad = call(
            functools.partial(gate_back_kernel, members=heads),
            [many(1), many(1, BF16), ((PAD, HEAD_DIM), F32), square],
            (*branch, *branch_other, mix_own, mixed, projected, gain, query, decays),
            [pltpu.VMEM((length, HEAD_DIM), F32)],
            ids,
        )
        back_carry = group.carry(start_grad, own_decay, -1)
        grad_rows3, grad_tail, edge, small = call(
            backward_kernel,
            [many(3, BF16), ((16, 3 * HEAD_DIM), F32), ((PAD, 3 * HEAD_DIM), F32), ((16, HEAD_DIM), F32)],
            (grad_mixed, conv, query, key, states, back_carry, halo, projected, taps, gap),
            [
                pltpu.VMEM((length + 16, 3 * HEAD_DIM), F32),
                pltpu.VMEM((length + 2 * PAD, 3 * HEAD_DIM), F32),
            ],
            us=8,
        )
        later = group.shift(edge, -1)
        turned_mix, mine, away, grad_norm1 = call(
            functools.partial(project_back_kernel, members=heads),
            [((4 * HEAD_DIM, length), BF16), all_rows, all_rows, ((PAD, width), F32)],
            (
                *normed1,
                *normed1_other,
                grad_rows3,
                grad_tail,
                later,
                grad_gate_rows,
                mix_own,
                norm1_gain.reshape(1, width),
            ),
            [pltpu.VMEM((length, 4 * HEAD_DIM), BF16)],
            ids,
            us=7,
            mib=28,
        )
        sums = jnp.concatenate([small[:13].reshape(-1), grad_group[0], grad_norm1[0], grad_norm2]).astype(BF16)
        sums = jnp.pad(sums, (0, extra * depth - sums.shape[0])).reshape(extra, depth)
        (grad_mix,) = call(
            functools.partial(mix_grad_kernel, members=heads),
            [((peers, 5 * HEAD_DIM + extra, depth), BF16)],
            (*normed1, *normed1_other, *branch, *branch_other, turned_mix, turned_gated, sums),
            (),
            everything,
            us=7,
            mib=28,
        )
        both = (mine.astype(F32) + group.other_core(away).astype(F32)).astype(BF16)
        return grad_hidden, grad_mix, both

    extra = -(-(14 * HEAD_DIM + 2 * width) // (16 * depth)) * 16
    grad_hidden, grad_mix, both = together(
        backward_steps, mine, other, kept, hidden, inverse2, normed1, normed1_other, turned_gated
    )
    grad_normed1 = lax.psum_scatter(both, "seq", axis_index_groups=group.lists)
    mix_got = lax.all_to_all(after(grad_mix, feed_away), "seq", 0, 0, tiled=True)
    feed_total = group.over_groups(feed_grad, feed_args, feed_away, (grad_mix,), 8)
    (block_mine, block_away) = call(
        block_kernel, [all_rows, all_rows], (inner, feed_own), [pltpu.VMEM((wide, width), BF16)], None, (feed_total,)
    )
    feed_got = group.spread(after(feed_total, mix_got))
    mix_total, out_total = call(
        mix_total_kernel,
        [((4, depth, heads * HEAD_DIM), F32), ((heads * HEAD_DIM, depth), F32)],
        (mix_got.reshape(groups, heads, 5 * HEAD_DIM + extra, depth),),
        us=4,
    )
    sums = mix_got[:, 5 * HEAD_DIM :].reshape(groups, heads, -1).astype(F32).sum(0)
    own_sums = sums[:, : 14 * HEAD_DIM].reshape(heads, 14, HEAD_DIM).transpose(1, 0, 2).reshape(14, heads * HEAD_DIM)
    norms = sums[:, 14 * HEAD_DIM : 14 * HEAD_DIM + 2 * width].sum(0).reshape(2, width)
    norms = norms + group.other_core(norms)
    block_half = hidden + group.scatter(
        block_mine, group.other_core(block_away), (mix_total, out_total, own_sums, norms)
    )
    grad_normed1 = after(grad_normed1, block_half).astype(F32)
    grad_rows1 = norm_back(half_tokens, half_inverse1, norm1_gain, grad_normed1)[0]
    grad_tokens = grad_hidden + grad_rows1
    up_total, down_total = call(
        feed_total_kernel,
        [((2, depth, heads * units), F32), ((heads * units, depth), F32)],
        (feed_got,),
        [pltpu.VMEM((heads * units, depth), F32)],
    )
    block_out = both_halves(block_half)
    grad_tokens = both_halves(grad_tokens)

    inverse_rms = jnp.stack([inverse1[:, 0], inverse2_all[:, 0]])
    return (
        block_out,
        grad_tokens,
        norms[0],
        mix_total,
        own_sums[:12].reshape(3, 4, heads * HEAD_DIM),
        own_sums[12],
        own_sums[13],
        out_total,
        norms[1],
        up_total,
        down_total,
        inverse_rms,
    )


def solution(mesh):
    in_specs = (
        P("seq", None),
        P(),
        P(None, "seq", "head"),
        P(None, None, "head"),
        P("head"),
        P("head"),
        P("head", "seq"),
        P(),
        P(None, "seq", "head"),
        P("head", "seq"),
        P("seq", None),
    )
    out_specs = (
        P("seq", None),
        P("seq", None),
        P(),
        P(None, "seq", "head"),
        P(None, None, "head"),
        P("head"),
        P("head"),
        P("head", "seq"),
        P(),
        P(None, "seq", "head"),
        P("head", "seq"),
        P(None, "seq"),
    )
    return jax.shard_map(shards, mesh=mesh, in_specs=in_specs, out_specs=out_specs, check_vma=False)
```

```python
import functools

import jax
import jax.numpy as jnp
from jax import lax
from jax.experimental import pallas as pl
from jax.experimental.pallas import tpu as pltpu
from jax.sharding import PartitionSpec as P

HEAD_DIM = 128
CHUNK = 128
PAD = 8
STEP = 4
EPS_TOKEN = 1e-06
EPS_GROUP = 1e-05
HIGH = lax.Precision.HIGHEST
F32 = jnp.float32
BF16 = jnp.bfloat16
MIB = 1024 * 1024


def mul(a, b, ca, cb, precision=HIGH):
    return lax.dot_general(
        a, b, (((ca,), (cb,)), ((), ())), precision=precision, preferred_element_type=F32
    )


def dsilu(v):
    s = jax.nn.sigmoid(v)
    return s * (1.0 + v * (1.0 - s))


def triangle(lower):
    row = lax.broadcasted_iota(jnp.int32, (CHUNK, CHUNK), 0)
    col = lax.broadcasted_iota(jnp.int32, (CHUNK, CHUNK), 1)
    return (row >= col) if lower else (row <= col)


def forward_kernel(
    proj, halo, taps, gap, conv_out, query_out, key_out, total_out, state_out, local_out, last_out, rows
):
    length = proj.shape[0]
    rows[0:16, :] = halo[...].astype(F32)
    rows[16:, :] = proj[:, : 3 * HEAD_DIM].astype(F32)
    lower = triangle(True)
    ones = lower.astype(F32)
    state = jnp.zeros((HEAD_DIM, HEAD_DIM), F32)
    before = jnp.zeros((1, HEAD_DIM), F32)
    for c in range(length // CHUNK):
        at = c * CHUNK
        here = slice(at, at + CHUNK)
        conv = []
        for j in range(3):
            cols = slice(j * HEAD_DIM, (j + 1) * HEAD_DIM)
            total = taps[4 * j : 4 * j + 1, :] * rows[16 + at : 16 + at + CHUNK, cols]
            for d in range(1, 4):
                total = total + taps[4 * j + d : 4 * j + d + 1, :] * rows[16 + at - d : 16 + at - d + CHUNK, cols]
            conv.append(total)
            conv_out[here, cols] = total
        queries = conv[0] * jax.nn.sigmoid(conv[0])
        open_share = 1.0 - jax.nn.sigmoid(conv[1])
        keys = gap[...] * open_share
        log_forget = jnp.log(1.0 - keys)
        values = conv[2]
        running = mul(ones, log_forget, 1, 0)
        last = running[CHUNK - 1 : CHUNK, :]
        query = queries * jnp.exp(running)
        key = keys * jnp.exp(-running)
        carried = keys * jnp.exp(last - running)
        query_out[here, :] = query
        key_out[here, :] = key
        total_out[c : c + 1, :] = before
        state_out[c] = state
        scores = jnp.where(lower, mul(query, key, 1, 1), 0.0)
        local_out[here, :] = mul(scores, values, 1, 0) + mul(query, state, 1, 1)
        state = state * jnp.exp(last) + mul(values, carried, 0, 0)
        before = before + last
    last_out[0:HEAD_DIM, :] = state
    last_out[HEAD_DIM:, :] = jnp.broadcast_to(jnp.exp(before), (PAD, HEAD_DIM))


def gate_kernel(
    ids, local, query, total, state, carry, gate, gain, weights, mixed_out, state_out, turned_out, mine, away, gated
):
    length = local.shape[0]
    members, half, _ = mine.shape
    start = carry[...]
    for c in range(length // CHUNK):
        here = slice(c * CHUNK, (c + 1) * CHUNK)
        grown = start * jnp.exp(total[c : c + 1, :])
        state_out[c] = state[c] + grown
        mixed = local[here, :] + mul(query[here, :], grown, 1, 1)
        mixed_out[here, :] = mixed
        inverse = lax.rsqrt(jnp.mean(mixed * mixed, axis=-1, keepdims=True) + EPS_GROUP)
        g = gate[here, 3 * HEAD_DIM :].astype(F32)
        gated[here, :] = (mixed * inverse * gain[...] * (g * jax.nn.sigmoid(g))).astype(BF16)
    parts = []
    for k, b, block in blocks_of(ids, members):
        parts.append(gated[pl.ds(pl.multiple_of(block * half, half), half), :])
        if len(parts) == STEP:
            x = jnp.concatenate(parts, axis=0)
            at = (k * members + b + 1 - STEP) * half
            turned_out[:, at : at + STEP * half] = x.astype(F32).T.astype(BF16)
            result = mul(x, weights[:, 4 * HEAD_DIM :], 1, 1, None).astype(BF16)
            (mine, away)[k][b + 1 - STEP : b + 1] = result.reshape(STEP, half, -1)
            parts = []


def gate_back_kernel(
    ids, *refs, members
):
    own, other = refs[:members], refs[members : 2 * members]
    weights, mixed, gate, gain, query, decay = refs[2 * members : 2 * members + 6]
    grad_mixed_out, grad_gate_out, grad_gain_out, start_out, grad_gated = refs[2 * members + 6 :]
    half = own[0].shape[0]
    at = 0
    blocks = list(blocks_of(ids, members))
    for at in range(0, len(blocks), STEP):
        k, b, _ = blocks[at]
        result = mul(rows_of((own, other)[k], b), weights[:, 4 * HEAD_DIM :], 1, 0, None)
        for i in range(STEP):
            to = pl.multiple_of(blocks[at + i][2] * half, half)
            grad_gated[pl.ds(to, half), :] = result[i * half : (i + 1) * half]
    length = mixed.shape[0]
    count = length // CHUNK
    grad_gain = jnp.zeros((1, HEAD_DIM), F32)
    state = jnp.zeros((HEAD_DIM, HEAD_DIM), F32)
    for c in reversed(range(count)):
        here = slice(c * CHUNK, (c + 1) * CHUNK)
        grad = grad_gated[here, :]
        mix = mixed[here, :]
        inverse = lax.rsqrt(jnp.mean(mix * mix, axis=-1, keepdims=True) + EPS_GROUP)
        g = gate[here, 3 * HEAD_DIM :].astype(F32)
        s = jax.nn.sigmoid(g)
        unit = mix * inverse
        w = grad * gain[...] * (g * s)
        grad_gain = grad_gain + jnp.sum(grad * unit * (g * s), axis=0, keepdims=True)
        grad_gate_out[here, :] = (grad * unit * gain[...] * (s * (1.0 + g * (1.0 - s)))).astype(BF16)
        grad_mixed = inverse * w - mix * (inverse * inverse * inverse) * jnp.mean(w * mix, axis=-1, keepdims=True)
        grad_mixed_out[here, :] = grad_mixed
        state = state * decay[c : c + 1, :] + mul(grad_mixed, query[here, :], 0, 0)
    start_out[...] = state
    grad_gain_out[...] = jnp.broadcast_to(grad_gain, (PAD, HEAD_DIM))


def backward_kernel(
    grad_mixed,
    conv,
    query,
    key,
    states,
    carry,
    halo,
    proj,
    taps,
    gap,
    grad_out,
    tail_out,
    edge_out,
    small_out,
    rows,
    grads,
):
    length = grad_mixed.shape[0]
    count = length // CHUNK
    rows[0:16, :] = halo[...].astype(F32)
    rows[16:, :] = proj[:, : 3 * HEAD_DIM].astype(F32)
    grads[0:PAD, :] = jnp.zeros((PAD, 3 * HEAD_DIM), F32)
    grads[PAD + length :, :] = jnp.zeros((PAD, 3 * HEAD_DIM), F32)
    lower = triangle(True)
    ones = lower.astype(F32)
    upper = triangle(False).astype(F32)
    last_row = lax.broadcasted_iota(jnp.int32, (CHUNK, HEAD_DIM), 0) == CHUNK - 1
    back = carry[...]
    grad_gap = jnp.zeros((1, HEAD_DIM), F32)
    sums = [jnp.zeros((1, HEAD_DIM), F32) for _ in range(12)]
    for c in reversed(range(count)):
        at = c * CHUNK
        here = slice(at, at + CHUNK)
        c0, c1, values = (conv[here, j * HEAD_DIM : (j + 1) * HEAD_DIM] for j in range(3))
        s1 = jax.nn.sigmoid(c1)
        open_share = 1.0 - s1
        keys = gap[...] * open_share
        forget = 1.0 - keys
        running = mul(ones, jnp.log(forget), 1, 0)
        last = running[CHUNK - 1 : CHUNK, :]
        grown, shrunk, rest = jnp.exp(running), jnp.exp(-running), jnp.exp(last - running)
        q, k, g = query[here, :], key[here, :], grad_mixed[here, :]
        carried = keys * rest
        state = states[c]
        scores = jnp.where(lower, mul(q, k, 1, 1), 0.0)
        grad_scores = jnp.where(lower, mul(g, values, 1, 1), 0.0)
        grad_values = mul(scores, g, 0, 0) + mul(carried, back, 1, 1)
        grad_query = mul(grad_scores, k, 1, 0) + mul(g, state, 1, 0)
        grad_key = mul(grad_scores, q, 0, 0)
        grad_carried = mul(values, back, 1, 0)
        grad_last = jnp.exp(last) * jnp.sum(back * state, axis=0, keepdims=True) + jnp.sum(
            grad_carried * carried, axis=0, keepdims=True
        )
        grad_running = grad_query * q - grad_key * k - grad_carried * carried
        grad_running = grad_running + jnp.where(last_row, grad_last, 0.0)
        grad_keys = grad_key * shrunk + grad_carried * rest
        grad_forget = mul(upper, grad_running, 1, 0) / forget
        inner = grad_forget - grad_keys
        grad_gap = grad_gap - jnp.sum(open_share * inner, axis=0, keepdims=True)
        sigmoid0 = jax.nn.sigmoid(c0)
        new = (
            grad_query * grown * (sigmoid0 * (1.0 + c0 * (1.0 - sigmoid0))),
            gap[...] * s1 * open_share * inner,
            grad_values,
        )
        back = back * jnp.exp(last) + mul(g, q, 0, 0)
        for j in range(3):
            cols = slice(j * HEAD_DIM, (j + 1) * HEAD_DIM)
            grads[PAD + at : PAD + at + CHUNK, cols] = new[j]
            for d in range(4):
                sums[4 * j + d] = sums[4 * j + d] + jnp.sum(
                    new[j] * rows[16 + at - d : 16 + at - d + CHUNK, cols], axis=0, keepdims=True
                )
            total = taps[4 * j : 4 * j + 1, :] * new[j]
            for d in range(1, 4):
                total = total + taps[4 * j + d : 4 * j + d + 1, :] * grads[PAD + at + d : PAD + at + d + CHUNK, cols]
            grad_out[here, cols] = total.astype(BF16)
            if c == count - 1:
                tail_out[:, cols] = total[CHUNK - 16 :]
    for j in range(3):
        cols = slice(j * HEAD_DIM, (j + 1) * HEAD_DIM)
        total = taps[4 * j + 1 : 4 * j + 2, :] * grads[1 : 1 + PAD, cols]
        for d in range(2, 4):
            total = total + taps[4 * j + d : 4 * j + d + 1, :] * grads[d : d + PAD, cols]
        edge_out[:, cols] = total
    for i in range(12):
        small_out[i : i + 1, :] = sums[i]
    small_out[12:13, :] = grad_gap
    small_out[13:16, :] = jnp.zeros((3, HEAD_DIM), F32)


def blocks_of(ids, count):
    member, core = ids[0], ids[1]
    for k in range(2):
        for b in range(count):
            yield k, b, (member ^ b) * 2 + (core ^ k)


def rows_of(blocks, first, count=STEP, cols=slice(None)):
    if isinstance(blocks, (tuple, list)):
        return jnp.concatenate([blocks[first + i][:, cols] for i in range(count)], axis=0)
    part = blocks[first : first + count, :, cols]
    return part.reshape(-1, part.shape[-1])


def fill_columns(weights, source, first, target, rows):
    groups, members, _, depth = source.shape
    per = max(1, 128 // depth)
    for at in range(0, groups * members, per):
        parts = [source[(at + i) // members, (at + i) % members, first : first + rows, :] for i in range(per)]
        part = parts[0] if per == 1 else jnp.concatenate(parts, axis=1)
        weights[target : target + rows, at * depth : (at + per) * depth] = part


def mix_blocks_kernel(mix, out_weight, out):
    groups, heads, depth, _ = out.shape
    for m in range(heads):
        cols = slice(m * HEAD_DIM, (m + 1) * HEAD_DIM)
        turned = out_weight[cols, :].astype(F32).T.astype(BF16)
        for g in range(groups):
            for j in range(4):
                out[g, m, :, j * HEAD_DIM : (j + 1) * HEAD_DIM] = mix[j, :, cols]
            out[g, m, :, 4 * HEAD_DIM :] = turned


def feed_blocks_kernel(up, down, out, turned):
    _, _, units = up.shape
    heads = out.shape[0]
    rows = units // heads
    for j in range(2):
        for t in range(units // 128):
            block = up[j, :, t * 128 : (t + 1) * 128].astype(F32)
            turned[t * 128 : (t + 1) * 128, :] = block.T.astype(BF16)
        for m in range(heads):
            out[m, j * rows : (j + 1) * rows, :] = turned[m * rows : (m + 1) * rows, :]
    for m in range(heads):
        out[m, 2 * rows :, :] = down[m * rows : (m + 1) * rows, :]


def project_kernel(ids, *refs, members):
    own, other = refs[:members], refs[members : 2 * members]
    weights, out, tail = refs[2 * members :]
    half = own[0].shape[0]
    blocks = list(blocks_of(ids, members))
    for at in range(0, len(blocks), STEP):
        k, b, _ = blocks[at]
        result = mul(rows_of((own, other)[k], b), weights[:, : 4 * HEAD_DIM], 1, 0, None).astype(BF16)
        for i in range(STEP):
            to = pl.multiple_of(blocks[at + i][2] * half, half)
            out[pl.ds(to, half), :] = result[i * half : (i + 1) * half]
    tail[...] = out[out.shape[0] - 16 :, : tail.shape[1]]


def feed_kernel(*refs, members):
    own, other, cot_own, cot_other = (refs[i * members : (i + 1) * members] for i in range(4))
    feed, turned, inner_out, mine, away, weights = refs[4 * members :]
    half, width = own[0].shape
    units = feed.shape[2] // 3
    wide = turned.shape[0] // 3
    for j in range(3):
        weights[j * wide + units : (j + 1) * wide, :] = jnp.zeros((wide - units, width), BF16)
        fill_columns(weights, feed, j * units, j * wide, units)
    for k in range(2):
        for b in range(0, members, STEP):
            x = rows_of((own, other)[k], b)
            c = rows_of((cot_own, cot_other)[k], b)
            lifted = mul(x, weights[: 2 * wide], 1, 1, None)
            gate, up_in = lifted[:, :wide], lifted[:, wide:]
            grad = mul(c, weights[2 * wide :], 1, 1, None)
            s = jax.nn.sigmoid(gate)
            act = gate * s
            inner = act * up_in
            grad_gate = grad * up_in * (s * (1.0 + gate * (1.0 - s)))
            grad_up = grad * act
            at = (k * members + b) * half
            cols = slice(at, at + STEP * half)
            turned[0:wide, cols] = grad_gate.T.astype(BF16)
            turned[wide : 2 * wide, cols] = grad_up.T.astype(BF16)
            turned[2 * wide :, cols] = inner.T.astype(BF16)
            inner_out[cols, :] = inner.astype(BF16)
            lift = jnp.concatenate([grad_gate.astype(BF16), grad_up.astype(BF16)], axis=1)
            (mine, away)[k][b : b + STEP] = (
                mul(lift, weights[: 2 * wide], 1, 0, None).astype(BF16).reshape(STEP, half, width)
            )


def block_kernel(inner, feed, mine, away, weights):
    members, half, width = mine.shape
    units, wide = feed.shape[2] // 3, inner.shape[1]
    weights[units:, :] = jnp.zeros((wide - units, width), BF16)
    fill_columns(weights, feed, 2 * units, 0, units)
    for k in range(2):
        for b in range(0, members, STEP):
            at = (k * members + b) * half
            result = mul(inner[at : at + STEP * half, :], weights[...], 1, 0, None)
            (mine, away)[k][b : b + STEP] = result.astype(BF16).reshape(STEP, half, width)


def product_into(ids, out, first, turned, spans, own, other, members, got=None):
    rows = turned.shape[1] // 2
    shards, _, depth = out.shape
    low, high = spans[0][0], spans[-1][1]
    for at in range(0, shards * depth, 256):
        cols = pl.ds(pl.multiple_of(ids[2] * (shards * depth) + at, 128), 256)
        result = mul(turned[low:high, :rows], rows_of(own, 0, members, cols), 1, 0, None)
        result += mul(turned[low:high, rows:], rows_of(other, 0, members, cols), 1, 0, None)
        to = first
        for start, stop in spans:
            here = slice(to, to + stop - start)
            for i in range(256 // depth):
                part = result[start - low : stop - low, i * depth : (i + 1) * depth]
                if got is not None:
                    part = part + got[ids[3], at // depth + i, here, :].astype(F32)
                out[at // depth + i, here, :] = part.astype(BF16)
            to += stop - start


def feed_grad_kernel(ids, *refs, members):
    own, other, cot_own, cot_other = (refs[i * members : (i + 1) * members] for i in range(4))
    turned, *got, out = refs[4 * members :]
    got = got[0] if got else None
    units, wide = out.shape[1] // 3, turned.shape[0] // 3
    product_into(ids, out, 0, turned, [(0, units), (wide, wide + units)], own, other, members, got)
    product_into(ids, out, 2 * units, turned, [(2 * wide, 2 * wide + units)], cot_own, cot_other, members, got)


def mix_grad_kernel(ids, *refs, members):
    own, other, branch_own, branch_other = (refs[i * members : (i + 1) * members] for i in range(4))
    turned, turned_gated, sums, *got, out = refs[4 * members :]
    got = got[0] if got else None
    for m in range(out.shape[0]):
        total = sums[...]
        if got is not None:
            total = total + got[ids[3], m, 5 * HEAD_DIM :, :].astype(F32)
        out[m, 5 * HEAD_DIM :, :] = total.astype(BF16)
    product_into(ids, out, 0, turned, [(0, 4 * HEAD_DIM)], own, other, members, got)
    product_into(ids, out, 4 * HEAD_DIM, turned_gated, [(0, HEAD_DIM)], branch_own, branch_other, members, got)


def project_back_kernel(ids, *refs, members):
    own, other = refs[:members], refs[members : 2 * members]
    grad3, tail, later, grad_gate, weights, norm_gain, turned, mine_out, away_out, norm_out, grads = refs[2 * members :]
    length = grad3.shape[0]
    members, half, width = mine_out.shape
    three = grad3.shape[1]
    grads[:, :three] = grad3[...]
    end = tail.shape[0]
    edge = jnp.concatenate([jnp.zeros((end - later.shape[0], three), F32), later[...]], axis=0)
    grads[length - end :, :three] = (tail[...] + edge).astype(BF16)
    grads[:, three:] = grad_gate[...]
    grad_norm = jnp.zeros((1, width), F32)
    parts = []
    for k, b, block in blocks_of(ids, members):
        parts.append(grads[pl.ds(pl.multiple_of(block * half, half), half), :])
        if len(parts) == STEP:
            x = jnp.concatenate(parts, axis=0)
            at = (k * members + b + 1 - STEP) * half
            turned[:, at : at + STEP * half] = x.astype(F32).T.astype(BF16)
            result = mul(x, weights[:, : 4 * HEAD_DIM], 1, 1, None)
            normed = rows_of((own, other)[k], b + 1 - STEP).astype(F32)
            grad_norm = grad_norm + jnp.sum(result * normed, axis=0, keepdims=True)
            for i in range(STEP):
                to = ids[0] ^ (b + 1 - STEP + i)
                (mine_out, away_out)[k][to] = result[i * half : (i + 1) * half].astype(BF16)
            parts = []
    norm_out[...] = jnp.broadcast_to(grad_norm / norm_gain[...], norm_out.shape)


def mix_total_kernel(got, mix_out, out_out):
    groups, heads, _, depth = got.shape

    def total(i, rows):
        result = got[0, i, rows, :].astype(F32)
        for g in range(1, groups):
            result = result + got[g, i, rows, :].astype(F32)
        return result

    for i in range(heads):
        cols = slice(i * HEAD_DIM, (i + 1) * HEAD_DIM)
        for j in range(4):
            mix_out[j, :, cols] = total(i, slice(j * HEAD_DIM, (j + 1) * HEAD_DIM)).T
        out_out[cols, :] = total(i, slice(4 * HEAD_DIM, 5 * HEAD_DIM))


def feed_total_kernel(got, up_out, down_out, rows):
    heads, three, depth = got.shape
    units = three // 3
    for j in range(2):
        for i in range(heads):
            rows[i * units : (i + 1) * units, :] = got[i, j * units : (j + 1) * units, :].astype(F32)
        for t in range(heads * units // 128):
            up_out[j, :, t * 128 : (t + 1) * 128] = rows[t * 128 : (t + 1) * 128, :].T
    for i in range(heads):
        down_out[i * units : (i + 1) * units, :] = got[i, 2 * units :, :].astype(F32)


def call(kernel, outs, args, scratch=(), ids=None, behind=(), us=5, mib=20):
    specs = [pl.BlockSpec(memory_space=pltpu.VMEM)] * len(args)
    if ids is not None:
        specs = [pl.BlockSpec(memory_space=pltpu.SMEM)] + specs
        args = (ids,) + tuple(args)
    real = len(args)

    def body(*refs):
        kernel(*refs[:real], *refs[real + len(behind) :])

    return pl.pallas_call(
        body,
        out_shape=[jax.ShapeDtypeStruct(s, d) for s, d in outs],
        in_specs=specs + [pl.BlockSpec(memory_space=pl.ANY)] * len(behind),
        out_specs=[pl.BlockSpec(memory_space=pltpu.VMEM)] * len(outs),
        scratch_shapes=list(scratch),
        compiler_params=pltpu.CompilerParams(vmem_limit_bytes=mib * MIB),
        cost_estimate=pl.CostEstimate(flops=0, bytes_accessed=us * 3000000, transcendentals=0),
    )(*args, *behind)


class Group:
    def __init__(self, heads):
        self.size = heads
        self.peers = lax.axis_size("seq")
        self.count = self.peers // heads
        self.member = lax.rem(lax.axis_index("seq"), heads)
        self.index = lax.div(lax.axis_index("seq"), heads)
        self.core = lax.axis_index("head")
        self.ids = jnp.stack([self.member, self.core]).astype(jnp.int32)
        self.lists = [list(range(g * heads, (g + 1) * heads)) for g in range(self.count)]
        self.columns = [list(range(m, self.peers, heads)) for m in range(heads)]

    def swap(self, value, bits):
        return lax.ppermute(value, "seq", [(s, s ^ bits) for s in range(self.peers)])

    def other_core(self, value):
        return lax.ppermute(value, "head", [(0, 1), (1, 0)])

    def shift(self, value, groups):
        step = groups * self.size
        pairs = [(s, s + step) for s in range(self.peers) if 0 <= s + step < self.peers]
        return lax.ppermute(value, "seq", pairs)

    def carry(self, state, decay, sign):
        total = None
        for k in reversed(range(1, self.count)):
            new = self.shift(state, sign * k)
            total = new if total is None else new + total * self.shift(decay, sign * k)
        return jnp.zeros_like(state) if total is None else total

    def gather(self, half):
        got = {0: half}
        for bits in (4, 1, 2):
            got[bits] = self.swap(half, bits)
        got[6] = self.swap(got[4], 2)
        got[5] = self.swap(got[4], 1)
        got[3] = self.swap(got[2], 1)
        got[7] = self.swap(got[5], 2)
        own = [got[bits] for bits in range(self.size)]
        return own, [self.other_core(block) for block in own]

    def over_members(self, part, before_last=()):
        def add(to, source, bits):
            part[to] = part[to] + self.swap(part[source].astype(BF16), bits).astype(F32)

        add(5, 7, 2)
        add(2, 3, 1)
        add(4, 6, 2)
        add(0, 1, 1)
        add(4, 5, 1)
        add(0, 2, 2)
        part[4] = after(part[4], *before_last)
        add(0, 4, 4)
        return part[0]

    def scatter(self, mine, other, before_last=()):
        part = [mine[b].astype(F32) + other[b].astype(F32) for b in range(self.size)]
        return self.over_members(part, before_last)

    def spread(self, blocks):
        return lax.all_to_all(blocks, "seq", 0, 0, axis_index_groups=self.lists, tiled=True)

    def all_groups(self, value):
        return lax.all_gather(value, "seq", axis_index_groups=self.columns)

    def away(self, kernel, rows, depth, args, us):
        count = 1 if self.count == 2 else self.count
        ids = jnp.stack([self.member, self.core, (1 - self.index) * (count == 1), 0 * self.core]).astype(jnp.int32)
        (out,) = call(kernel, [((count * self.size, rows, depth), BF16)], args, (), ids, us=us, mib=28)
        if count == 1:
            return self.all_groups(out)
        out = out.reshape(count, self.size, rows, depth)
        return lax.psum_scatter(out, "seq", axis_index_groups=self.columns)

    def over_groups(self, kernel, args, got, behind, us):
        if self.count != 2:
            return got
        ids = jnp.stack([self.member, self.core, self.index, 1 - self.index]).astype(jnp.int32)
        return call(kernel, [(got.shape[1:], BF16)], (*args, got), (), ids, behind, us, 28)[0]


def inverse_of(rows):
    return lax.rsqrt(jnp.mean(rows * rows, axis=-1, keepdims=True) + EPS_TOKEN)


def norm_back(rows, inverse, gain, grad):
    scaled = grad * gain
    dot_term = jnp.mean(scaled * rows, axis=-1, keepdims=True)
    grad_rows = inverse * scaled - rows * (inverse * inverse * inverse) * dot_term
    return grad_rows, jnp.sum(grad * rows * inverse, axis=0)


def together(steps, *args):
    shapes = jax.eval_shape(steps, *args)
    always = lax.axis_index("seq") < 2 * lax.axis_size("seq")

    def never(*_):
        return jax.tree.map(lambda leaf: jnp.zeros(leaf.shape, leaf.dtype), shapes)

    return lax.cond(always, steps, never, *args)


def after(value, *earlier):
    return lax.optimization_barrier((value,) + earlier)[0]


def shards(
    tokens,
    norm1_gain,
    mix_weight,
    conv_weight,
    decay_gap,
    group_gain,
    out_weight,
    norm2_gain,
    up_pair,
    down_weight,
    cotangent,
):
    depth = mix_weight.shape[1]
    heads = mix_weight.shape[2] // HEAD_DIM
    units = down_weight.shape[0] // heads
    wide = -(-units // 128) * 128
    local, width = tokens.shape
    half = local // 2
    group = Group(heads)
    ids, member, core = group.ids, group.member, group.core
    length = heads * local
    count = length // CHUNK
    groups, peers = group.count, group.peers

    def my_half(rows):
        return lax.dynamic_slice_in_dim(rows, core * half, half, 0)

    def own_head(array):
        return lax.dynamic_slice_in_dim(array, member * HEAD_DIM, HEAD_DIM, array.ndim - 1)

    taps = own_head(conv_weight).reshape(12, HEAD_DIM)
    gap = own_head(decay_gap).reshape(1, HEAD_DIM)
    gain = own_head(group_gain).reshape(1, HEAD_DIM)

    everything = jnp.stack([member, core, 0 * core, 0 * core]).astype(jnp.int32)
    square = ((HEAD_DIM, HEAD_DIM), F32)
    all_rows = ((heads, half, width), BF16)

    def many(n, dtype=F32):
        return ((length, n * HEAD_DIM), dtype)

    token_rows = tokens.astype(F32)
    inverse1 = inverse_of(token_rows)
    half_tokens = my_half(token_rows)
    half_inverse1 = my_half(inverse1)
    cot_half = my_half(cotangent)

    def start_steps(rows, mix_weight, out_weight, up, down):
        own, other = group.gather(rows)
        (mix_blocks,) = call(
            mix_blocks_kernel, [((groups, heads, depth, 5 * HEAD_DIM), BF16)], (mix_weight, out_weight), us=2
        )
        mix_blocks = mix_blocks.reshape(peers, depth, 5 * HEAD_DIM)
        mix_own = lax.all_to_all(mix_blocks, "seq", 0, 0, tiled=True).reshape(width, 5 * HEAD_DIM)
        (feed_blocks,) = call(
            feed_blocks_kernel,
            [((heads, 3 * units, depth), BF16)],
            (up, down),
            [pltpu.VMEM((heads * units, depth), BF16)],
            us=3,
        )
        projected, tail = call(
            functools.partial(project_kernel, members=heads),
            [((length, 4 * HEAD_DIM), BF16), ((16, 3 * HEAD_DIM), BF16)],
            (*own, *other, mix_own),
            (),
            ids,
        )
        halo = group.shift(tail, 1)
        feed = group.spread(after(feed_blocks, halo))
        conv, query, key, totals, states, mixed_here, last = call(
            forward_kernel,
            [
                many(3),
                many(1),
                many(1),
                ((count, HEAD_DIM), F32),
                ((count, HEAD_DIM, HEAD_DIM), F32),
                many(1),
                ((HEAD_DIM + PAD, HEAD_DIM), F32),
            ],
            (projected, halo, taps, gap),
            [pltpu.VMEM((length + 16, 3 * HEAD_DIM), F32)],
        )
        own_decay = last[HEAD_DIM : HEAD_DIM + 1]
        carry = group.carry(last[:HEAD_DIM], own_decay, 1)
        decays = jnp.exp(jnp.concatenate([totals[1:] - totals[:-1], jnp.log(own_decay) - totals[-1:]], axis=0))
        kept = (mix_own, projected, halo, conv, query, key)
        return own, other, feed, kept, (own_decay, decays), (mixed_here, totals, states, carry)

    normed1, normed1_other, feed_here, kept, decay_rows, here = together(
        start_steps,
        (half_tokens * half_inverse1 * norm1_gain).astype(BF16),
        mix_weight,
        out_weight,
        up_pair,
        down_weight,
    )
    feed_own = group.all_groups(feed_here)

    def both_halves(rows):
        other = group.other_core(rows)
        return jnp.where(core == 0, jnp.concatenate([rows, other], 0), jnp.concatenate([other, rows], 0))

    def forward_steps(kept, here, cot_half):
        mix_own, projected, _, _, query, _ = kept
        mixed_here, totals, states, carry = here
        cot, cot_other = group.gather(cot_half)
        mixed, states, turned_gated, mine, away = call(
            gate_kernel,
            [many(1), ((count, HEAD_DIM, HEAD_DIM), F32), ((HEAD_DIM, length), BF16), all_rows, all_rows],
            (mixed_here, query, totals, states, carry, projected, gain, mix_own),
            [pltpu.VMEM((length, HEAD_DIM), BF16)],
            ids,
        )
        hidden = half_tokens + group.scatter(mine, group.other_core(away))
        inverse2 = inverse_of(hidden)
        normed2, normed2_other = group.gather((hidden * inverse2 * norm2_gain).astype(BF16))
        return (states, mixed), (*normed2, *normed2_other, *cot, *cot_other), (turned_gated, hidden, inverse2, both_halves(inverse2))

    mixed_rows, feed_rows, (turned_gated, hidden, inverse2, inverse2_all) = together(
        forward_steps, kept, here, cot_half
    )
    kept = (*kept, *mixed_rows, *decay_rows)
    turned, inner, mine, away = call(
        functools.partial(feed_kernel, members=heads),
        [((3 * wide, length), BF16), ((length, wide), BF16), all_rows, all_rows],
        (*feed_rows, feed_own),
        [pltpu.VMEM((3 * wide, width), BF16)],
        us=17,
        mib=38,
    )
    feed_grad = functools.partial(feed_grad_kernel, members=heads)
    feed_args = (*feed_rows, turned)
    other = group.other_core(away)
    feed_away = group.away(feed_grad, 3 * units, depth, feed_args, 7)

    def backward_steps(mine, other, kept, hidden, inverse2, normed1, normed1_other, turned_gated):
        mix_own, projected, halo, conv, query, key, states, mixed, own_decay, decays = kept
        grad_normed2 = group.scatter(mine, other)
        grad_hidden_norm, grad_norm2 = norm_back(hidden, inverse2, norm2_gain, grad_normed2)
        grad_hidden = cot_half.astype(F32) + grad_hidden_norm
        branch, branch_other = group.gather(grad_hidden.astype(BF16))
        grad_mixed, grad_gate_rows, grad_group, start_grad = call(
            functools.partial(gate_back_kernel, members=heads),
            [many(1), many(1, BF16), ((PAD, HEAD_DIM), F32), square],
            (*branch, *branch_other, mix_own, mixed, projected, gain, query, decays),
            [pltpu.VMEM((length, HEAD_DIM), F32)],
            ids,
        )
        back_carry = group.carry(start_grad, own_decay, -1)
        grad_rows3, grad_tail, edge, small = call(
            backward_kernel,
            [many(3, BF16), ((16, 3 * HEAD_DIM), F32), ((PAD, 3 * HEAD_DIM), F32), ((16, HEAD_DIM), F32)],
            (grad_mixed, conv, query, key, states, back_carry, halo, projected, taps, gap),
            [
                pltpu.VMEM((length + 16, 3 * HEAD_DIM), F32),
                pltpu.VMEM((length + 2 * PAD, 3 * HEAD_DIM), F32),
            ],
            us=8,
        )
        later = group.shift(edge, -1)
        turned_mix, mine, away, grad_norm1 = call(
            functools.partial(project_back_kernel, members=heads),
            [((4 * HEAD_DIM, length), BF16), all_rows, all_rows, ((PAD, width), F32)],
            (
                *normed1,
                *normed1_other,
                grad_rows3,
                grad_tail,
                later,
                grad_gate_rows,
                mix_own,
                norm1_gain.reshape(1, width),
            ),
            [pltpu.VMEM((length, 4 * HEAD_DIM), BF16)],
            ids,
            us=7,
            mib=28,
        )
        sums = jnp.concatenate([small[:13].reshape(-1), grad_group[0], grad_norm1[0], grad_norm2]).astype(BF16)
        sums = jnp.pad(sums, (0, extra * depth - sums.shape[0])).reshape(extra, depth)
        (grad_mix,) = call(
            functools.partial(mix_grad_kernel, members=heads),
            [((peers, 5 * HEAD_DIM + extra, depth), BF16)],
            (*normed1, *normed1_other, *branch, *branch_other, turned_mix, turned_gated, sums),
            (),
            everything,
            us=7,
            mib=28,
        )
        both = (mine.astype(F32) + group.other_core(away).astype(F32)).astype(BF16)
        return grad_hidden, grad_mix, both

    extra = -(-(14 * HEAD_DIM + 2 * width) // (16 * depth)) * 16
    grad_hidden, grad_mix, both = together(
        backward_steps, mine, other, kept, hidden, inverse2, normed1, normed1_other, turned_gated
    )
    grad_normed1 = lax.psum_scatter(both, "seq", axis_index_groups=group.lists)
    mix_got = lax.all_to_all(after(grad_mix, feed_away), "seq", 0, 0, tiled=True)
    feed_total = group.over_groups(feed_grad, feed_args, feed_away, (grad_mix,), 8)
    (block_mine, block_away) = call(
        block_kernel, [all_rows, all_rows], (inner, feed_own), [pltpu.VMEM((wide, width), BF16)], None, (feed_total,)
    )
    block_half = hidden + group.scatter(block_mine, group.other_core(block_away))
    feed_got = group.spread(after(feed_total, mix_got, block_half))
    mix_total, out_total = call(
        mix_total_kernel,
        [((4, depth, heads * HEAD_DIM), F32), ((heads * HEAD_DIM, depth), F32)],
        (mix_got.reshape(groups, heads, 5 * HEAD_DIM + extra, depth),),
        us=4,
    )
    sums = mix_got[:, 5 * HEAD_DIM :].reshape(groups, heads, -1).astype(F32).sum(0)
    own_sums = sums[:, : 14 * HEAD_DIM].reshape(heads, 14, HEAD_DIM).transpose(1, 0, 2).reshape(14, heads * HEAD_DIM)
    norms = sums[:, 14 * HEAD_DIM : 14 * HEAD_DIM + 2 * width].sum(0).reshape(2, width)
    norms = norms + group.other_core(norms)
    grad_normed1 = after(grad_normed1, block_half).astype(F32)
    grad_rows1 = norm_back(half_tokens, half_inverse1, norm1_gain, grad_normed1)[0]
    grad_tokens = grad_hidden + grad_rows1
    up_total, down_total = call(
        feed_total_kernel,
        [((2, depth, heads * units), F32), ((heads * units, depth), F32)],
        (feed_got,),
        [pltpu.VMEM((heads * units, depth), F32)],
    )
    block_out = both_halves(block_half)
    grad_tokens = both_halves(grad_tokens)

    inverse_rms = jnp.stack([inverse1[:, 0], inverse2_all[:, 0]])
    return (
        block_out,
        grad_tokens,
        norms[0],
        mix_total,
        own_sums[:12].reshape(3, 4, heads * HEAD_DIM),
        own_sums[12],
        own_sums[13],
        out_total,
        norms[1],
        up_total,
        down_total,
        inverse_rms,
    )


def solution(mesh):
    in_specs = (
        P("seq", None),
        P(),
        P(None, "seq", "head"),
        P(None, None, "head"),
        P("head"),
        P("head"),
        P("head", "seq"),
        P(),
        P(None, "seq", "head"),
        P("head", "seq"),
        P("seq", None),
    )
    out_specs = (
        P("seq", None),
        P("seq", None),
        P(),
        P(None, "seq", "head"),
        P(None, None, "head"),
        P("head"),
        P("head"),
        P("head", "seq"),
        P(),
        P(None, "seq", "head"),
        P("head", "seq"),
        P(None, "seq"),
    )
    return jax.shard_map(shards, mesh=mesh, in_specs=in_specs, out_specs=out_specs, check_vma=False)
```

```python
import functools

import jax
import jax.numpy as jnp
from jax import lax
from jax.experimental import pallas as pl
from jax.experimental.pallas import tpu as pltpu
from jax.sharding import PartitionSpec as P

HEAD_DIM = 128
CHUNK = 128
PAD = 8
STEP = 4
EPS_TOKEN = 1e-06
EPS_GROUP = 1e-05
HIGH = lax.Precision.HIGHEST
F32 = jnp.float32
BF16 = jnp.bfloat16
MIB = 1024 * 1024


def mul(a, b, ca, cb, precision=HIGH):
    return lax.dot_general(
        a, b, (((ca,), (cb,)), ((), ())), precision=precision, preferred_element_type=F32
    )


def dsilu(v):
    s = jax.nn.sigmoid(v)
    return s * (1.0 + v * (1.0 - s))


def triangle(lower):
    row = lax.broadcasted_iota(jnp.int32, (CHUNK, CHUNK), 0)
    col = lax.broadcasted_iota(jnp.int32, (CHUNK, CHUNK), 1)
    return (row >= col) if lower else (row <= col)


def forward_kernel(
    proj, halo, taps, gap, conv_out, query_out, key_out, total_out, state_out, local_out, last_out, rows
):
    length = proj.shape[0]
    rows[0:16, :] = halo[...].astype(F32)
    rows[16:, :] = proj[:, : 3 * HEAD_DIM].astype(F32)
    lower = triangle(True)
    ones = lower.astype(F32)
    state = jnp.zeros((HEAD_DIM, HEAD_DIM), F32)
    before = jnp.zeros((1, HEAD_DIM), F32)
    for c in range(length // CHUNK):
        at = c * CHUNK
        here = slice(at, at + CHUNK)
        conv = []
        for j in range(3):
            cols = slice(j * HEAD_DIM, (j + 1) * HEAD_DIM)
            total = taps[4 * j : 4 * j + 1, :] * rows[16 + at : 16 + at + CHUNK, cols]
            for d in range(1, 4):
                total = total + taps[4 * j + d : 4 * j + d + 1, :] * rows[16 + at - d : 16 + at - d + CHUNK, cols]
            conv.append(total)
            conv_out[here, cols] = total
        queries = conv[0] * jax.nn.sigmoid(conv[0])
        open_share = 1.0 - jax.nn.sigmoid(conv[1])
        keys = gap[...] * open_share
        log_forget = jnp.log(1.0 - keys)
        values = conv[2]
        running = mul(ones, log_forget, 1, 0)
        last = running[CHUNK - 1 : CHUNK, :]
        query = queries * jnp.exp(running)
        key = keys * jnp.exp(-running)
        carried = keys * jnp.exp(last - running)
        query_out[here, :] = query
        key_out[here, :] = key
        total_out[c : c + 1, :] = before
        state_out[c] = state
        scores = jnp.where(lower, mul(query, key, 1, 1), 0.0)
        local_out[here, :] = mul(scores, values, 1, 0) + mul(query, state, 1, 1)
        state = state * jnp.exp(last) + mul(values, carried, 0, 0)
        before = before + last
    last_out[0:HEAD_DIM, :] = state
    last_out[HEAD_DIM:, :] = jnp.broadcast_to(jnp.exp(before), (PAD, HEAD_DIM))


def gate_kernel(
    ids, local, query, total, state, carry, gate, gain, weights, mixed_out, state_out, turned_out, mine, away, gated
):
    length = local.shape[0]
    members, half, _ = mine.shape
    start = carry[...]
    for c in range(length // CHUNK):
        here = slice(c * CHUNK, (c + 1) * CHUNK)
        grown = start * jnp.exp(total[c : c + 1, :])
        state_out[c] = state[c] + grown
        mixed = local[here, :] + mul(query[here, :], grown, 1, 1)
        mixed_out[here, :] = mixed
        inverse = lax.rsqrt(jnp.mean(mixed * mixed, axis=-1, keepdims=True) + EPS_GROUP)
        g = gate[here, 3 * HEAD_DIM :].astype(F32)
        gated[here, :] = (mixed * inverse * gain[...] * (g * jax.nn.sigmoid(g))).astype(BF16)
    parts = []
    for k, b, block in blocks_of(ids, members):
        parts.append(gated[pl.ds(pl.multiple_of(block * half, half), half), :])
        if len(parts) == STEP:
            x = jnp.concatenate(parts, axis=0)
            at = (k * members + b + 1 - STEP) * half
            turned_out[:, at : at + STEP * half] = x.astype(F32).T.astype(BF16)
            result = mul(x, weights[:, 4 * HEAD_DIM :], 1, 1, None).astype(BF16)
            (mine, away)[k][b + 1 - STEP : b + 1] = result.reshape(STEP, half, -1)
            parts = []


def gate_back_kernel(
    ids, *refs, members
):
    own, other = refs[:members], refs[members : 2 * members]
    weights, mixed, gate, gain, query, decay = refs[2 * members : 2 * members + 6]
    grad_mixed_out, grad_gate_out, grad_gain_out, start_out, grad_gated = refs[2 * members + 6 :]
    half = own[0].shape[0]
    at = 0
    blocks = list(blocks_of(ids, members))
    for at in range(0, len(blocks), STEP):
        k, b, _ = blocks[at]
        result = mul(rows_of((own, other)[k], b), weights[:, 4 * HEAD_DIM :], 1, 0, None)
        for i in range(STEP):
            to = pl.multiple_of(blocks[at + i][2] * half, half)
            grad_gated[pl.ds(to, half), :] = result[i * half : (i + 1) * half]
    length = mixed.shape[0]
    count = length // CHUNK
    grad_gain = jnp.zeros((1, HEAD_DIM), F32)
    state = jnp.zeros((HEAD_DIM, HEAD_DIM), F32)
    for c in reversed(range(count)):
        here = slice(c * CHUNK, (c + 1) * CHUNK)
        grad = grad_gated[here, :]
        mix = mixed[here, :]
        inverse = lax.rsqrt(jnp.mean(mix * mix, axis=-1, keepdims=True) + EPS_GROUP)
        g = gate[here, 3 * HEAD_DIM :].astype(F32)
        s = jax.nn.sigmoid(g)
        unit = mix * inverse
        w = grad * gain[...] * (g * s)
        grad_gain = grad_gain + jnp.sum(grad * unit * (g * s), axis=0, keepdims=True)
        grad_gate_out[here, :] = (grad * unit * gain[...] * (s * (1.0 + g * (1.0 - s)))).astype(BF16)
        grad_mixed = inverse * w - mix * (inverse * inverse * inverse) * jnp.mean(w * mix, axis=-1, keepdims=True)
        grad_mixed_out[here, :] = grad_mixed
        state = state * decay[c : c + 1, :] + mul(grad_mixed, query[here, :], 0, 0)
    start_out[...] = state
    grad_gain_out[...] = jnp.broadcast_to(grad_gain, (PAD, HEAD_DIM))


def backward_kernel(
    grad_mixed,
    conv,
    query,
    key,
    states,
    carry,
    halo,
    proj,
    taps,
    gap,
    grad_out,
    tail_out,
    edge_out,
    small_out,
    rows,
    grads,
):
    length = grad_mixed.shape[0]
    count = length // CHUNK
    rows[0:16, :] = halo[...].astype(F32)
    rows[16:, :] = proj[:, : 3 * HEAD_DIM].astype(F32)
    grads[0:PAD, :] = jnp.zeros((PAD, 3 * HEAD_DIM), F32)
    grads[PAD + length :, :] = jnp.zeros((PAD, 3 * HEAD_DIM), F32)
    lower = triangle(True)
    ones = lower.astype(F32)
    upper = triangle(False).astype(F32)
    last_row = lax.broadcasted_iota(jnp.int32, (CHUNK, HEAD_DIM), 0) == CHUNK - 1
    back = carry[...]
    grad_gap = jnp.zeros((1, HEAD_DIM), F32)
    sums = [jnp.zeros((1, HEAD_DIM), F32) for _ in range(12)]
    for c in reversed(range(count)):
        at = c * CHUNK
        here = slice(at, at + CHUNK)
        c0, c1, values = (conv[here, j * HEAD_DIM : (j + 1) * HEAD_DIM] for j in range(3))
        s1 = jax.nn.sigmoid(c1)
        open_share = 1.0 - s1
        keys = gap[...] * open_share
        forget = 1.0 - keys
        running = mul(ones, jnp.log(forget), 1, 0)
        last = running[CHUNK - 1 : CHUNK, :]
        grown, shrunk, rest = jnp.exp(running), jnp.exp(-running), jnp.exp(last - running)
        q, k, g = query[here, :], key[here, :], grad_mixed[here, :]
        carried = keys * rest
        state = states[c]
        scores = jnp.where(lower, mul(q, k, 1, 1), 0.0)
        grad_scores = jnp.where(lower, mul(g, values, 1, 1), 0.0)
        grad_values = mul(scores, g, 0, 0) + mul(carried, back, 1, 1)
        grad_query = mul(grad_scores, k, 1, 0) + mul(g, state, 1, 0)
        grad_key = mul(grad_scores, q, 0, 0)
        grad_carried = mul(values, back, 1, 0)
        grad_last = jnp.exp(last) * jnp.sum(back * state, axis=0, keepdims=True) + jnp.sum(
            grad_carried * carried, axis=0, keepdims=True
        )
        grad_running = grad_query * q - grad_key * k - grad_carried * carried
        grad_running = grad_running + jnp.where(last_row, grad_last, 0.0)
        grad_keys = grad_key * shrunk + grad_carried * rest
        grad_forget = mul(upper, grad_running, 1, 0) / forget
        inner = grad_forget - grad_keys
        grad_gap = grad_gap - jnp.sum(open_share * inner, axis=0, keepdims=True)
        sigmoid0 = jax.nn.sigmoid(c0)
        new = (
            grad_query * grown * (sigmoid0 * (1.0 + c0 * (1.0 - sigmoid0))),
            gap[...] * s1 * open_share * inner,
            grad_values,
        )
        back = back * jnp.exp(last) + mul(g, q, 0, 0)
        for j in range(3):
            cols = slice(j * HEAD_DIM, (j + 1) * HEAD_DIM)
            grads[PAD + at : PAD + at + CHUNK, cols] = new[j]
            for d in range(4):
                sums[4 * j + d] = sums[4 * j + d] + jnp.sum(
                    new[j] * rows[16 + at - d : 16 + at - d + CHUNK, cols], axis=0, keepdims=True
                )
            total = taps[4 * j : 4 * j + 1, :] * new[j]
            for d in range(1, 4):
                total = total + taps[4 * j + d : 4 * j + d + 1, :] * grads[PAD + at + d : PAD + at + d + CHUNK, cols]
            grad_out[here, cols] = total.astype(BF16)
            if c == count - 1:
                tail_out[:, cols] = total[CHUNK - 16 :]
    for j in range(3):
        cols = slice(j * HEAD_DIM, (j + 1) * HEAD_DIM)
        total = taps[4 * j + 1 : 4 * j + 2, :] * grads[1 : 1 + PAD, cols]
        for d in range(2, 4):
            total = total + taps[4 * j + d : 4 * j + d + 1, :] * grads[d : d + PAD, cols]
        edge_out[:, cols] = total
    for i in range(12):
        small_out[i : i + 1, :] = sums[i]
    small_out[12:13, :] = grad_gap
    small_out[13:16, :] = jnp.zeros((3, HEAD_DIM), F32)


def blocks_of(ids, count):
    member, core = ids[0], ids[1]
    for k in range(2):
        for b in range(count):
            yield k, b, (member ^ b) * 2 + (core ^ k)


def rows_of(blocks, first, count=STEP, cols=slice(None)):
    if isinstance(blocks, (tuple, list)):
        return jnp.concatenate([blocks[first + i][:, cols] for i in range(count)], axis=0)
    part = blocks[first : first + count, :, cols]
    return part.reshape(-1, part.shape[-1])


def fill_columns(weights, source, first, target, rows):
    groups, members, _, depth = source.shape
    per = max(1, 128 // depth)
    for at in range(0, groups * members, per):
        parts = [source[(at + i) // members, (at + i) % members, first : first + rows, :] for i in range(per)]
        part = parts[0] if per == 1 else jnp.concatenate(parts, axis=1)
        weights[target : target + rows, at * depth : (at + per) * depth] = part


def mix_blocks_kernel(mix, out_weight, out):
    groups, heads, depth, _ = out.shape
    for m in range(heads):
        cols = slice(m * HEAD_DIM, (m + 1) * HEAD_DIM)
        turned = out_weight[cols, :].astype(F32).T.astype(BF16)
        for g in range(groups):
            for j in range(4):
                out[g, m, :, j * HEAD_DIM : (j + 1) * HEAD_DIM] = mix[j, :, cols]
            out[g, m, :, 4 * HEAD_DIM :] = turned


def feed_blocks_kernel(up, down, out, turned):
    _, _, units = up.shape
    heads = out.shape[0]
    rows = units // heads
    for j in range(2):
        for t in range(units // 128):
            block = up[j, :, t * 128 : (t + 1) * 128].astype(F32)
            turned[t * 128 : (t + 1) * 128, :] = block.T.astype(BF16)
        for m in range(heads):
            out[m, j * rows : (j + 1) * rows, :] = turned[m * rows : (m + 1) * rows, :]
    for m in range(heads):
        out[m, 2 * rows :, :] = down[m * rows : (m + 1) * rows, :]


def project_kernel(ids, *refs, members):
    own, other = refs[:members], refs[members : 2 * members]
    weights, out, tail = refs[2 * members :]
    half = own[0].shape[0]
    blocks = list(blocks_of(ids, members))
    for at in range(0, len(blocks), STEP):
        k, b, _ = blocks[at]
        result = mul(rows_of((own, other)[k], b), weights[:, : 4 * HEAD_DIM], 1, 0, None).astype(BF16)
        for i in range(STEP):
            to = pl.multiple_of(blocks[at + i][2] * half, half)
            out[pl.ds(to, half), :] = result[i * half : (i + 1) * half]
    tail[...] = out[out.shape[0] - 16 :, : tail.shape[1]]


def feed_kernel(*refs, members):
    own, other, cot_own, cot_other = (refs[i * members : (i + 1) * members] for i in range(4))
    feed, turned, inner_out, mine, away, weights = refs[4 * members :]
    half, width = own[0].shape
    units = feed.shape[2] // 3
    wide = turned.shape[0] // 3
    for j in range(3):
        weights[j * wide + units : (j + 1) * wide, :] = jnp.zeros((wide - units, width), BF16)
        fill_columns(weights, feed, j * units, j * wide, units)
    for k in range(2):
        for b in range(0, members, STEP):
            x = rows_of((own, other)[k], b)
            c = rows_of((cot_own, cot_other)[k], b)
            lifted = mul(x, weights[: 2 * wide], 1, 1, None)
            gate, up_in = lifted[:, :wide], lifted[:, wide:]
            grad = mul(c, weights[2 * wide :], 1, 1, None)
            s = jax.nn.sigmoid(gate)
            act = gate * s
            inner = act * up_in
            grad_gate = grad * up_in * (s * (1.0 + gate * (1.0 - s)))
            grad_up = grad * act
            at = (k * members + b) * half
            cols = slice(at, at + STEP * half)
            turned[0:wide, cols] = grad_gate.T.astype(BF16)
            turned[wide : 2 * wide, cols] = grad_up.T.astype(BF16)
            turned[2 * wide :, cols] = inner.T.astype(BF16)
            inner_out[cols, :] = inner.astype(BF16)
            lift = jnp.concatenate([grad_gate.astype(BF16), grad_up.astype(BF16)], axis=1)
            (mine, away)[k][b : b + STEP] = (
                mul(lift, weights[: 2 * wide], 1, 0, None).astype(BF16).reshape(STEP, half, width)
            )


def block_kernel(inner, feed, mine, away, weights):
    members, half, width = mine.shape
    units, wide = feed.shape[2] // 3, inner.shape[1]
    weights[units:, :] = jnp.zeros((wide - units, width), BF16)
    fill_columns(weights, feed, 2 * units, 0, units)
    for k in range(2):
        for b in range(0, members, STEP):
            at = (k * members + b) * half
            result = mul(inner[at : at + STEP * half, :], weights[...], 1, 0, None)
            (mine, away)[k][b : b + STEP] = result.astype(BF16).reshape(STEP, half, width)


def product_into(ids, out, first, turned, spans, own, other, members, got=None):
    rows = turned.shape[1] // 2
    shards, _, depth = out.shape
    low, high = spans[0][0], spans[-1][1]
    for at in range(0, shards * depth, 256):
        cols = pl.ds(pl.multiple_of(ids[2] * (shards * depth) + at, 128), 256)
        result = mul(turned[low:high, :rows], rows_of(own, 0, members, cols), 1, 0, None)
        result += mul(turned[low:high, rows:], rows_of(other, 0, members, cols), 1, 0, None)
        to = first
        for start, stop in spans:
            here = slice(to, to + stop - start)
            for i in range(256 // depth):
                part = result[start - low : stop - low, i * depth : (i + 1) * depth]
                if got is not None:
                    part = part + got[ids[3], at // depth + i, here, :].astype(F32)
                out[at // depth + i, here, :] = part.astype(BF16)
            to += stop - start


def feed_grad_kernel(ids, *refs, members):
    own, other, cot_own, cot_other = (refs[i * members : (i + 1) * members] for i in range(4))
    turned, *got, out = refs[4 * members :]
    got = got[0] if got else None
    units, wide = out.shape[1] // 3, turned.shape[0] // 3
    product_into(ids, out, 0, turned, [(0, units), (wide, wide + units)], own, other, members, got)
    product_into(ids, out, 2 * units, turned, [(2 * wide, 2 * wide + units)], cot_own, cot_other, members, got)


def mix_grad_kernel(ids, *refs, members):
    own, other, branch_own, branch_other = (refs[i * members : (i + 1) * members] for i in range(4))
    turned, turned_gated, sums, *got, out = refs[4 * members :]
    got = got[0] if got else None
    for m in range(out.shape[0]):
        total = sums[...]
        if got is not None:
            total = total + got[ids[3], m, 5 * HEAD_DIM :, :].astype(F32)
        out[m, 5 * HEAD_DIM :, :] = total.astype(BF16)
    product_into(ids, out, 0, turned, [(0, 4 * HEAD_DIM)], own, other, members, got)
    product_into(ids, out, 4 * HEAD_DIM, turned_gated, [(0, HEAD_DIM)], branch_own, branch_other, members, got)


def project_back_kernel(ids, *refs, members):
    own, other = refs[:members], refs[members : 2 * members]
    grad3, tail, later, grad_gate, weights, norm_gain, turned, mine_out, away_out, norm_out, grads = refs[2 * members :]
    length = grad3.shape[0]
    members, half, width = mine_out.shape
    three = grad3.shape[1]
    grads[:, :three] = grad3[...]
    end = tail.shape[0]
    edge = jnp.concatenate([jnp.zeros((end - later.shape[0], three), F32), later[...]], axis=0)
    grads[length - end :, :three] = (tail[...] + edge).astype(BF16)
    grads[:, three:] = grad_gate[...]
    grad_norm = jnp.zeros((1, width), F32)
    parts = []
    for k, b, block in blocks_of(ids, members):
        parts.append(grads[pl.ds(pl.multiple_of(block * half, half), half), :])
        if len(parts) == STEP:
            x = jnp.concatenate(parts, axis=0)
            at = (k * members + b + 1 - STEP) * half
            turned[:, at : at + STEP * half] = x.astype(F32).T.astype(BF16)
            result = mul(x, weights[:, : 4 * HEAD_DIM], 1, 1, None)
            normed = rows_of((own, other)[k], b + 1 - STEP).astype(F32)
            grad_norm = grad_norm + jnp.sum(result * normed, axis=0, keepdims=True)
            for i in range(STEP):
                to = ids[0] ^ (b + 1 - STEP + i)
                (mine_out, away_out)[k][to] = result[i * half : (i + 1) * half].astype(BF16)
            parts = []
    norm_out[...] = jnp.broadcast_to(grad_norm / norm_gain[...], norm_out.shape)


def mix_total_kernel(got, mix_out, out_out):
    groups, heads, _, depth = got.shape

    def total(i, rows):
        result = got[0, i, rows, :].astype(F32)
        for g in range(1, groups):
            result = result + got[g, i, rows, :].astype(F32)
        return result

    for i in range(heads):
        cols = slice(i * HEAD_DIM, (i + 1) * HEAD_DIM)
        for j in range(4):
            mix_out[j, :, cols] = total(i, slice(j * HEAD_DIM, (j + 1) * HEAD_DIM)).T
        out_out[cols, :] = total(i, slice(4 * HEAD_DIM, 5 * HEAD_DIM))


def feed_total_kernel(got, up_out, down_out, rows):
    heads, three, depth = got.shape
    units = three // 3
    for j in range(2):
        for i in range(heads):
            rows[i * units : (i + 1) * units, :] = got[i, j * units : (j + 1) * units, :].astype(F32)
        for t in range(heads * units // 128):
            up_out[j, :, t * 128 : (t + 1) * 128] = rows[t * 128 : (t + 1) * 128, :].T
    for i in range(heads):
        down_out[i * units : (i + 1) * units, :] = got[i, 2 * units :, :].astype(F32)


def call(kernel, outs, args, scratch=(), ids=None, behind=(), us=5, mib=20):
    specs = [pl.BlockSpec(memory_space=pltpu.VMEM)] * len(args)
    if ids is not None:
        specs = [pl.BlockSpec(memory_space=pltpu.SMEM)] + specs
        args = (ids,) + tuple(args)
    real = len(args)

    def body(*refs):
        kernel(*refs[:real], *refs[real + len(behind) :])

    return pl.pallas_call(
        body,
        out_shape=[jax.ShapeDtypeStruct(s, d) for s, d in outs],
        in_specs=specs + [pl.BlockSpec(memory_space=pl.ANY)] * len(behind),
        out_specs=[pl.BlockSpec(memory_space=pltpu.VMEM)] * len(outs),
        scratch_shapes=list(scratch),
        compiler_params=pltpu.CompilerParams(vmem_limit_bytes=mib * MIB),
        cost_estimate=pl.CostEstimate(flops=0, bytes_accessed=us * 3000000, transcendentals=0),
    )(*args, *behind)


class Group:
    def __init__(self, heads):
        self.size = heads
        self.peers = lax.axis_size("seq")
        self.count = self.peers // heads
        self.member = lax.rem(lax.axis_index("seq"), heads)
        self.index = lax.div(lax.axis_index("seq"), heads)
        self.core = lax.axis_index("head")
        self.ids = jnp.stack([self.member, self.core]).astype(jnp.int32)
        self.lists = [list(range(g * heads, (g + 1) * heads)) for g in range(self.count)]
        self.columns = [list(range(m, self.peers, heads)) for m in range(heads)]

    def swap(self, value, bits):
        return lax.ppermute(value, "seq", [(s, s ^ bits) for s in range(self.peers)])

    def other_core(self, value):
        return lax.ppermute(value, "head", [(0, 1), (1, 0)])

    def shift(self, value, groups):
        step = groups * self.size
        pairs = [(s, s + step) for s in range(self.peers) if 0 <= s + step < self.peers]
        return lax.ppermute(value, "seq", pairs)

    def carry(self, state, decay, sign):
        total = None
        for k in reversed(range(1, self.count)):
            new = self.shift(state, sign * k)
            total = new if total is None else new + total * self.shift(decay, sign * k)
        return jnp.zeros_like(state) if total is None else total

    def gather(self, half):
        got = {0: half}
        for bits in (4, 1, 2):
            got[bits] = self.swap(half, bits)
        got[6] = self.swap(got[4], 2)
        got[5] = self.swap(got[4], 1)
        got[3] = self.swap(got[2], 1)
        got[7] = self.swap(got[5], 2)
        own = [got[bits] for bits in range(self.size)]
        return own, [self.other_core(block) for block in own]

    def over_members(self, part, before_last=()):
        def add(to, source, bits):
            part[to] = part[to] + self.swap(part[source].astype(BF16), bits).astype(F32)

        add(5, 7, 2)
        add(2, 3, 1)
        add(4, 6, 2)
        add(0, 1, 1)
        add(4, 5, 1)
        add(0, 2, 2)
        part[4] = after(part[4], *before_last)
        add(0, 4, 4)
        return part[0]

    def scatter(self, mine, other, before_last=()):
        part = [mine[b].astype(F32) + other[b].astype(F32) for b in range(self.size)]
        return self.over_members(part, before_last)

    def spread(self, blocks):
        return lax.all_to_all(blocks, "seq", 0, 0, axis_index_groups=self.lists, tiled=True)

    def all_groups(self, value):
        return lax.all_gather(value, "seq", axis_index_groups=self.columns)

    def away(self, kernel, rows, depth, args, us):
        count = 1 if self.count == 2 else self.count
        ids = jnp.stack([self.member, self.core, (1 - self.index) * (count == 1), 0 * self.core]).astype(jnp.int32)
        (out,) = call(kernel, [((count * self.size, rows, depth), BF16)], args, (), ids, us=us, mib=28)
        if count == 1:
            return self.all_groups(out)
        out = out.reshape(count, self.size, rows, depth)
        return lax.psum_scatter(out, "seq", axis_index_groups=self.columns)

    def over_groups(self, kernel, args, got, behind, us):
        if self.count != 2:
            return got
        ids = jnp.stack([self.member, self.core, self.index, 1 - self.index]).astype(jnp.int32)
        return call(kernel, [(got.shape[1:], BF16)], (*args, got), (), ids, behind, us, 28)[0]


def inverse_of(rows):
    return lax.rsqrt(jnp.mean(rows * rows, axis=-1, keepdims=True) + EPS_TOKEN)


def norm_back(rows, inverse, gain, grad):
    scaled = grad * gain
    dot_term = jnp.mean(scaled * rows, axis=-1, keepdims=True)
    grad_rows = inverse * scaled - rows * (inverse * inverse * inverse) * dot_term
    return grad_rows, jnp.sum(grad * rows * inverse, axis=0)


def together(steps, *args):
    shapes = jax.eval_shape(steps, *args)
    always = lax.axis_index("seq") < 2 * lax.axis_size("seq")

    def never(*_):
        return jax.tree.map(lambda leaf: jnp.zeros(leaf.shape, leaf.dtype), shapes)

    return lax.cond(always, steps, never, *args)


def after(value, *earlier):
    return lax.optimization_barrier((value,) + earlier)[0]


def shards(
    tokens,
    norm1_gain,
    mix_weight,
    conv_weight,
    decay_gap,
    group_gain,
    out_weight,
    norm2_gain,
    up_pair,
    down_weight,
    cotangent,
):
    depth = mix_weight.shape[1]
    heads = mix_weight.shape[2] // HEAD_DIM
    units = down_weight.shape[0] // heads
    wide = -(-units // 128) * 128
    local, width = tokens.shape
    half = local // 2
    group = Group(heads)
    ids, member, core = group.ids, group.member, group.core
    length = heads * local
    count = length // CHUNK
    groups, peers = group.count, group.peers

    def my_half(rows):
        return lax.dynamic_slice_in_dim(rows, core * half, half, 0)

    def own_head(array):
        return lax.dynamic_slice_in_dim(array, member * HEAD_DIM, HEAD_DIM, array.ndim - 1)

    taps = own_head(conv_weight).reshape(12, HEAD_DIM)
    gap = own_head(decay_gap).reshape(1, HEAD_DIM)
    gain = own_head(group_gain).reshape(1, HEAD_DIM)

    everything = jnp.stack([member, core, 0 * core, 0 * core]).astype(jnp.int32)
    square = ((HEAD_DIM, HEAD_DIM), F32)
    all_rows = ((heads, half, width), BF16)

    def many(n, dtype=F32):
        return ((length, n * HEAD_DIM), dtype)

    token_rows = tokens.astype(F32)
    inverse1 = inverse_of(token_rows)
    half_tokens = my_half(token_rows)
    half_inverse1 = my_half(inverse1)
    cot_half = my_half(cotangent)

    def start_steps(rows, mix_weight, out_weight, up, down):
        own, other = group.gather(rows)
        (mix_blocks,) = call(
            mix_blocks_kernel, [((groups, heads, depth, 5 * HEAD_DIM), BF16)], (mix_weight, out_weight), us=2
        )
        mix_blocks = mix_blocks.reshape(peers, depth, 5 * HEAD_DIM)
        mix_own = lax.all_to_all(mix_blocks, "seq", 0, 0, tiled=True).reshape(width, 5 * HEAD_DIM)
        (feed_blocks,) = call(
            feed_blocks_kernel,
            [((heads, 3 * units, depth), BF16)],
            (up, down),
            [pltpu.VMEM((heads * units, depth), BF16)],
            us=3,
        )
        projected, tail = call(
            functools.partial(project_kernel, members=heads),
            [((length, 4 * HEAD_DIM), BF16), ((16, 3 * HEAD_DIM), BF16)],
            (*own, *other, mix_own),
            (),
            ids,
        )
        halo = group.shift(tail, 1)
        feed = group.spread(after(feed_blocks, halo))
        conv, query, key, totals, states, mixed_here, last = call(
            forward_kernel,
            [
                many(3),
                many(1),
                many(1),
                ((count, HEAD_DIM), F32),
                ((count, HEAD_DIM, HEAD_DIM), F32),
                many(1),
                ((HEAD_DIM + PAD, HEAD_DIM), F32),
            ],
            (projected, halo, taps, gap),
            [pltpu.VMEM((length + 16, 3 * HEAD_DIM), F32)],
        )
        own_decay = last[HEAD_DIM : HEAD_DIM + 1]
        carry = group.carry(last[:HEAD_DIM], own_decay, 1)
        decays = jnp.exp(jnp.concatenate([totals[1:] - totals[:-1], jnp.log(own_decay) - totals[-1:]], axis=0))
        kept = (mix_own, projected, halo, conv, query, key)
        return own, other, feed, kept, (own_decay, decays), (mixed_here, totals, states, carry)

    normed1, normed1_other, feed_here, kept, decay_rows, here = together(
        start_steps,
        (half_tokens * half_inverse1 * norm1_gain).astype(BF16),
        mix_weight,
        out_weight,
        up_pair,
        down_weight,
    )
    feed_own = group.all_groups(feed_here)

    def both_halves(rows):
        other = group.other_core(rows)
        return jnp.where(core == 0, jnp.concatenate([rows, other], 0), jnp.concatenate([other, rows], 0))

    def forward_steps(kept, here, cot_half):
        mix_own, projected, _, _, query, _ = kept
        mixed_here, totals, states, carry = here
        cot, cot_other = group.gather(cot_half)
        mixed, states, turned_gated, mine, away = call(
            gate_kernel,
            [many(1), ((count, HEAD_DIM, HEAD_DIM), F32), ((HEAD_DIM, length), BF16), all_rows, all_rows],
            (mixed_here, query, totals, states, carry, projected, gain, mix_own),
            [pltpu.VMEM((length, HEAD_DIM), BF16)],
            ids,
        )
        hidden = half_tokens + group.scatter(mine, group.other_core(away))
        inverse2 = inverse_of(hidden)
        normed2, normed2_other = group.gather((hidden * inverse2 * norm2_gain).astype(BF16))
        return (states, mixed), (*normed2, *normed2_other, *cot, *cot_other), (turned_gated, hidden, inverse2, both_halves(inverse2))

    mixed_rows, feed_rows, (turned_gated, hidden, inverse2, inverse2_all) = together(
        forward_steps, kept, here, cot_half
    )
    kept = (*kept, *mixed_rows, *decay_rows)
    turned, inner, mine, away = call(
        functools.partial(feed_kernel, members=heads),
        [((3 * wide, length), BF16), ((length, wide), BF16), all_rows, all_rows],
        (*feed_rows, feed_own),
        [pltpu.VMEM((3 * wide, width), BF16)],
        us=17,
        mib=38,
    )
    feed_grad = functools.partial(feed_grad_kernel, members=heads)
    feed_args = (*feed_rows, turned)
    other = group.other_core(away)
    feed_away = group.away(feed_grad, 3 * units, depth, feed_args, 7)

    def backward_steps(mine, other, kept, hidden, inverse2, normed1, normed1_other, turned_gated):
        mix_own, projected, halo, conv, query, key, states, mixed, own_decay, decays = kept
        grad_normed2 = group.scatter(mine, other)
        grad_hidden_norm, grad_norm2 = norm_back(hidden, inverse2, norm2_gain, grad_normed2)
        grad_hidden = cot_half.astype(F32) + grad_hidden_norm
        branch, branch_other = group.gather(grad_hidden.astype(BF16))
        grad_mixed, grad_gate_rows, grad_group, start_grad = call(
            functools.partial(gate_back_kernel, members=heads),
            [many(1), many(1, BF16), ((PAD, HEAD_DIM), F32), square],
            (*branch, *branch_other, mix_own, mixed, projected, gain, query, decays),
            [pltpu.VMEM((length, HEAD_DIM), F32)],
            ids,
        )
        back_carry = group.carry(start_grad, own_decay, -1)
        grad_rows3, grad_tail, edge, small = call(
            backward_kernel,
            [many(3, BF16), ((16, 3 * HEAD_DIM), F32), ((PAD, 3 * HEAD_DIM), F32), ((16, HEAD_DIM), F32)],
            (grad_mixed, conv, query, key, states, back_carry, halo, projected, taps, gap),
            [
                pltpu.VMEM((length + 16, 3 * HEAD_DIM), F32),
                pltpu.VMEM((length + 2 * PAD, 3 * HEAD_DIM), F32),
            ],
            us=8,
        )
        later = group.shift(edge, -1)
        turned_mix, mine, away, grad_norm1 = call(
            functools.partial(project_back_kernel, members=heads),
            [((4 * HEAD_DIM, length), BF16), all_rows, all_rows, ((PAD, width), F32)],
            (
                *normed1,
                *normed1_other,
                grad_rows3,
                grad_tail,
                later,
                grad_gate_rows,
                mix_own,
                norm1_gain.reshape(1, width),
            ),
            [pltpu.VMEM((length, 4 * HEAD_DIM), BF16)],
            ids,
            us=7,
            mib=28,
        )
        sums = jnp.concatenate([small[:13].reshape(-1), grad_group[0], grad_norm1[0], grad_norm2]).astype(BF16)
        sums = jnp.pad(sums, (0, extra * depth - sums.shape[0])).reshape(extra, depth)
        (grad_mix,) = call(
            functools.partial(mix_grad_kernel, members=heads),
            [((peers, 5 * HEAD_DIM + extra, depth), BF16)],
            (*normed1, *normed1_other, *branch, *branch_other, turned_mix, turned_gated, sums),
            (),
            everything,
            us=7,
            mib=28,
        )
        both = (mine.astype(F32) + group.other_core(away).astype(F32)).astype(BF16)
        return grad_hidden, grad_mix, both

    extra = -(-(14 * HEAD_DIM + 2 * width) // (16 * depth)) * 16
    grad_hidden, grad_mix, both = together(
        backward_steps, mine, other, kept, hidden, inverse2, normed1, normed1_other, turned_gated
    )
    grad_normed1 = lax.psum_scatter(both, "seq", axis_index_groups=group.lists)
    mix_got = lax.all_to_all(after(grad_mix, feed_away), "seq", 0, 0, tiled=True)
    (block_mine, block_away) = call(
        block_kernel, [all_rows, all_rows], (inner, feed_own), [pltpu.VMEM((wide, width), BF16)], None, (grad_mix,)
    )
    feed_total = group.over_groups(feed_grad, feed_args, feed_away, (block_mine,), 8)
    block_half = hidden + group.scatter(block_mine, group.other_core(block_away))
    feed_got = group.spread(after(feed_total, mix_got, block_half))
    mix_total, out_total = call(
        mix_total_kernel,
        [((4, depth, heads * HEAD_DIM), F32), ((heads * HEAD_DIM, depth), F32)],
        (mix_got.reshape(groups, heads, 5 * HEAD_DIM + extra, depth),),
        us=4,
    )
    sums = mix_got[:, 5 * HEAD_DIM :].reshape(groups, heads, -1).astype(F32).sum(0)
    own_sums = sums[:, : 14 * HEAD_DIM].reshape(heads, 14, HEAD_DIM).transpose(1, 0, 2).reshape(14, heads * HEAD_DIM)
    norms = sums[:, 14 * HEAD_DIM : 14 * HEAD_DIM + 2 * width].sum(0).reshape(2, width)
    norms = norms + group.other_core(norms)
    grad_normed1 = after(grad_normed1, block_half).astype(F32)
    grad_rows1 = norm_back(half_tokens, half_inverse1, norm1_gain, grad_normed1)[0]
    grad_tokens = grad_hidden + grad_rows1
    up_total, down_total = call(
        feed_total_kernel,
        [((2, depth, heads * units), F32), ((heads * units, depth), F32)],
        (feed_got,),
        [pltpu.VMEM((heads * units, depth), F32)],
    )
    block_out = both_halves(block_half)
    grad_tokens = both_halves(grad_tokens)

    inverse_rms = jnp.stack([inverse1[:, 0], inverse2_all[:, 0]])
    return (
        block_out,
        grad_tokens,
        norms[0],
        mix_total,
        own_sums[:12].reshape(3, 4, heads * HEAD_DIM),
        own_sums[12],
        own_sums[13],
        out_total,
        norms[1],
        up_total,
        down_total,
        inverse_rms,
    )


def solution(mesh):
    in_specs = (
        P("seq", None),
        P(),
        P(None, "seq", "head"),
        P(None, None, "head"),
        P("head"),
        P("head"),
        P("head", "seq"),
        P(),
        P(None, "seq", "head"),
        P("head", "seq"),
        P("seq", None),
    )
    out_specs = (
        P("seq", None),
        P("seq", None),
        P(),
        P(None, "seq", "head"),
        P(None, None, "head"),
        P("head"),
        P("head"),
        P("head", "seq"),
        P(),
        P(None, "seq", "head"),
        P("head", "seq"),
        P(None, "seq"),
    )
    return jax.shard_map(shards, mesh=mesh, in_specs=in_specs, out_specs=out_specs, check_vma=False)
```
